32 devices in a mesh: groups: 2 (over y), blk: 8 (over z, x), fsdp: 2 (over core).
Axes of the slice: x: 2, y: 2, z: 4, core: 2. Of those that a mesh axis runs over, the one named last changes fastest.
Arguments:
- query_out: bfloat16 [28672, 64], P('blk'), may hold values from -6 to 6
- query_act: bfloat16 [8192, 64], P('blk'), may hold values from -6 to 6
- out_basis: bfloat16 [28672, 512], P('blk', 'fsdp'), may hold values from -0.03125 to 0.03125
- act_basis: bfloat16 [8192, 256], P('blk', 'fsdp'), may hold values from -0.0625 to 0.0625
- eigenvalues: float32 [512, 256], P('fsdp'), may hold values from 0.05 to 5
- train_out: bfloat16 [32, 32, 512], P(('groups', 'blk', 'fsdp')), parts along dimension 0, may hold values from -0.078125 to 0.078125
- train_act: bfloat16 [32, 32, 256], P(('groups', 'blk', 'fsdp')), parts along dimension 0, may hold values from -0.078125 to 0.078125
- train_tokens: int32 [32], P(('groups', 'blk', 'fsdp')), parts along dimension 0, may hold values from 1 to 32, 256 in all
- train_ids: int32 [32], P(('groups', 'blk', 'fsdp')), parts along dimension 0, may hold values from 0 to 15, each once
Outputs:
- scores: float32 [16, 32], P('blk', 'groups'), parts along dimension 1
The draws below stay inside these ranges and needn't reach their ends.
There are 2 independent parts, one for each index of `groups`. The reference program is written for one: setup_inputs(seed, part) draws one part's arguments, and reference() takes and returns one part's arrays. A program takes and returns all parts, laid end to end along the dimension named above; an argument that names none is the same for every part. Nothing has to cross between parts.
Inputs may be any that keep to these rules, and one draw needn't show every extreme that they name: `train_tokens`: number of tokens of each training example; its factor rows from this number on are padding and hold stale values. Some example has exactly 32. `train_ids`: A permutation of the score columns: every column is named by exactly one stored training example.
All inputs are finite; a program needn't handle non-finite values. No bound on the sum of `train_tokens` on one device may be relied on, other than what follows from the above.
Results may differ from the reference program's by a relative error of at most 0.0029.
Values may be sent and summed in bfloat16 or wider, within the bound.
No kernel may reach another device: no remote copies, remote signals or barrier semaphores. Data moves between devices by JAX's collectives and lax.ppermute only.
A program may use at most 64 MiB of HBM per device.

```python
import math
import jax
import jax.numpy as jnp
import numpy as np
from jax import lax

D = 8192
FF = 28672
KS = 512
KA = 256
R = 32
RQ = 4
QUERIES = 16
TRAIN = 16


def raised(entries, key, source, target, parts, factor):
    def block_of(position):
        return (jnp.arange(entries.shape[position]) // (entries.shape[position] // parts)).reshape((-1,) + (1,) * (entries.ndim - 1 - position))

    first = jax.random.permutation(key, parts)[block_of(target)]
    far = (block_of(target) + parts // 2) % parts
    return jnp.where((block_of(source) == first) | (block_of(source) == far), factor * entries, entries)


def shard_levels(rng, dims, shards, smallest, high):
    gain = 1.0
    for position, shards_of in shards:
        heights = jax.random.uniform(jax.random.fold_in(jax.random.fold_in(rng, 6), position), (shards_of,), jnp.float32, smallest / len(shards), high / len(shards))
        gain = gain * jnp.repeat(jnp.exp(heights), dims[position] // shards_of).reshape((-1,) + (1,) * (len(dims) - 1 - position))
    return gain


def split_up(number_of, total, reach, lean):
    loads = [(1 << 20) // math.isqrt(standing ** lean) + 1 for standing in range(2, number_of + 1)]
    spare, given = total - reach - (number_of - 1), [1] * (number_of - 1)
    while spare > 0:
        free = [i for i in range(number_of - 1) if given[i] < reach]
        pool, remaining = sum([loads[i] for i in free]), spare
        for i in free:
            extra = min(reach - given[i], max(1, remaining * loads[i] // pool), spare)
            given[i] = given[i] + extra
            spare = spare - extra
    return np.array([reach] + given)


def uneven_parts(stream_key, amount, total, most, slope):
    if amount == 2:
        one = jax.random.randint(stream_key, (), max(1, total - most), min(most, total - 1) + 1)
        return jnp.stack([one, total - one])
    sizes = jnp.asarray(split_up(amount, total, most, slope), jnp.int32)
    twos = (amount - 1) // 2
    giver, taker = sizes[1:1 + 2 * twos:2], sizes[2:2 + 2 * twos:2]
    margin = jnp.minimum(giver - 1, most - taker)
    shifted = jax.random.randint(jax.random.fold_in(stream_key, 1), (twos,), 0, 1 << 20) % (margin + 1)
    sizes = sizes.at[1:1 + 2 * twos:2].set(giver - shifted).at[2:2 + 2 * twos:2].set(taker + shifted)
    return sizes[jax.random.permutation(jax.random.fold_in(stream_key, 2), amount)]


def gaussian(own_key, extent, spread, bound, cuts=(), held_as=jnp.bfloat16):
    gain = shard_levels(own_key, extent, cuts, -0.22, 0.18) if cuts else 1.0
    result = jax.random.normal(own_key, extent, jnp.float32) * spread * gain
    return jnp.minimum(jnp.maximum(result, -bound), bound).astype(held_as)


def gaussian_with(key, extent, deviation, limit, split, heavy, held_as=jnp.bfloat16):
    array = deviation * jax.random.normal(key, extent, jnp.float32)
    if split:
        array = array * shard_levels(key, extent, split, -0.22, 0.18)
    return jnp.clip(raised(array, jax.random.fold_in(key, 3), *heavy), -limit, limit).astype(held_as)


def setup_inputs(seed: int = 0, part: int = 0) -> dict:
    key_of = jax.random.split(jax.random.key(seed), 10)
    own_keys = jax.random.split(jax.random.fold_in(key_of[9], part), 10)
    return {
        "query_out": gaussian_with(key_of[0], (FF, QUERIES * RQ), 1.0, 6.0, ((0, 8),), (0, 1, 8, 2.0)),
        "query_act": gaussian_with(key_of[1], (D, QUERIES * RQ), 1.0, 6.0, ((0, 8),), (0, 1, 8, 2.0)),
        "out_basis": gaussian(key_of[2], (FF, KS), FF ** -0.5, 0.03125, ((0, 8), (1, 2))),
        "act_basis": gaussian(key_of[3], (D, KA), D ** -0.5, 0.0625, ((0, 8), (1, 2))),
        "eigenvalues": jnp.clip(jnp.exp(math.log(5.0) - 4.6051702 * jax.random.uniform(key_of[4], (KS, KA), jnp.float32) ** shard_levels(key_of[4], (KS, KA), ((0, 2),), -0.2, 0.2)), 0.05, 5.0),
        "train_out": gaussian(own_keys[5], (TRAIN, R, KS), 0.0125, 0.078125, ((0, 16),)),
        "train_act": gaussian(own_keys[6], (TRAIN, R, KA), 0.0125, 0.078125, ((0, 16),)),
        "train_tokens": uneven_parts(own_keys[7], TRAIN, TRAIN * R // 2, R, 2).astype(jnp.int32),
        "train_ids": jax.random.permutation(own_keys[8], TRAIN).astype(jnp.int32),
    }


damping = 0.1


def reference(query_out, query_act, out_basis, act_basis, eigenvalues, train_out, train_act, train_tokens, train_ids):
    out_coords = jnp.dot(query_out.T, out_basis, preferred_element_type=jnp.float32)
    act_coords = jnp.dot(query_act.T, act_basis, preferred_element_type=jnp.float32)
    queries = out_coords.shape[0] // RQ
    out_three = out_coords.reshape(queries, RQ, KS)
    act_three = act_coords.reshape(queries, RQ, KA)
    numer = jnp.einsum("qri,qrj->qij", out_three, act_three, precision=lax.Precision.HIGHEST)
    precond = (numer / (eigenvalues + damping)).astype(jnp.bfloat16)
    flat_precond = precond.astype(jnp.float32).reshape(queries, KS * KA)
    factor_rows = train_out.shape[1]

    def score_example(example):
        out_rows, act_rows, tokens = example
        valid = (jnp.arange(factor_rows, dtype=jnp.int32) < tokens).astype(jnp.float32)
        dense = jnp.dot(out_rows.astype(jnp.float32).T, act_rows.astype(jnp.float32) * valid[:, None], precision=lax.Precision.HIGHEST)
        return jnp.dot(flat_precond, dense.reshape(KS * KA), precision=lax.Precision.HIGHEST)

    columns = lax.map(score_example, (train_out, train_act, train_tokens))
    total = train_out.shape[0]
    return jnp.zeros((queries, total), jnp.float32).at[:, train_ids].set(columns.T)
```

```python
import functools

import jax
import jax.numpy as jnp
from jax import lax
from jax.experimental import pallas as pl
from jax.experimental.pallas import tpu as pltpu
from jax.sharding import PartitionSpec as P

RQ = 4
LANES = 128
MOST_DIRECT = 16


damping = 0.1


def chunk_count(rows):
    for chunks in (4, 2):
        if rows % (chunks * LANES) == 0:
            return chunks
    return 1


def project_kernel(
    chunks,
    parts,
    place_ref,
    query_out,
    query_act,
    out_basis,
    act_basis,
    *rest,
):
    pieces = rest[:parts]
    q_out, q_act, b_out, b_act, total, sems = rest[parts:]
    rows = query_out.shape[1] // chunks
    copies = []
    for c in range(chunks):
        cut = pl.ds(c * rows, rows)
        copies.append(
            (
                pltpu.make_async_copy(query_out.at[:, cut], q_out.at[:, cut], sems.at[2 * c]),
                pltpu.make_async_copy(out_basis.at[cut, :], b_out.at[cut, :], sems.at[2 * c + 1]),
            )
        )
    copies.append(
        (
            pltpu.make_async_copy(query_act, q_act, sems.at[2 * chunks]),
            pltpu.make_async_copy(act_basis, b_act, sems.at[2 * chunks + 1]),
        )
    )
    for pair in copies:
        for copy in pair:
            copy.start()
    out_part = None
    for c in range(chunks):
        for copy in copies[c]:
            copy.wait()
        cut = pl.ds(c * rows, rows)
        term = jnp.dot(q_out[:, cut], b_out[cut, :], preferred_element_type=jnp.float32)
        out_part = term if out_part is None else out_part + term
    for copy in copies[chunks]:
        copy.wait()
    half_ks = b_out.shape[1]
    total[:, :half_ks] = out_part
    total[:, half_ks:] = jnp.dot(q_act[...], b_act[...], preferred_element_type=jnp.float32)
    place = place_ref[0]
    local_rows = total.shape[0] // parts
    for k in range(parts):
        target = lax.rem(place + k, parts)
        start = pl.multiple_of(target * local_rows, local_rows)
        pieces[k][...] = total[pl.ds(start, local_rows), :]


def project(place, query_out, query_act, out_basis, act_basis, parts):
    columns = query_out.shape[0]
    width = out_basis.shape[1] + act_basis.shape[1]
    chunks = chunk_count(query_out.shape[1])
    anywhere = pl.BlockSpec(memory_space=pl.ANY)
    return pl.pallas_call(
        functools.partial(project_kernel, chunks, parts),
        out_shape=[jax.ShapeDtypeStruct((columns // parts, width), jnp.float32)] * parts,
        in_specs=[pl.BlockSpec(memory_space=pltpu.SMEM)] + [anywhere] * 4,
        out_specs=[pl.BlockSpec(memory_space=pltpu.VMEM)] * parts,
        scratch_shapes=[
            pltpu.VMEM(query_out.shape, query_out.dtype),
            pltpu.VMEM(query_act.shape, query_act.dtype),
            pltpu.VMEM(out_basis.shape, out_basis.dtype),
            pltpu.VMEM(act_basis.shape, act_basis.dtype),
            pltpu.VMEM((columns, width), jnp.float32),
            pltpu.SemaphoreType.DMA((2 * chunks + 2,)),
        ],
        compiler_params=pltpu.CompilerParams(vmem_limit_bytes=24 * 2**20),
    )(place, query_out, query_act, out_basis, act_basis)


def pack_kernel(meta_ref, train_out, train_act, packed):
    rows, ks = train_out.shape[1:]
    ka = train_act.shape[2]
    keep = lax.broadcasted_iota(jnp.int32, (rows, ka), 0) < meta_ref[0]
    act = jnp.where(keep, train_act[0].astype(jnp.float32), 0.0)
    packed[:, :ks] = train_out[0]
    packed[:, ks : ks + ka] = act.astype(packed.dtype)
    ident = jnp.full((rows, LANES), meta_ref[1], jnp.int32).astype(jnp.float32)
    packed[:, ks + ka :] = ident.astype(packed.dtype)


def pack(train_out, train_act, train_tokens, train_ids):
    rows, ks = train_out.shape[1:]
    width = ks + train_act.shape[2] + LANES
    return pl.pallas_call(
        pack_kernel,
        out_shape=jax.ShapeDtypeStruct((rows, width), train_out.dtype),
        in_specs=[pl.BlockSpec(memory_space=pltpu.SMEM)] + [pl.BlockSpec(memory_space=pltpu.VMEM)] * 2,
        out_specs=pl.BlockSpec(memory_space=pltpu.VMEM),
    )(jnp.concatenate([train_tokens, train_ids]), train_out, train_act)


def score_kernel(ks, ka, place_ref, coords, other_coords, eigen, other_eigen, *rest):
    blocks, out = rest[:-1], rest[-1]
    first = place_ref[0] == 0
    half = ks // 2
    low, high = (
        jnp.where(first, coords[...], other_coords[...]),
        jnp.where(first, other_coords[...], coords[...]),
    )
    low_eigen, high_eigen = (
        jnp.where(first, eigen[...], other_eigen[...]),
        jnp.where(first, other_eigen[...], eigen[...]),
    )
    act = jnp.concatenate([low[:, half:], high[:, half:]], axis=1)
    rows = jnp.concatenate([b[...].reshape(-1, b.shape[-1]) for b in blocks], axis=0)
    weights = rows[:, ks : ks + ka].astype(jnp.float32)
    column = lax.broadcasted_iota(jnp.int32, (rows.shape[0], LANES), 1).astype(jnp.float32)
    hot = rows[:, ks + ka :].astype(jnp.float32) == column
    for q in range(low.shape[0] // RQ):
        cut = slice(q * RQ, (q + 1) * RQ)
        projected = None
        for part, values, part_eigen in ((0, low, low_eigen), (1, high, high_eigen)):
            numer = lax.dot_general(
                values[cut, :half],
                act[cut],
                (((0,), (0,)), ((), ())),
                precision=lax.Precision.HIGHEST,
                preferred_element_type=jnp.float32,
            )
            precond = (numer / (part_eigen + damping)).astype(jnp.bfloat16)
            term = jnp.dot(
                rows[:, part * half : (part + 1) * half], precond, preferred_element_type=jnp.float32
            )
            projected = term if projected is None else projected + term
        per_row = jnp.sum(projected * weights, axis=1, keepdims=True)
        scores = jnp.sum(jnp.where(hot, per_row, 0.0), axis=0, keepdims=True)
        out[q : q + 1, :] = scores[:, : out.shape[1]]


def score(place, coords, other_coords, eigen, other_eigen, blocks, ks, ka, total):
    return pl.pallas_call(
        functools.partial(score_kernel, ks, ka),
        out_shape=jax.ShapeDtypeStruct((coords.shape[0] // RQ, total), jnp.float32),
        in_specs=[pl.BlockSpec(memory_space=pltpu.SMEM)]
        + [pl.BlockSpec(memory_space=pltpu.VMEM)] * (4 + len(blocks)),
        out_specs=pl.BlockSpec(memory_space=pltpu.VMEM),
        compiler_params=pltpu.CompilerParams(vmem_limit_bytes=32 * 2**20),
    )(place, coords, other_coords, eigen, other_eigen, *blocks)


def direct(
    query_out,
    query_act,
    out_basis,
    act_basis,
    eigenvalues,
    train_out,
    train_act,
    train_tokens,
    train_ids,
):
    parts = lax.axis_size("blk")
    ks, ka = train_out.shape[2], train_act.shape[2]
    swap = [(0, 1), (1, 0)]
    packed = pack(train_out, train_act, train_tokens, train_ids)
    other_eigen = lax.ppermute(eigenvalues, "fsdp", swap)
    blocks = [packed]
    for k in range(1, parts):
        blocks.append(lax.ppermute(packed, "blk", [(s, (s + k) % parts) for s in range(parts)]))
    stacked = jnp.stack(blocks)
    other = lax.ppermute(stacked, "fsdp", swap)
    place = lax.axis_index("blk").reshape(1)
    pieces = project(place, query_out.T, query_act.T, out_basis, act_basis, parts)
    coords = pieces[0]
    for k in range(1, parts):
        coords = coords + lax.ppermute(pieces[k], "blk", [(s, (s + k) % parts) for s in range(parts)])
    other_coords = lax.ppermute(coords, "fsdp", swap)
    core = lax.axis_index("fsdp").reshape(1)
    total = parts * 2 * train_out.shape[0]
    return score(
        core, coords, other_coords, eigenvalues, other_eigen, [stacked, other], ks, ka, total
    )


def score_block(precond, out_rows, act_rows, token_counts):
    factor_rows = out_rows.shape[1]
    valid = (
        lax.broadcasted_iota(jnp.int32, (out_rows.shape[0], factor_rows), 1) < token_counts[:, None]
    ).astype(jnp.float32)
    projected = jnp.einsum("nri,qij->nrqj", out_rows, precond, preferred_element_type=jnp.float32)
    weights = act_rows.astype(jnp.float32) * valid[:, :, None]
    return jnp.einsum("nrqj,nrj->qn", projected, weights, precision=lax.Precision.HIGHEST)


def gathered(
    query_out,
    query_act,
    out_basis,
    act_basis,
    eigenvalues,
    train_out,
    train_act,
    train_tokens,
    train_ids,
):
    half_ks = out_basis.shape[1]
    local_rows = query_out.shape[1] // lax.axis_size("blk")
    out_part = lax.dot_general(
        query_out, out_basis, (((0,), (0,)), ((), ())), preferred_element_type=jnp.float32
    )
    act_part = lax.dot_general(
        query_act, act_basis, (((0,), (0,)), ((), ())), preferred_element_type=jnp.float32
    )
    rotated = lax.psum_scatter(
        jnp.concatenate([out_part, act_part], axis=1), "blk", scatter_dimension=0, tiled=True
    )
    out_coords = rotated[:, :half_ks]
    act_half = rotated[:, half_ks:]
    act_coords = lax.all_gather(act_half, "fsdp", axis=1, tiled=True)
    queries = local_rows // RQ
    out_three = out_coords.reshape(queries, RQ, half_ks)
    act_three = act_coords.reshape(queries, RQ, act_coords.shape[1])
    numer = jnp.einsum("qri,qrj->qij", out_three, act_three, precision=lax.Precision.HIGHEST)
    precond = (numer / (eigenvalues + damping)).astype(jnp.bfloat16)
    train_total = train_out.shape[0] * lax.axis_size("blk") * lax.axis_size("fsdp")
    empty = jnp.zeros((queries, train_total), jnp.float32)
    full_precond = lax.all_gather(precond, "fsdp", axis=1, tiled=True)
    out_rows = lax.all_gather(train_out, "blk", axis=0, tiled=True)
    act_rows = lax.all_gather(train_act, "blk", axis=0, tiled=True)
    token_counts = lax.all_gather(train_tokens, "blk", axis=0, tiled=True)
    column_ids = lax.all_gather(train_ids, "blk", axis=0, tiled=True)
    scores = empty.at[:, column_ids].add(
        score_block(full_precond, out_rows, act_rows, token_counts)
    )
    return lax.psum(scores, "fsdp")


def solution(mesh):
    few = mesh.shape["blk"] <= MOST_DIRECT and mesh.shape["fsdp"] == 2
    return jax.shard_map(
        direct if few else gathered,
        mesh=mesh,
        in_specs=(
            P("blk", None),
            P("blk", None),
            P("blk", "fsdp"),
            P("blk", "fsdp"),
            P("fsdp", None),
            P(("groups", "blk", "fsdp"), None, None),
            P(("groups", "blk", "fsdp"), None, None),
            P(("groups", "blk", "fsdp")),
            P(("groups", "blk", "fsdp")),
        ),
        out_specs=P("blk", "groups"),
        check_vma=False,
    )
```

```python
import functools

import jax
import jax.numpy as jnp
from jax import lax
from jax.experimental import pallas as pl
from jax.experimental.pallas import tpu as pltpu
from jax.sharding import PartitionSpec as P

RQ = 4
LANES = 128
MOST_DIRECT = 16


damping = 0.1


def chunk_count(rows):
    for chunks in (4, 2):
        if rows % (chunks * LANES) == 0:
            return chunks
    return 1


def project_kernel(
    chunks, query_out, query_act, out_basis, act_basis, pieces, q_out, q_act, b_out, b_act, sems
):
    rows = query_out.shape[1] // chunks
    copies = []
    for c in range(chunks):
        cut = pl.ds(c * rows, rows)
        copies.append(
            (
                pltpu.make_async_copy(query_out.at[:, cut], q_out.at[:, cut], sems.at[2 * c]),
                pltpu.make_async_copy(out_basis.at[cut, :], b_out.at[cut, :], sems.at[2 * c + 1]),
            )
        )
    copies.append(
        (
            pltpu.make_async_copy(query_act, q_act, sems.at[2 * chunks]),
            pltpu.make_async_copy(act_basis, b_act, sems.at[2 * chunks + 1]),
        )
    )
    for pair in copies:
        for copy in pair:
            copy.start()
    out_part = None
    for c in range(chunks):
        for copy in copies[c]:
            copy.wait()
        cut = pl.ds(c * rows, rows)
        term = jnp.dot(q_out[:, cut], b_out[cut, :], preferred_element_type=jnp.float32)
        out_part = term if out_part is None else out_part + term
    for copy in copies[chunks]:
        copy.wait()
    act_part = jnp.dot(q_act[...], b_act[...], preferred_element_type=jnp.float32)
    parts, cores, local_rows, _ = pieces.shape
    half_ks = b_out.shape[1]
    for part in range(parts):
        cut = slice(part * local_rows, (part + 1) * local_rows)
        for core in range(cores):
            pieces[part, core, :, :half_ks] = out_part[cut]
            pieces[part, core, :, half_ks:] = act_part[cut]


def project(query_out, query_act, out_basis, act_basis, parts, cores):
    columns = query_out.shape[0]
    width = out_basis.shape[1] + act_basis.shape[1]
    chunks = chunk_count(query_out.shape[1])
    return pl.pallas_call(
        functools.partial(project_kernel, chunks),
        out_shape=jax.ShapeDtypeStruct((parts, cores, columns // parts, width), jnp.float32),
        in_specs=[pl.BlockSpec(memory_space=pltpu.HBM)] * 4,
        out_specs=pl.BlockSpec(memory_space=pltpu.VMEM),
        scratch_shapes=[
            pltpu.VMEM(query_out.shape, query_out.dtype),
            pltpu.VMEM(query_act.shape, query_act.dtype),
            pltpu.VMEM(out_basis.shape, out_basis.dtype),
            pltpu.VMEM(act_basis.shape, act_basis.dtype),
            pltpu.SemaphoreType.DMA((2 * chunks + 2,)),
        ],
        compiler_params=pltpu.CompilerParams(vmem_limit_bytes=60 * 2**20),
    )(query_out, query_act, out_basis, act_basis)


def pack_kernel(tokens_ref, ids_ref, train_out, train_act, packed):
    rows, ks = train_out.shape[1:]
    ka = train_act.shape[2]
    keep = lax.broadcasted_iota(jnp.int32, (rows, ka), 0) < tokens_ref[0]
    act = jnp.where(keep, train_act[0].astype(jnp.float32), 0.0).astype(packed.dtype)
    ident = jnp.full((rows, LANES), ids_ref[0], jnp.int32).astype(jnp.float32).astype(packed.dtype)
    for part in range(packed.shape[0]):
        packed[part, :, :ks] = train_out[0]
        packed[part, :, ks : ks + ka] = act
        packed[part, :, ks + ka :] = ident


def pack(train_out, train_act, train_tokens, train_ids, parts):
    rows, ks = train_out.shape[1:]
    width = ks + train_act.shape[2] + LANES
    return pl.pallas_call(
        pack_kernel,
        out_shape=jax.ShapeDtypeStruct((parts, rows, width), train_out.dtype),
        in_specs=[pl.BlockSpec(memory_space=pltpu.SMEM)] * 2
        + [pl.BlockSpec(memory_space=pltpu.VMEM)] * 2,
        out_specs=pl.BlockSpec(memory_space=pltpu.VMEM),
    )(train_tokens, train_ids, train_out, train_act)


def score_kernel(ks, ka, place_ref, pieces, eigen, other_eigen, *rest):
    blocks, out = rest[:-1], rest[-1]
    first = place_ref[0] == 0
    half = ks // 2
    values = jnp.sum(pieces[...], axis=0)
    coords = (values[0], values[1])
    eigens = (
        jnp.where(first, eigen[...], other_eigen[...]),
        jnp.where(first, other_eigen[...], eigen[...]),
    )
    act = jnp.concatenate([v[:, half:] for v in coords], axis=1)
    rows = jnp.concatenate([b[...].reshape(-1, b.shape[-1]) for b in blocks], axis=0)
    weights = rows[:, ks : ks + ka].astype(jnp.float32)
    column = lax.broadcasted_iota(jnp.int32, (rows.shape[0], LANES), 1).astype(jnp.float32)
    hot = rows[:, ks + ka :].astype(jnp.float32) == column
    for q in range(act.shape[0] // RQ):
        cut = slice(q * RQ, (q + 1) * RQ)
        projected = None
        for part in range(2):
            numer = lax.dot_general(
                coords[part][cut, :half],
                act[cut],
                (((0,), (0,)), ((), ())),
                precision=lax.Precision.HIGHEST,
                preferred_element_type=jnp.float32,
            )
            precond = (numer / (eigens[part] + damping)).astype(jnp.bfloat16)
            term = jnp.dot(
                rows[:, part * half : (part + 1) * half], precond, preferred_element_type=jnp.float32
            )
            projected = term if projected is None else projected + term
        per_row = jnp.sum(projected * weights, axis=1, keepdims=True)
        scores = jnp.sum(jnp.where(hot, per_row, 0.0), axis=0, keepdims=True)
        out[q : q + 1, :] = scores[:, : out.shape[1]]


def score(core, pieces, eigen, other_eigen, blocks, ks, ka, total):
    return pl.pallas_call(
        functools.partial(score_kernel, ks, ka),
        out_shape=jax.ShapeDtypeStruct((pieces.shape[2] // RQ, total), jnp.float32),
        in_specs=[pl.BlockSpec(memory_space=pltpu.SMEM)]
        + [pl.BlockSpec(memory_space=pltpu.VMEM)] * (3 + len(blocks)),
        out_specs=pl.BlockSpec(memory_space=pltpu.VMEM),
        compiler_params=pltpu.CompilerParams(vmem_limit_bytes=32 * 2**20),
    )(core, pieces, eigen, other_eigen, *blocks)


def direct(
    query_out,
    query_act,
    out_basis,
    act_basis,
    eigenvalues,
    train_out,
    train_act,
    train_tokens,
    train_ids,
):
    parts, cores = lax.axis_size("blk"), lax.axis_size("fsdp")
    ks, ka = train_out.shape[2], train_act.shape[2]
    swap = [(0, 1), (1, 0)]
    pieces = project(query_out.T, query_act.T, out_basis, act_basis, parts, cores)
    pieces = lax.all_to_all(
        pieces.reshape(parts * cores, *pieces.shape[2:]), ("blk", "fsdp"), 0, 0, tiled=True
    ).reshape(pieces.shape)
    packed = pack(train_out, train_act, train_tokens, train_ids, parts)
    stacked = lax.all_to_all(packed, "blk", 0, 0, tiled=True)
    other = lax.ppermute(stacked, "fsdp", swap)
    other_eigen = lax.ppermute(eigenvalues, "fsdp", swap)
    core = lax.axis_index("fsdp").reshape(1)
    total = parts * cores * train_out.shape[0]
    return score(core, pieces, eigenvalues, other_eigen, [stacked, other], ks, ka, total)


def score_block(precond, out_rows, act_rows, token_counts):
    factor_rows = out_rows.shape[1]
    valid = (
        lax.broadcasted_iota(jnp.int32, (out_rows.shape[0], factor_rows), 1) < token_counts[:, None]
    ).astype(jnp.float32)
    projected = jnp.einsum("nri,qij->nrqj", out_rows, precond, preferred_element_type=jnp.float32)
    weights = act_rows.astype(jnp.float32) * valid[:, :, None]
    return jnp.einsum("nrqj,nrj->qn", projected, weights, precision=lax.Precision.HIGHEST)


def gathered(
    query_out,
    query_act,
    out_basis,
    act_basis,
    eigenvalues,
    train_out,
    train_act,
    train_tokens,
    train_ids,
):
    half_ks = out_basis.shape[1]
    local_rows = query_out.shape[1] // lax.axis_size("blk")
    out_part = lax.dot_general(
        query_out, out_basis, (((0,), (0,)), ((), ())), preferred_element_type=jnp.float32
    )
    act_part = lax.dot_general(
        query_act, act_basis, (((0,), (0,)), ((), ())), preferred_element_type=jnp.float32
    )
    rotated = lax.psum_scatter(
        jnp.concatenate([out_part, act_part], axis=1), "blk", scatter_dimension=0, tiled=True
    )
    out_coords = rotated[:, :half_ks]
    act_half = rotated[:, half_ks:]
    act_coords = lax.all_gather(act_half, "fsdp", axis=1, tiled=True)
    queries = local_rows // RQ
    out_three = out_coords.reshape(queries, RQ, half_ks)
    act_three = act_coords.reshape(queries, RQ, act_coords.shape[1])
    numer = jnp.einsum("qri,qrj->qij", out_three, act_three, precision=lax.Precision.HIGHEST)
    precond = (numer / (eigenvalues + damping)).astype(jnp.bfloat16)
    train_total = train_out.shape[0] * lax.axis_size("blk") * lax.axis_size("fsdp")
    empty = jnp.zeros((queries, train_total), jnp.float32)
    full_precond = lax.all_gather(precond, "fsdp", axis=1, tiled=True)
    out_rows = lax.all_gather(train_out, "blk", axis=0, tiled=True)
    act_rows = lax.all_gather(train_act, "blk", axis=0, tiled=True)
    token_counts = lax.all_gather(train_tokens, "blk", axis=0, tiled=True)
    column_ids = lax.all_gather(train_ids, "blk", axis=0, tiled=True)
    scores = empty.at[:, column_ids].add(
        score_block(full_precond, out_rows, act_rows, token_counts)
    )
    return lax.psum(scores, "fsdp")


def solution(mesh):
    few = mesh.shape["blk"] <= MOST_DIRECT and mesh.shape["fsdp"] == 2
    return jax.shard_map(
        direct if few else gathered,
        mesh=mesh,
        in_specs=(
            P("blk", None),
            P("blk", None),
            P("blk", "fsdp"),
            P("blk", "fsdp"),
            P("fsdp", None),
            P(("groups", "blk", "fsdp"), None, None),
            P(("groups", "blk", "fsdp"), None, None),
            P(("groups", "blk", "fsdp")),
            P(("groups", "blk", "fsdp")),
        ),
        out_specs=P("blk", "groups"),
        check_vma=False,
    )
```

```python
import functools

import jax
import jax.numpy as jnp
from jax import lax
from jax.experimental import pallas as pl
from jax.experimental.pallas import tpu as pltpu
from jax.sharding import PartitionSpec as P

RQ = 4
LANES = 128
MOST_DIRECT = 16


damping = 0.1


def chunk_count(rows):
    for chunks in (4, 2):
        if rows % (chunks * LANES) == 0:
            return chunks
    return 1


def project_kernel(
    chunks,
    place_ref,
    query_out,
    query_act,
    out_basis,
    act_basis,
    pieces,
    q_out,
    q_act,
    b_out,
    b_act,
    total,
    sems,
):
    rows = query_out.shape[1] // chunks
    copies = []
    for c in range(chunks):
        cut = pl.ds(c * rows, rows)
        copies.append(
            (
                pltpu.make_async_copy(query_out.at[:, cut], q_out.at[:, cut], sems.at[2 * c]),
                pltpu.make_async_copy(out_basis.at[cut, :], b_out.at[cut, :], sems.at[2 * c + 1]),
            )
        )
    copies.append(
        (
            pltpu.make_async_copy(query_act, q_act, sems.at[2 * chunks]),
            pltpu.make_async_copy(act_basis, b_act, sems.at[2 * chunks + 1]),
        )
    )
    for pair in copies:
        for copy in pair:
            copy.start()
    out_part = None
    for c in range(chunks):
        for copy in copies[c]:
            copy.wait()
        cut = pl.ds(c * rows, rows)
        term = jnp.dot(q_out[:, cut], b_out[cut, :], preferred_element_type=jnp.float32)
        out_part = term if out_part is None else out_part + term
    for copy in copies[chunks]:
        copy.wait()
    act_part = jnp.dot(q_act[...], b_act[...], preferred_element_type=jnp.float32)
    half_ks = b_out.shape[1]
    total[:, :half_ks] = out_part
    total[:, half_ks:] = act_part
    parts, local_rows, _ = pieces.shape
    for part in range(parts):
        start = pl.multiple_of((place_ref[0] ^ part) * local_rows, local_rows)
        pieces[part] = total[pl.ds(start, local_rows), :]


def project(place, query_out, query_act, out_basis, act_basis, parts):
    columns = query_out.shape[0]
    width = out_basis.shape[1] + act_basis.shape[1]
    chunks = chunk_count(query_out.shape[1])
    return pl.pallas_call(
        functools.partial(project_kernel, chunks),
        out_shape=jax.ShapeDtypeStruct((parts, columns // parts, width), jnp.float32),
        in_specs=[pl.BlockSpec(memory_space=pltpu.SMEM)]
        + [pl.BlockSpec(memory_space=pltpu.HBM)] * 4,
        out_specs=pl.BlockSpec(memory_space=pltpu.VMEM),
        scratch_shapes=[
            pltpu.VMEM(query_out.shape, query_out.dtype),
            pltpu.VMEM(query_act.shape, query_act.dtype),
            pltpu.VMEM(out_basis.shape, out_basis.dtype),
            pltpu.VMEM(act_basis.shape, act_basis.dtype),
            pltpu.VMEM((columns, width), jnp.float32),
            pltpu.SemaphoreType.DMA((2 * chunks + 2,)),
        ],
        compiler_params=pltpu.CompilerParams(vmem_limit_bytes=60 * 2**20),
    )(place, query_out, query_act, out_basis, act_basis)


def pack_kernel(tokens_ref, ids_ref, train_out, train_act, packed):
    rows, ks = train_out.shape[1:]
    ka = train_act.shape[2]
    keep = lax.broadcasted_iota(jnp.int32, (rows, ka), 0) < tokens_ref[0]
    act = jnp.where(keep, train_act[0].astype(jnp.float32), 0.0).astype(packed.dtype)
    ident = jnp.full((rows, LANES), ids_ref[0], jnp.int32).astype(jnp.float32).astype(packed.dtype)
    packed[0, :, :ks] = train_out[0]
    packed[0, :, ks : ks + ka] = act
    packed[0, :, ks + ka :] = ident


def pack(train_out, train_act, train_tokens, train_ids):
    rows, ks = train_out.shape[1:]
    width = ks + train_act.shape[2] + LANES
    return pl.pallas_call(
        pack_kernel,
        out_shape=jax.ShapeDtypeStruct((1, rows, width), train_out.dtype),
        in_specs=[pl.BlockSpec(memory_space=pltpu.SMEM)] * 2
        + [pl.BlockSpec(memory_space=pltpu.VMEM)] * 2,
        out_specs=pl.BlockSpec(memory_space=pltpu.VMEM),
    )(train_tokens, train_ids, train_out, train_act)


def score_kernel(ks, ka, place_ref, own, other, eigen, other_eigen, *rest):
    blocks, out = rest[:-1], rest[-1]
    first = place_ref[0] == 0
    half = ks // 2
    coords = (
        jnp.where(first, own[...], other[...]),
        jnp.where(first, other[...], own[...]),
    )
    eigens = (
        jnp.where(first, eigen[...], other_eigen[...]),
        jnp.where(first, other_eigen[...], eigen[...]),
    )
    act = jnp.concatenate([v[:, half:] for v in coords], axis=1)
    rows = jnp.concatenate([b[...].reshape(-1, b.shape[-1]) for b in blocks], axis=0)
    weights = rows[:, ks : ks + ka].astype(jnp.float32)
    column = lax.broadcasted_iota(jnp.int32, (rows.shape[0], LANES), 1).astype(jnp.float32)
    hot = rows[:, ks + ka :].astype(jnp.float32) == column
    for q in range(act.shape[0] // RQ):
        cut = slice(q * RQ, (q + 1) * RQ)
        projected = None
        for part in range(2):
            numer = lax.dot_general(
                coords[part][cut, :half],
                act[cut],
                (((0,), (0,)), ((), ())),
                precision=lax.Precision.HIGHEST,
                preferred_element_type=jnp.float32,
            )
            precond = (numer / (eigens[part] + damping)).astype(jnp.bfloat16)
            term = jnp.dot(
                rows[:, part * half : (part + 1) * half], precond, preferred_element_type=jnp.float32
            )
            projected = term if projected is None else projected + term
        per_row = jnp.sum(projected * weights, axis=1, keepdims=True)
        scores = jnp.sum(jnp.where(hot, per_row, 0.0), axis=0, keepdims=True)
        out[q : q + 1, :] = scores[:, : out.shape[1]]


def score(core, own, other, eigen, other_eigen, blocks, ks, ka, total):
    return pl.pallas_call(
        functools.partial(score_kernel, ks, ka),
        out_shape=jax.ShapeDtypeStruct((own.shape[0] // RQ, total), jnp.float32),
        in_specs=[pl.BlockSpec(memory_space=pltpu.SMEM)]
        + [pl.BlockSpec(memory_space=pltpu.VMEM)] * (4 + len(blocks)),
        out_specs=pl.BlockSpec(memory_space=pltpu.VMEM),
        compiler_params=pltpu.CompilerParams(vmem_limit_bytes=32 * 2**20),
    )(core, own, other, eigen, other_eigen, *blocks)


def direct(
    query_out,
    query_act,
    out_basis,
    act_basis,
    eigenvalues,
    train_out,
    train_act,
    train_tokens,
    train_ids,
):
    parts, cores = lax.axis_size("blk"), lax.axis_size("fsdp")
    ks, ka = train_out.shape[2], train_act.shape[2]
    swap = [(0, 1), (1, 0)]

    def across(x, bit):
        return lax.ppermute(x, "blk", [(s, s ^ bit) for s in range(parts)])

    bits = [1 << i for i in range(parts.bit_length() - 1)]
    place = lax.axis_index("blk").reshape(1)
    core = lax.axis_index("fsdp").reshape(1)
    block = pack(train_out, train_act, train_tokens, train_ids)
    for bit in reversed(bits):
        block = jnp.concatenate([block, across(block, bit)], axis=0)
    other_block = lax.ppermute(block, "fsdp", swap)
    other_eigen = lax.ppermute(eigenvalues, "fsdp", swap)
    pieces = project(place, query_out.T, query_act.T, out_basis, act_basis, parts)
    pieces = pieces.reshape((2,) * len(bits) + pieces.shape[1:])
    for bit in bits:
        moved = lax.index_in_dim(pieces, 1, len(bits) - bit.bit_length(), keepdims=True)
        kept = lax.index_in_dim(pieces, 0, len(bits) - bit.bit_length(), keepdims=True)
        pieces = kept + across(moved, bit)
    coords = pieces.reshape(pieces.shape[-2:])
    other = lax.ppermute(coords, "fsdp", swap)
    total = parts * cores * train_out.shape[0]
    return score(
        core, coords, other, eigenvalues, other_eigen, [block, other_block], ks, ka, total
    )


def score_block(precond, out_rows, act_rows, token_counts):
    factor_rows = out_rows.shape[1]
    valid = (
        lax.broadcasted_iota(jnp.int32, (out_rows.shape[0], factor_rows), 1) < token_counts[:, None]
    ).astype(jnp.float32)
    projected = jnp.einsum("nri,qij->nrqj", out_rows, precond, preferred_element_type=jnp.float32)
    weights = act_rows.astype(jnp.float32) * valid[:, :, None]
    return jnp.einsum("nrqj,nrj->qn", projected, weights, precision=lax.Precision.HIGHEST)


def gathered(
    query_out,
    query_act,
    out_basis,
    act_basis,
    eigenvalues,
    train_out,
    train_act,
    train_tokens,
    train_ids,
):
    half_ks = out_basis.shape[1]
    local_rows = query_out.shape[1] // lax.axis_size("blk")
    out_part = lax.dot_general(
        query_out, out_basis, (((0,), (0,)), ((), ())), preferred_element_type=jnp.float32
    )
    act_part = lax.dot_general(
        query_act, act_basis, (((0,), (0,)), ((), ())), preferred_element_type=jnp.float32
    )
    rotated = lax.psum_scatter(
        jnp.concatenate([out_part, act_part], axis=1), "blk", scatter_dimension=0, tiled=True
    )
    out_coords = rotated[:, :half_ks]
    act_half = rotated[:, half_ks:]
    act_coords = lax.all_gather(act_half, "fsdp", axis=1, tiled=True)
    queries = local_rows // RQ
    out_three = out_coords.reshape(queries, RQ, half_ks)
    act_three = act_coords.reshape(queries, RQ, act_coords.shape[1])
    numer = jnp.einsum("qri,qrj->qij", out_three, act_three, precision=lax.Precision.HIGHEST)
    precond = (numer / (eigenvalues + damping)).astype(jnp.bfloat16)
    train_total = train_out.shape[0] * lax.axis_size("blk") * lax.axis_size("fsdp")
    empty = jnp.zeros((queries, train_total), jnp.float32)
    full_precond = lax.all_gather(precond, "fsdp", axis=1, tiled=True)
    out_rows = lax.all_gather(train_out, "blk", axis=0, tiled=True)
    act_rows = lax.all_gather(train_act, "blk", axis=0, tiled=True)
    token_counts = lax.all_gather(train_tokens, "blk", axis=0, tiled=True)
    column_ids = lax.all_gather(train_ids, "blk", axis=0, tiled=True)
    scores = empty.at[:, column_ids].add(
        score_block(full_precond, out_rows, act_rows, token_counts)
    )
    return lax.psum(scores, "fsdp")


def solution(mesh):
    parts = mesh.shape["blk"]
    few = parts <= MOST_DIRECT and parts & (parts - 1) == 0 and mesh.shape["fsdp"] == 2
    return jax.shard_map(
        direct if few else gathered,
        mesh=mesh,
        in_specs=(
            P("blk", None),
            P("blk", None),
            P("blk", "fsdp"),
            P("blk", "fsdp"),
            P("fsdp", None),
            P(("groups", "blk", "fsdp"), None, None),
            P(("groups", "blk", "fsdp"), None, None),
            P(("groups", "blk", "fsdp")),
            P(("groups", "blk", "fsdp")),
        ),
        out_specs=P("blk", "groups"),
        check_vma=False,
    )
```

```python
import functools

import jax
import jax.numpy as jnp
from jax import lax
from jax.experimental import pallas as pl
from jax.experimental.pallas import tpu as pltpu
from jax.sharding import PartitionSpec as P

RQ = 4
LANES = 128
MOST_DIRECT = 16


damping = 0.1


def chunk_count(rows):
    for chunks in (4, 2):
        if rows % (chunks * LANES) == 0:
            return chunks
    return 1


def project_kernel(
    chunks,
    place_ref,
    tokens_ref,
    ids_ref,
    query_out,
    query_act,
    out_basis,
    act_basis,
    pieces,
    q_out,
    q_act,
    b_out,
    b_act,
    sems,
):
    rows = query_out.shape[1] // chunks
    copies = []
    for c in range(chunks):
        cut = pl.ds(c * rows, rows)
        copies.append(
            (
                pltpu.make_async_copy(query_out.at[:, cut], q_out.at[:, cut], sems.at[2 * c]),
                pltpu.make_async_copy(out_basis.at[cut, :], b_out.at[cut, :], sems.at[2 * c + 1]),
            )
        )
    copies.append(
        (
            pltpu.make_async_copy(query_act, q_act, sems.at[2 * chunks]),
            pltpu.make_async_copy(act_basis, b_act, sems.at[2 * chunks + 1]),
        )
    )
    for pair in copies:
        for copy in pair:
            copy.start()
    parts, local_rows, _ = pieces.shape
    half_ks, half_ka = b_out.shape[1], b_act.shape[1]
    row = lax.broadcasted_iota(jnp.int32, (local_rows, LANES), 0)
    lane = lax.broadcasted_iota(jnp.int32, (local_rows, LANES), 1)
    facts = jnp.where(lane < LANES // 2, ids_ref[0], tokens_ref[0]).astype(jnp.float32)
    for part in range(parts):
        slot = doubling_slot(part, parts)
        pieces[place_ref[0] ^ part, :, half_ks + half_ka :] = jnp.where(row == slot, facts, 0.0)
    out_part = None
    for c in range(chunks):
        for copy in copies[c]:
            copy.wait()
        cut = pl.ds(c * rows, rows)
        term = jnp.dot(q_out[:, cut], b_out[cut, :], preferred_element_type=jnp.float32)
        out_part = term if out_part is None else out_part + term
    pieces[:, :, :half_ks] = out_part.reshape(parts, local_rows, half_ks)
    for copy in copies[chunks]:
        copy.wait()
    act_part = jnp.dot(q_act[...], b_act[...], preferred_element_type=jnp.float32)
    pieces[:, :, half_ks : half_ks + half_ka] = act_part.reshape(parts, local_rows, half_ka)


def doubling_slot(distance, parts):
    bits = parts.bit_length() - 1
    return sum(1 << (bits - 1 - i) for i in range(bits) if distance >> i & 1)


def project(place, tokens, ids, query_out, query_act, out_basis, act_basis, parts):
    columns = query_out.shape[0]
    width = out_basis.shape[1] + act_basis.shape[1] + LANES
    chunks = chunk_count(query_out.shape[1])
    return pl.pallas_call(
        functools.partial(project_kernel, chunks),
        out_shape=jax.ShapeDtypeStruct((parts, columns // parts, width), jnp.float32),
        in_specs=[pl.BlockSpec(memory_space=pltpu.SMEM)] * 3
        + [pl.BlockSpec(memory_space=pltpu.HBM)] * 4,
        out_specs=pl.BlockSpec(memory_space=pltpu.VMEM),
        scratch_shapes=[
            pltpu.VMEM(query_out.shape, query_out.dtype),
            pltpu.VMEM(query_act.shape, query_act.dtype),
            pltpu.VMEM(out_basis.shape, out_basis.dtype),
            pltpu.VMEM(act_basis.shape, act_basis.dtype),
            pltpu.SemaphoreType.DMA((2 * chunks + 2,)),
        ],
        compiler_params=pltpu.CompilerParams(vmem_limit_bytes=60 * 2**20),
        cost_estimate=pl.CostEstimate(
            flops=2 * columns * (out_basis.size + act_basis.size),
            bytes_accessed=2 * (out_basis.size + act_basis.size + query_out.size + query_act.size),
            transcendentals=0,
        ),
    )(place, tokens, ids, query_out, query_act, out_basis, act_basis)


def precondition_kernel(core_ref, own, other, eigen, other_eigen, precond):
    first = core_ref[0] == 0
    half = eigen.shape[0]
    ka = eigen.shape[1]
    coords = (
        jnp.where(first, own[...], other[...]),
        jnp.where(first, other[...], own[...]),
    )
    eigens = (
        jnp.where(first, eigen[...], other_eigen[...]),
        jnp.where(first, other_eigen[...], eigen[...]),
    )
    act = jnp.concatenate([v[:, half : half + ka // 2] for v in coords], axis=1)
    for part in range(2):
        scale = eigens[part] + damping
        for q in range(precond.shape[0]):
            cut = slice(q * RQ, (q + 1) * RQ)
            numer = lax.dot_general(
                coords[part][cut, :half],
                act[cut],
                (((0,), (0,)), ((), ())),
                precision=lax.Precision.HIGHEST,
                preferred_element_type=jnp.float32,
            )
            precond[q, part * half : (part + 1) * half, :] = (numer / scale).astype(jnp.bfloat16)


def precondition(core, own, other, eigen, other_eigen):
    half, ka = eigen.shape
    return pl.pallas_call(
        precondition_kernel,
        out_shape=jax.ShapeDtypeStruct((own.shape[0] // RQ, 2 * half, ka), jnp.bfloat16),
        in_specs=[pl.BlockSpec(memory_space=pltpu.SMEM)]
        + [pl.BlockSpec(memory_space=pltpu.VMEM)] * 4,
        out_specs=pl.BlockSpec(memory_space=pltpu.VMEM),
        cost_estimate=pl.CostEstimate(
            flops=16 * own.shape[0] * half * ka, bytes_accessed=16 * half * ka, transcendentals=0
        ),
    )(core, own, other, eigen, other_eigen)


def score_kernel(precond, own, other, block, other_block, out):
    ks, ka = precond.shape[1:]
    examples, factor_rows, _ = block.shape
    scores = [0.0] * precond.shape[0]
    for coords, rows in ((own, block), (other, other_block)):
        facts = coords[:, coords.shape[1] - LANES :]
        ids, tokens = facts[:, :1], facts[:, LANES // 2 : LANES // 2 + 1]
        lane = lax.broadcasted_iota(jnp.int32, (examples, LANES), 1).astype(jnp.float32)
        hot = lane == ids
        row = lax.broadcasted_iota(jnp.int32, (examples, factor_rows, ka), 1).astype(jnp.float32)
        weights = jnp.where(row < tokens[:, :, None], rows[:, :, ks:].astype(jnp.float32), 0.0)
        flat = rows[:, :, :ks].reshape(examples * factor_rows, ks)
        for q in range(precond.shape[0]):
            projected = jnp.dot(flat, precond[q], preferred_element_type=jnp.float32)
            terms = projected.reshape(examples, factor_rows, ka) * weights
            per_example = jnp.sum(jnp.sum(terms, axis=1), axis=1, keepdims=True)
            scores[q] += jnp.sum(jnp.where(hot, per_example, 0.0), axis=0, keepdims=True)
    for q, value in enumerate(scores):
        out[q : q + 1, :] = value[:, : out.shape[1]]


def score(precond, own, other, block, other_block):
    return pl.pallas_call(
        score_kernel,
        out_shape=jax.ShapeDtypeStruct(
            (precond.shape[0], block.shape[0] + other_block.shape[0]), jnp.float32
        ),
        in_specs=[pl.BlockSpec(memory_space=pltpu.VMEM)] * 5,
        out_specs=pl.BlockSpec(memory_space=pltpu.VMEM),
    )(precond, own, other, block, other_block)


def direct(
    query_out,
    query_act,
    out_basis,
    act_basis,
    eigenvalues,
    train_out,
    train_act,
    train_tokens,
    train_ids,
):
    parts = lax.axis_size("blk")
    swap = [(0, 1), (1, 0)]
    place = lax.axis_index("blk").reshape(1)
    core = lax.axis_index("fsdp").reshape(1)
    block = jnp.concatenate([train_out, train_act], axis=2)
    for i in reversed(range(parts.bit_length() - 1)):
        pairs = [(s, s ^ (1 << i)) for s in range(parts)]
        block = jnp.concatenate([block, lax.ppermute(block, "blk", pairs)], axis=0)
    other_block = lax.ppermute(block, "fsdp", swap)
    other_eigen = lax.ppermute(eigenvalues, "fsdp", swap)
    pieces = project(
        place, train_tokens, train_ids, query_out.T, query_act.T, out_basis, act_basis, parts
    )
    own = jnp.sum(lax.all_to_all(pieces, "blk", 0, 0, tiled=True), axis=0)
    other = lax.ppermute(own, "fsdp", swap)
    precond = precondition(core, own, other, eigenvalues, other_eigen)
    return score(precond, own, other, block, other_block)


def score_block(precond, out_rows, act_rows, token_counts):
    factor_rows = out_rows.shape[1]
    valid = (
        lax.broadcasted_iota(jnp.int32, (out_rows.shape[0], factor_rows), 1) < token_counts[:, None]
    ).astype(jnp.float32)
    projected = jnp.einsum("nri,qij->nrqj", out_rows, precond, preferred_element_type=jnp.float32)
    weights = act_rows.astype(jnp.float32) * valid[:, :, None]
    return jnp.einsum("nrqj,nrj->qn", projected, weights, precision=lax.Precision.HIGHEST)


def gathered(
    query_out,
    query_act,
    out_basis,
    act_basis,
    eigenvalues,
    train_out,
    train_act,
    train_tokens,
    train_ids,
):
    half_ks = out_basis.shape[1]
    local_rows = query_out.shape[1] // lax.axis_size("blk")
    out_part = lax.dot_general(
        query_out, out_basis, (((0,), (0,)), ((), ())), preferred_element_type=jnp.float32
    )
    act_part = lax.dot_general(
        query_act, act_basis, (((0,), (0,)), ((), ())), preferred_element_type=jnp.float32
    )
    rotated = lax.psum_scatter(
        jnp.concatenate([out_part, act_part], axis=1), "blk", scatter_dimension=0, tiled=True
    )
    out_coords = rotated[:, :half_ks]
    act_half = rotated[:, half_ks:]
    act_coords = lax.all_gather(act_half, "fsdp", axis=1, tiled=True)
    queries = local_rows // RQ
    out_three = out_coords.reshape(queries, RQ, half_ks)
    act_three = act_coords.reshape(queries, RQ, act_coords.shape[1])
    numer = jnp.einsum("qri,qrj->qij", out_three, act_three, precision=lax.Precision.HIGHEST)
    precond = (numer / (eigenvalues + damping)).astype(jnp.bfloat16)
    train_total = train_out.shape[0] * lax.axis_size("blk") * lax.axis_size("fsdp")
    empty = jnp.zeros((queries, train_total), jnp.float32)
    full_precond = lax.all_gather(precond, "fsdp", axis=1, tiled=True)
    out_rows = lax.all_gather(train_out, "blk", axis=0, tiled=True)
    act_rows = lax.all_gather(train_act, "blk", axis=0, tiled=True)
    token_counts = lax.all_gather(train_tokens, "blk", axis=0, tiled=True)
    column_ids = lax.all_gather(train_ids, "blk", axis=0, tiled=True)
    scores = empty.at[:, column_ids].add(
        score_block(full_precond, out_rows, act_rows, token_counts)
    )
    return lax.psum(scores, "fsdp")


def solution(mesh):
    parts = mesh.shape["blk"]
    few = parts <= MOST_DIRECT and parts & (parts - 1) == 0 and mesh.shape["fsdp"] == 2
    return jax.shard_map(
        direct if few else gathered,
        mesh=mesh,
        in_specs=(
            P("blk", None),
            P("blk", None),
            P("blk", "fsdp"),
            P("blk", "fsdp"),
            P("fsdp", None),
            P(("groups", "blk", "fsdp"), None, None),
            P(("groups", "blk", "fsdp"), None, None),
            P(("groups", "blk", "fsdp")),
            P(("groups", "blk", "fsdp")),
        ),
        out_specs=P("blk", "groups"),
        check_vma=False,
    )
```

```python
import functools

import jax
import jax.numpy as jnp
from jax import lax
from jax.experimental import pallas as pl
from jax.experimental.pallas import tpu as pltpu
from jax.sharding import PartitionSpec as P

RQ = 4
LANES = 128
MOST_DIRECT = 16


damping = 0.1


def chunk_count(rows):
    for chunks in (4, 2):
        if rows % (chunks * LANES) == 0:
            return chunks
    return 1


def pinned(x):
    return pltpu.with_memory_space_constraint(x, pltpu.HBM)


def spec(space):
    return pl.BlockSpec(memory_space=space)


def pack_kernel(train_out, train_act, packed, sems):
    ks = train_out.shape[2]
    copies = (
        pltpu.make_async_copy(train_out, packed.at[:, :, :ks], sems.at[0]),
        pltpu.make_async_copy(train_act, packed.at[:, :, ks:], sems.at[1]),
    )
    for copy in copies:
        copy.start()
    for copy in copies:
        copy.wait()


def pack(train_out, train_act):
    examples, rows, ks = train_out.shape
    shape = (examples, rows, ks + train_act.shape[2])
    return pl.pallas_call(
        pack_kernel,
        out_shape=jax.ShapeDtypeStruct(shape, train_out.dtype),
        in_specs=[spec(pltpu.HBM)] * 2,
        out_specs=spec(pltpu.VMEM),
        scratch_shapes=[pltpu.SemaphoreType.DMA((2,))],
    )(pinned(train_out), pinned(train_act))


def join_kernel(after, first, second, joined):
    del after
    count = first.shape[0]
    joined[:count] = first[...]
    joined[count:] = second[...]


def joined_shape(first, second):
    return jax.ShapeDtypeStruct(
        (first.shape[0] + second.shape[0],) + first.shape[1:], first.dtype
    )


def join(after, first, second):
    return pl.pallas_call(
        join_kernel,
        out_shape=joined_shape(first, second),
        in_specs=[spec(pl.ANY)] + [spec(pltpu.VMEM)] * 2,
        out_specs=spec(pltpu.VMEM),
    )(after, first, second)


def fold_kernel(held, summand, first, second, kept, moved, joined):
    for part in range(kept.shape[0]):
        kept[part] = held[2 * part] + summand[2 * part]
        moved[part] = held[2 * part + 1] + summand[2 * part + 1]
    join_kernel(None, first, second, joined)


def fold(held, summand, first, second):
    half = jax.ShapeDtypeStruct((held.shape[0] // 2,) + held.shape[1:], held.dtype)
    return pl.pallas_call(
        fold_kernel,
        out_shape=[half, half, joined_shape(first, second)],
        in_specs=[spec(pltpu.VMEM)] * 4,
        out_specs=[spec(pltpu.VMEM)] * 3,
    )(held, summand, first, second)


def project_kernel(
    chunks, query_out, query_act, out_basis, act_basis, total, q_out, q_act, b_out, b_act, sems
):
    rows = query_out.shape[1] // chunks
    copies = []
    for c in range(chunks):
        cut = pl.ds(c * rows, rows)
        copies.append(
            (
                pltpu.make_async_copy(query_out.at[:, cut], q_out.at[:, cut], sems.at[2 * c]),
                pltpu.make_async_copy(out_basis.at[cut, :], b_out.at[cut, :], sems.at[2 * c + 1]),
            )
        )
    copies.append(
        (
            pltpu.make_async_copy(query_act, q_act, sems.at[2 * chunks]),
            pltpu.make_async_copy(act_basis, b_act, sems.at[2 * chunks + 1]),
        )
    )
    for pair in copies:
        for copy in pair:
            copy.start()
    half_ks = b_out.shape[1]
    out_part = None
    for c in range(chunks):
        for copy in copies[c]:
            copy.wait()
        cut = pl.ds(c * rows, rows)
        term = jnp.dot(q_out[:, cut], b_out[cut, :], preferred_element_type=jnp.float32)
        out_part = term if out_part is None else out_part + term
    total[:, :half_ks] = out_part
    for copy in copies[chunks]:
        copy.wait()
    total[:, half_ks:] = jnp.dot(q_act[...], b_act[...], preferred_element_type=jnp.float32)


def project(query_out, query_act, out_basis, act_basis):
    columns = query_out.shape[0]
    width = out_basis.shape[1] + act_basis.shape[1]
    chunks = chunk_count(query_out.shape[1])
    operands = (query_out, query_act, out_basis, act_basis)
    return pl.pallas_call(
        functools.partial(project_kernel, chunks),
        out_shape=jax.ShapeDtypeStruct((columns, width), jnp.float32),
        in_specs=[spec(pltpu.HBM)] * len(operands),
        out_specs=spec(pltpu.VMEM),
        scratch_shapes=[pltpu.VMEM(x.shape, x.dtype) for x in operands]
        + [pltpu.SemaphoreType.DMA((2 * chunks + 2,))],
        compiler_params=pltpu.CompilerParams(vmem_limit_bytes=16 * 2**20),
        cost_estimate=pl.CostEstimate(
            flops=2 * columns * (out_basis.size + act_basis.size),
            bytes_accessed=2 * sum(x.size for x in operands),
            transcendentals=0,
        ),
    )(*[pinned(x) for x in operands])


def doubling_slot(distance, parts):
    bits = parts.bit_length() - 1
    return sum(1 << (bits - 1 - i) for i in range(bits) if distance >> i & 1)


def spread_kernel(
    place_ref, tokens_ref, ids_ref, after, total, first, second, kept, moved, joined
):
    del after
    parts = 2 * kept.shape[0]
    local_rows = kept.shape[1]
    width = total.shape[1]
    row = lax.broadcasted_iota(jnp.int32, (local_rows, LANES), 0)
    lane = lax.broadcasted_iota(jnp.int32, (local_rows, LANES), 1)
    facts = jnp.where(lane < LANES // 2, ids_ref[0], tokens_ref[0]).astype(jnp.float32)
    for part in range(parts):
        start = pl.multiple_of((place_ref[0] ^ part) * local_rows, local_rows)
        piece = (moved if part % 2 else kept).at[part // 2]
        piece[:, :width] = total[pl.ds(start, local_rows), :]
        piece[:, width:] = jnp.where(row == doubling_slot(part, parts), facts, 0.0)
    join_kernel(None, first, second, joined)


def spread(place, tokens, ids, after, total, first, second, parts):
    half = jax.ShapeDtypeStruct(
        (parts // 2, total.shape[0] // parts, total.shape[1] + LANES), jnp.float32
    )
    return pl.pallas_call(
        spread_kernel,
        out_shape=[half, half, joined_shape(first, second)],
        in_specs=[spec(pltpu.SMEM)] * 3 + [spec(pl.ANY)] + [spec(pltpu.VMEM)] * 3,
        out_specs=[spec(pltpu.VMEM)] * 3,
    )(place, tokens, ids, after, total, first, second)


def split_three(x):
    high = x.astype(jnp.bfloat16)
    rest = x - high.astype(jnp.float32)
    middle = rest.astype(jnp.bfloat16)
    low = (rest - middle.astype(jnp.float32)).astype(jnp.bfloat16)
    return high, middle, low


def score_kernel(core_ref, own, other, eigen, other_eigen, block, other_block, out):
    first = core_ref[0] == 0
    half, ka = eigen.shape
    examples, factor_rows, width = block.shape
    ks = width - ka
    coords = (
        jnp.where(first, own[...], other[...]),
        jnp.where(first, other[...], own[...]),
    )
    eigens = (
        jnp.where(first, eigen[...], other_eigen[...]),
        jnp.where(first, other_eigen[...], eigen[...]),
    )
    scales = [1.0 / (e + damping) for e in eigens]
    act = jnp.concatenate([v[:, half : half + ka // 2] for v in coords], axis=1)
    act_terms = split_three(act)
    out_terms = [split_three(v[:, :half]) for v in coords]
    order = ((0, 0), (0, 1), (1, 0), (1, 1), (0, 2), (2, 0))
    weights, hot, flat = [], [], []
    lane = lax.broadcasted_iota(jnp.int32, (examples, LANES), 1).astype(jnp.float32)
    row = lax.broadcasted_iota(jnp.int32, (examples, factor_rows, ka), 1).astype(jnp.float32)
    for facts, rows in ((own, block), (other, other_block)):
        facts = facts[:, facts.shape[1] - LANES :]
        hot.append(lane == facts[:, :1])
        keep = row < facts[:, LANES // 2 : LANES // 2 + 1][:, :, None]
        weights.append(jnp.where(keep, rows[:, :, ks:].astype(jnp.float32), 0.0))
        flat.append(rows[:, :, :ks].reshape(examples * factor_rows, ks))
    for q in range(out.shape[0]):
        cut = slice(q * RQ, (q + 1) * RQ)
        right = jnp.concatenate([act_terms[b][cut] for _, b in order], axis=0)
        precond = []
        for part in range(2):
            left = jnp.concatenate([out_terms[part][a][cut] for a, _ in order], axis=0)
            numer = lax.dot_general(
                left, right, (((0,), (0,)), ((), ())), preferred_element_type=jnp.float32
            )
            precond.append((numer * scales[part]).astype(jnp.bfloat16))
        precond = jnp.concatenate(precond, axis=0)
        scores = 0.0
        for side in range(2):
            projected = jnp.dot(flat[side], precond, preferred_element_type=jnp.float32)
            terms = projected.reshape(examples, factor_rows, ka) * weights[side]
            per_example = jnp.sum(jnp.sum(terms, axis=1), axis=1, keepdims=True)
            scores += jnp.sum(jnp.where(hot[side], per_example, 0.0), axis=0, keepdims=True)
        out[q : q + 1, :] = scores[:, : out.shape[1]]


def score(core, own, other, eigen, other_eigen, block, other_block):
    return pl.pallas_call(
        score_kernel,
        out_shape=jax.ShapeDtypeStruct(
            (own.shape[0] // RQ, block.shape[0] + other_block.shape[0]), jnp.float32
        ),
        in_specs=[spec(pltpu.SMEM)] + [spec(pltpu.VMEM)] * 6,
        out_specs=spec(pltpu.VMEM),
        compiler_params=pltpu.CompilerParams(vmem_limit_bytes=16 * 2**20),
    )(core, own, other, eigen, other_eigen, block, other_block)


def direct(
    query_out,
    query_act,
    out_basis,
    act_basis,
    eigenvalues,
    train_out,
    train_act,
    train_tokens,
    train_ids,
):
    parts = lax.axis_size("blk")
    steps = parts.bit_length() - 1
    swap = [(0, 1), (1, 0)]

    def across(x, i):
        return lax.ppermute(x, "blk", [(s, s ^ (1 << i)) for s in range(parts)])

    place = lax.axis_index("blk").reshape(1)
    core = lax.axis_index("fsdp").reshape(1)
    other_eigen = lax.ppermute(eigenvalues, "fsdp", swap)
    block = pack(train_out, train_act)
    arrived = across(block, steps - 1)
    total = project(query_out.T, query_act.T, out_basis, act_basis)
    kept, moved, block = spread(
        place, train_tokens, train_ids, other_eigen, total, block, arrived, parts
    )
    for i in range(steps):
        summand = across(moved, i)
        if i < steps - 1:
            arrived = across(block, steps - 2 - i)
        if i < steps - 2:
            kept, moved, block = fold(kept, summand, block, arrived)
        elif i < steps - 1:
            sums = kept + summand
            kept, moved = sums[:1], sums[1:]
    own = kept + summand
    block = join(own, block, arrived)
    own = own.reshape(own.shape[1:])
    other = lax.ppermute(own, "fsdp", swap)
    other_block = lax.ppermute(block, "fsdp", swap)
    return score(core, own, other, eigenvalues, other_eigen, block, other_block)


def score_block(precond, out_rows, act_rows, token_counts):
    factor_rows = out_rows.shape[1]
    valid = (
        lax.broadcasted_iota(jnp.int32, (out_rows.shape[0], factor_rows), 1) < token_counts[:, None]
    ).astype(jnp.float32)
    projected = jnp.einsum("nri,qij->nrqj", out_rows, precond, preferred_element_type=jnp.float32)
    weights = act_rows.astype(jnp.float32) * valid[:, :, None]
    return jnp.einsum("nrqj,nrj->qn", projected, weights, precision=lax.Precision.HIGHEST)


def gathered(
    query_out,
    query_act,
    out_basis,
    act_basis,
    eigenvalues,
    train_out,
    train_act,
    train_tokens,
    train_ids,
):
    half_ks = out_basis.shape[1]
    local_rows = query_out.shape[1] // lax.axis_size("blk")
    out_part = lax.dot_general(
        query_out, out_basis, (((0,), (0,)), ((), ())), preferred_element_type=jnp.float32
    )
    act_part = lax.dot_general(
        query_act, act_basis, (((0,), (0,)), ((), ())), preferred_element_type=jnp.float32
    )
    rotated = lax.psum_scatter(
        jnp.concatenate([out_part, act_part], axis=1), "blk", scatter_dimension=0, tiled=True
    )
    out_coords = rotated[:, :half_ks]
    act_half = rotated[:, half_ks:]
    act_coords = lax.all_gather(act_half, "fsdp", axis=1, tiled=True)
    queries = local_rows // RQ
    out_three = out_coords.reshape(queries, RQ, half_ks)
    act_three = act_coords.reshape(queries, RQ, act_coords.shape[1])
    numer = jnp.einsum("qri,qrj->qij", out_three, act_three, precision=lax.Precision.HIGHEST)
    precond = (numer / (eigenvalues + damping)).astype(jnp.bfloat16)
    train_total = train_out.shape[0] * lax.axis_size("blk") * lax.axis_size("fsdp")
    empty = jnp.zeros((queries, train_total), jnp.float32)
    full_precond = lax.all_gather(precond, "fsdp", axis=1, tiled=True)
    out_rows = lax.all_gather(train_out, "blk", axis=0, tiled=True)
    act_rows = lax.all_gather(train_act, "blk", axis=0, tiled=True)
    token_counts = lax.all_gather(train_tokens, "blk", axis=0, tiled=True)
    column_ids = lax.all_gather(train_ids, "blk", axis=0, tiled=True)
    scores = empty.at[:, column_ids].add(
        score_block(full_precond, out_rows, act_rows, token_counts)
    )
    return lax.psum(scores, "fsdp")


def solution(mesh):
    parts = mesh.shape["blk"]
    few = parts <= MOST_DIRECT and parts & (parts - 1) == 0 and mesh.shape["fsdp"] == 2
    return jax.shard_map(
        direct if few else gathered,
        mesh=mesh,
        in_specs=(
            P("blk", None),
            P("blk", None),
            P("blk", "fsdp"),
            P("blk", "fsdp"),
            P("fsdp", None),
            P(("groups", "blk", "fsdp"), None, None),
            P(("groups", "blk", "fsdp"), None, None),
            P(("groups", "blk", "fsdp")),
            P(("groups", "blk", "fsdp")),
        ),
        out_specs=P("blk", "groups"),
        check_vma=False,
    )
```

```python
import functools

import jax
import jax.numpy as jnp
from jax import lax
from jax.experimental import pallas as pl
from jax.experimental.pallas import tpu as pltpu
from jax.sharding import PartitionSpec as P

RQ = 4
LANES = 128
MOST_DIRECT = 16


damping = 0.1


def chunk_count(rows):
    for chunks in (4, 2):
        if rows % (chunks * LANES) == 0:
            return chunks
    return 1


def pinned(x):
    return pltpu.with_memory_space_constraint(x, pltpu.HBM)


def grant(mebibytes):
    return pltpu.CompilerParams(vmem_limit_bytes=mebibytes * 2**20)


def spec(space):
    return pl.BlockSpec(memory_space=space)


def pack_kernel(train_out, train_act, packed, sems):
    ks = train_out.shape[2]
    copies = (
        pltpu.make_async_copy(train_out, packed.at[:, :, :ks], sems.at[0]),
        pltpu.make_async_copy(train_act, packed.at[:, :, ks:], sems.at[1]),
    )
    for copy in copies:
        copy.start()
    for copy in copies:
        copy.wait()


def pack(train_out, train_act):
    examples, rows, ks = train_out.shape
    shape = (examples, rows, ks + train_act.shape[2])
    return pl.pallas_call(
        pack_kernel,
        out_shape=jax.ShapeDtypeStruct(shape, train_out.dtype),
        in_specs=[spec(pltpu.HBM)] * 2,
        out_specs=spec(pltpu.VMEM),
        scratch_shapes=[pltpu.SemaphoreType.DMA((2,))],
        compiler_params=grant(2),
    )(pinned(train_out), pinned(train_act))


def join_kernel(after, first, second, joined):
    del after
    count = first.shape[0]
    joined[:count] = first[...]
    joined[count:] = second[...]


def joined_shape(first, second):
    return jax.ShapeDtypeStruct(
        (first.shape[0] + second.shape[0],) + first.shape[1:], first.dtype
    )


def join(after, first, second):
    return pl.pallas_call(
        join_kernel,
        out_shape=joined_shape(first, second),
        in_specs=[spec(pl.ANY)] + [spec(pltpu.VMEM)] * 2,
        out_specs=spec(pltpu.VMEM),
        compiler_params=grant(4),
    )(after, first, second)


def project_kernel(
    chunks, query_out, query_act, out_basis, act_basis, total, q_out, q_act, b_out, b_act, sems
):
    rows = query_out.shape[1] // chunks
    copies = []
    for c in range(chunks):
        cut = pl.ds(c * rows, rows)
        copies.append(
            (
                pltpu.make_async_copy(query_out.at[:, cut], q_out.at[:, cut], sems.at[2 * c]),
                pltpu.make_async_copy(out_basis.at[cut, :], b_out.at[cut, :], sems.at[2 * c + 1]),
            )
        )
    copies.append(
        (
            pltpu.make_async_copy(query_act, q_act, sems.at[2 * chunks]),
            pltpu.make_async_copy(act_basis, b_act, sems.at[2 * chunks + 1]),
        )
    )
    for pair in copies:
        for copy in pair:
            copy.start()
    half_ks = b_out.shape[1]
    out_part = None
    for c in range(chunks):
        for copy in copies[c]:
            copy.wait()
        cut = pl.ds(c * rows, rows)
        term = jnp.dot(q_out[:, cut], b_out[cut, :], preferred_element_type=jnp.float32)
        out_part = term if out_part is None else out_part + term
    total[:, :half_ks] = out_part
    for copy in copies[chunks]:
        copy.wait()
    total[:, half_ks:] = jnp.dot(q_act[...], b_act[...], preferred_element_type=jnp.float32)


def project(query_out, query_act, out_basis, act_basis):
    columns = query_out.shape[0]
    width = out_basis.shape[1] + act_basis.shape[1]
    chunks = chunk_count(query_out.shape[1])
    operands = (query_out, query_act, out_basis, act_basis)
    return pl.pallas_call(
        functools.partial(project_kernel, chunks),
        out_shape=jax.ShapeDtypeStruct((columns, width), jnp.float32),
        in_specs=[spec(pltpu.HBM)] * len(operands),
        out_specs=spec(pltpu.VMEM),
        scratch_shapes=[pltpu.VMEM(x.shape, x.dtype) for x in operands]
        + [pltpu.SemaphoreType.DMA((2 * chunks + 2,))],
        compiler_params=grant(8),
        cost_estimate=pl.CostEstimate(
            flops=2 * columns * (out_basis.size + act_basis.size),
            bytes_accessed=2 * sum(x.size for x in operands),
            transcendentals=0,
        ),
    )(*[pinned(x) for x in operands])


def doubling_slot(distance, parts):
    bits = parts.bit_length() - 1
    return sum(1 << (bits - 1 - i) for i in range(bits) if distance >> i & 1)


def spread_kernel(
    place_ref, tokens_ref, ids_ref, after, total, first, second, kept, moved, joined
):
    del after
    parts = 2 * kept.shape[0]
    local_rows = kept.shape[1]
    width = total.shape[1]
    row = lax.broadcasted_iota(jnp.int32, (local_rows, LANES), 0)
    lane = lax.broadcasted_iota(jnp.int32, (local_rows, LANES), 1)
    facts = jnp.where(lane < LANES // 2, ids_ref[0], tokens_ref[0]).astype(jnp.float32)
    for part in range(parts):
        start = pl.multiple_of((place_ref[0] ^ part) * local_rows, local_rows)
        piece = (moved if part % 2 else kept).at[part // 2]
        piece[:, :width] = total[pl.ds(start, local_rows), :]
        piece[:, width:] = jnp.where(row == doubling_slot(part, parts), facts, 0.0)
    join_kernel(None, first, second, joined)


def spread(place, tokens, ids, after, total, first, second, parts):
    half = jax.ShapeDtypeStruct(
        (parts // 2, total.shape[0] // parts, total.shape[1] + LANES), jnp.float32
    )
    return pl.pallas_call(
        spread_kernel,
        out_shape=[half, half, joined_shape(first, second)],
        in_specs=[spec(pltpu.SMEM)] * 3 + [spec(pl.ANY)] + [spec(pltpu.VMEM)] * 3,
        out_specs=[spec(pltpu.VMEM)] * 3,
        compiler_params=grant(4),
    )(place, tokens, ids, after, total, first, second)


def split_three(x):
    high = x.astype(jnp.bfloat16)
    rest = x - high.astype(jnp.float32)
    middle = rest.astype(jnp.bfloat16)
    low = (rest - middle.astype(jnp.float32)).astype(jnp.bfloat16)
    return high, middle, low


def score_kernel(core_ref, own, other, eigen, other_eigen, block, other_block, out):
    first = core_ref[0] == 0
    half, ka = eigen.shape
    examples, factor_rows, width = block.shape
    ks = width - ka
    coords = (
        jnp.where(first, own[...], other[...]),
        jnp.where(first, other[...], own[...]),
    )
    eigens = (
        jnp.where(first, eigen[...], other_eigen[...]),
        jnp.where(first, other_eigen[...], eigen[...]),
    )
    scales = [1.0 / (e + damping) for e in eigens]
    act = jnp.concatenate([v[:, half : half + ka // 2] for v in coords], axis=1)
    act_terms = split_three(act)
    out_terms = [split_three(v[:, :half]) for v in coords]
    order = ((0, 0), (0, 1), (1, 0), (1, 1), (0, 2), (2, 0))
    weights, hot, flat = [], [], []
    lane = lax.broadcasted_iota(jnp.int32, (examples, LANES), 1).astype(jnp.float32)
    row = lax.broadcasted_iota(jnp.int32, (examples, factor_rows, ka), 1).astype(jnp.float32)
    for facts, rows in ((own, block), (other, other_block)):
        facts = facts[:, facts.shape[1] - LANES :]
        hot.append(lane == facts[:, :1])
        keep = row < facts[:, LANES // 2 : LANES // 2 + 1][:, :, None]
        weights.append(jnp.where(keep, rows[:, :, ks:].astype(jnp.float32), 0.0))
        flat.append(rows[:, :, :ks].reshape(examples * factor_rows, ks))
    for q in range(out.shape[0]):
        cut = slice(q * RQ, (q + 1) * RQ)
        right = jnp.concatenate([act_terms[b][cut] for _, b in order], axis=0)
        precond = []
        for part in range(2):
            left = jnp.concatenate([out_terms[part][a][cut] for a, _ in order], axis=0)
            numer = lax.dot_general(
                left, right, (((0,), (0,)), ((), ())), preferred_element_type=jnp.float32
            )
            precond.append((numer * scales[part]).astype(jnp.bfloat16))
        precond = jnp.concatenate(precond, axis=0)
        scores = 0.0
        for side in range(2):
            projected = jnp.dot(flat[side], precond, preferred_element_type=jnp.float32)
            terms = projected.reshape(examples, factor_rows, ka) * weights[side]
            per_example = jnp.sum(jnp.sum(terms, axis=1), axis=1, keepdims=True)
            scores += jnp.sum(jnp.where(hot[side], per_example, 0.0), axis=0, keepdims=True)
        out[q : q + 1, :] = scores[:, : out.shape[1]]


def score(core, own, other, eigen, other_eigen, block, other_block):
    return pl.pallas_call(
        score_kernel,
        out_shape=jax.ShapeDtypeStruct(
            (own.shape[0] // RQ, block.shape[0] + other_block.shape[0]), jnp.float32
        ),
        in_specs=[spec(pltpu.SMEM)] + [spec(pltpu.VMEM)] * 6,
        out_specs=spec(pltpu.VMEM),
        compiler_params=grant(12),
    )(core, own, other, eigen, other_eigen, block, other_block)


def direct(
    query_out,
    query_act,
    out_basis,
    act_basis,
    eigenvalues,
    train_out,
    train_act,
    train_tokens,
    train_ids,
):
    parts = lax.axis_size("blk")
    steps = parts.bit_length() - 1
    swap = [(0, 1), (1, 0)]

    def across(x, i):
        return lax.ppermute(x, "blk", [(s, s ^ (1 << i)) for s in range(parts)])

    place = lax.axis_index("blk").reshape(1)
    core = lax.axis_index("fsdp").reshape(1)
    other_eigen = lax.ppermute(eigenvalues, "fsdp", swap)
    block = pack(train_out, train_act)
    arrived = across(block, steps - 1)
    total = project(query_out.T, query_act.T, out_basis, act_basis)
    kept, moved, block = spread(
        place, train_tokens, train_ids, other_eigen, total, block, arrived, parts
    )
    for i in range(steps - 1):
        sums = kept + across(moved, i)
        sums = sums.reshape((sums.shape[0] // 2, 2) + sums.shape[1:])
        arrived = across(block, steps - 2 - i)
        kept, moved = sums[:, 0], sums[:, 1]
        block = join(kept, block, arrived)
    own = (kept + across(moved, steps - 1)).reshape(kept.shape[1:])
    other = lax.ppermute(own, "fsdp", swap)
    other_block = lax.ppermute(block, "fsdp", swap)
    return score(core, own, other, eigenvalues, other_eigen, block, other_block)


def score_block(precond, out_rows, act_rows, token_counts):
    factor_rows = out_rows.shape[1]
    valid = (
        lax.broadcasted_iota(jnp.int32, (out_rows.shape[0], factor_rows), 1) < token_counts[:, None]
    ).astype(jnp.float32)
    projected = jnp.einsum("nri,qij->nrqj", out_rows, precond, preferred_element_type=jnp.float32)
    weights = act_rows.astype(jnp.float32) * valid[:, :, None]
    return jnp.einsum("nrqj,nrj->qn", projected, weights, precision=lax.Precision.HIGHEST)


def gathered(
    query_out,
    query_act,
    out_basis,
    act_basis,
    eigenvalues,
    train_out,
    train_act,
    train_tokens,
    train_ids,
):
    half_ks = out_basis.shape[1]
    local_rows = query_out.shape[1] // lax.axis_size("blk")
    out_part = lax.dot_general(
        query_out, out_basis, (((0,), (0,)), ((), ())), preferred_element_type=jnp.float32
    )
    act_part = lax.dot_general(
        query_act, act_basis, (((0,), (0,)), ((), ())), preferred_element_type=jnp.float32
    )
    rotated = lax.psum_scatter(
        jnp.concatenate([out_part, act_part], axis=1), "blk", scatter_dimension=0, tiled=True
    )
    out_coords = rotated[:, :half_ks]
    act_half = rotated[:, half_ks:]
    act_coords = lax.all_gather(act_half, "fsdp", axis=1, tiled=True)
    queries = local_rows // RQ
    out_three = out_coords.reshape(queries, RQ, half_ks)
    act_three = act_coords.reshape(queries, RQ, act_coords.shape[1])
    numer = jnp.einsum("qri,qrj->qij", out_three, act_three, precision=lax.Precision.HIGHEST)
    precond = (numer / (eigenvalues + damping)).astype(jnp.bfloat16)
    train_total = train_out.shape[0] * lax.axis_size("blk") * lax.axis_size("fsdp")
    empty = jnp.zeros((queries, train_total), jnp.float32)
    full_precond = lax.all_gather(precond, "fsdp", axis=1, tiled=True)
    out_rows = lax.all_gather(train_out, "blk", axis=0, tiled=True)
    act_rows = lax.all_gather(train_act, "blk", axis=0, tiled=True)
    token_counts = lax.all_gather(train_tokens, "blk", axis=0, tiled=True)
    column_ids = lax.all_gather(train_ids, "blk", axis=0, tiled=True)
    scores = empty.at[:, column_ids].add(
        score_block(full_precond, out_rows, act_rows, token_counts)
    )
    return lax.psum(scores, "fsdp")


def solution(mesh):
    parts = mesh.shape["blk"]
    few = parts <= MOST_DIRECT and parts & (parts - 1) == 0 and mesh.shape["fsdp"] == 2
    return jax.shard_map(
        direct if few else gathered,
        mesh=mesh,
        in_specs=(
            P("blk", None),
            P("blk", None),
            P("blk", "fsdp"),
            P("blk", "fsdp"),
            P("fsdp", None),
            P(("groups", "blk", "fsdp"), None, None),
            P(("groups", "blk", "fsdp"), None, None),
            P(("groups", "blk", "fsdp")),
            P(("groups", "blk", "fsdp")),
        ),
        out_specs=P("blk", "groups"),
        check_vma=False,
    )
```

```python
import functools

import jax
import jax.numpy as jnp
from jax import lax
from jax.experimental import pallas as pl
from jax.experimental.pallas import tpu as pltpu
from jax.sharding import PartitionSpec as P

RQ = 4
LANES = 128
DIRECT_PARTS = 8


damping = 0.1


def chunk_count(rows):
    for chunks in (4, 2):
        if rows % (chunks * LANES) == 0:
            return chunks
    return 1


def pinned(x):
    return pltpu.with_memory_space_constraint(x, pltpu.HBM)


def grant(mebibytes):
    return pltpu.CompilerParams(vmem_limit_bytes=mebibytes * 2**20)


def spec(space):
    return pl.BlockSpec(memory_space=space)


def pack_kernel(train_out, train_act, packed, sems):
    ks = train_out.shape[2]
    copies = (
        pltpu.make_async_copy(train_out, packed.at[:, :, :ks], sems.at[0]),
        pltpu.make_async_copy(train_act, packed.at[:, :, ks:], sems.at[1]),
    )
    for copy in copies:
        copy.start()
    for copy in copies:
        copy.wait()


def pack(train_out, train_act):
    examples, rows, ks = train_out.shape
    shape = (examples, rows, ks + train_act.shape[2])
    return pl.pallas_call(
        pack_kernel,
        out_shape=jax.ShapeDtypeStruct(shape, train_out.dtype),
        in_specs=[spec(pltpu.HBM)] * 2,
        out_specs=spec(pltpu.VMEM),
        scratch_shapes=[pltpu.SemaphoreType.DMA((2,))],
        compiler_params=grant(2),
    )(pinned(train_out), pinned(train_act))


def joined_shape(blocks):
    first = blocks[0]
    count = sum(x.shape[0] for x in blocks)
    return jax.ShapeDtypeStruct((count,) + first.shape[1:], first.dtype)


def join_into(joined, blocks):
    start = 0
    for block in blocks:
        joined[start : start + block.shape[0]] = block[...]
        start += block.shape[0]


def finish_kernel(held, summand, *rest):
    blocks, (own, joined) = rest[:-2], rest[-2:]
    own[...] = held[...] + summand[...]
    join_into(joined, blocks)


def finish(held, summand, blocks):
    return pl.pallas_call(
        finish_kernel,
        out_shape=[jax.ShapeDtypeStruct(held.shape, held.dtype), joined_shape(blocks)],
        in_specs=[spec(pltpu.VMEM)] * (2 + len(blocks)),
        out_specs=[spec(pltpu.VMEM)] * 2,
        compiler_params=grant(4),
    )(held, summand, *blocks)


def fold_kernel(after, held, summand, kept, moved):
    del after
    for part in range(kept.shape[0]):
        kept[part] = held[2 * part] + summand[2 * part]
        moved[part] = held[2 * part + 1] + summand[2 * part + 1]


def fold(after, held, summand):
    half = jax.ShapeDtypeStruct((held.shape[0] // 2,) + held.shape[1:], held.dtype)
    return pl.pallas_call(
        fold_kernel,
        out_shape=[half, half],
        in_specs=[spec(pl.ANY)] + [spec(pltpu.VMEM)] * 2,
        out_specs=[spec(pltpu.VMEM)] * 2,
        compiler_params=grant(4),
    )(after, held, summand)


def relay_kernel(after, source, target):
    del after
    target[...] = source[...]


def relay(after, source):
    return pl.pallas_call(
        relay_kernel,
        out_shape=jax.ShapeDtypeStruct(source.shape, source.dtype),
        in_specs=[spec(pl.ANY), spec(pltpu.VMEM)],
        out_specs=spec(pltpu.VMEM),
        compiler_params=grant(2),
    )(after, source)


def project_kernel(
    chunks, query_out, query_act, out_basis, act_basis, total, q_out, q_act, b_out, b_act, sems
):
    rows = query_out.shape[1] // chunks
    copies = []
    for c in range(chunks):
        cut = pl.ds(c * rows, rows)
        copies.append(
            (
                pltpu.make_async_copy(query_out.at[:, cut], q_out.at[:, cut], sems.at[2 * c]),
                pltpu.make_async_copy(out_basis.at[cut, :], b_out.at[cut, :], sems.at[2 * c + 1]),
            )
        )
    copies.append(
        (
            pltpu.make_async_copy(query_act, q_act, sems.at[2 * chunks]),
            pltpu.make_async_copy(act_basis, b_act, sems.at[2 * chunks + 1]),
        )
    )
    for pair in copies:
        for copy in pair:
            copy.start()
    half_ks = b_out.shape[1]
    out_part = None
    for c in range(chunks):
        for copy in copies[c]:
            copy.wait()
        cut = pl.ds(c * rows, rows)
        term = jnp.dot(q_out[:, cut], b_out[cut, :], preferred_element_type=jnp.float32)
        out_part = term if out_part is None else out_part + term
    total[:, :half_ks] = out_part
    for copy in copies[chunks]:
        copy.wait()
    total[:, half_ks:] = jnp.dot(q_act[...], b_act[...], preferred_element_type=jnp.float32)


def project(query_out, query_act, out_basis, act_basis):
    columns = query_out.shape[0]
    width = out_basis.shape[1] + act_basis.shape[1]
    chunks = chunk_count(query_out.shape[1])
    operands = (query_out, query_act, out_basis, act_basis)
    return pl.pallas_call(
        functools.partial(project_kernel, chunks),
        out_shape=jax.ShapeDtypeStruct((columns, width), jnp.float32),
        in_specs=[spec(pltpu.HBM)] * len(operands),
        out_specs=spec(pltpu.VMEM),
        scratch_shapes=[pltpu.VMEM(x.shape, x.dtype) for x in operands]
        + [pltpu.SemaphoreType.DMA((2 * chunks + 2,))],
        compiler_params=grant(8),
        cost_estimate=pl.CostEstimate(
            flops=2 * columns * (out_basis.size + act_basis.size),
            bytes_accessed=2 * sum(x.size for x in operands),
            transcendentals=0,
        ),
    )(*[pinned(x) for x in operands])


def doubling_slot(distance, parts):
    bits = parts.bit_length() - 1
    return sum(1 << (bits - 1 - i) for i in range(bits) if distance >> i & 1)


def spread_kernel(
    place_ref, tokens_ref, ids_ref, after, total, first, second, kept, moved, joined
):
    del after
    parts = 2 * kept.shape[0]
    local_rows = kept.shape[1]
    width = total.shape[1]
    row = lax.broadcasted_iota(jnp.int32, (local_rows, LANES), 0)
    lane = lax.broadcasted_iota(jnp.int32, (local_rows, LANES), 1)
    facts = jnp.where(lane < LANES // 2, ids_ref[0], tokens_ref[0]).astype(jnp.float32)
    for part in range(parts):
        start = pl.multiple_of((place_ref[0] ^ part) * local_rows, local_rows)
        piece = (moved if part % 2 else kept).at[part // 2]
        piece[:, :width] = total[pl.ds(start, local_rows), :]
        piece[:, width:] = jnp.where(row == doubling_slot(part, parts), facts, 0.0)
    join_into(joined, (first, second))


def spread(place, tokens, ids, after, total, first, second, parts):
    half = jax.ShapeDtypeStruct(
        (parts // 2, total.shape[0] // parts, total.shape[1] + LANES), jnp.float32
    )
    return pl.pallas_call(
        spread_kernel,
        out_shape=[half, half, joined_shape((first, second))],
        in_specs=[spec(pltpu.SMEM)] * 3 + [spec(pl.ANY)] + [spec(pltpu.VMEM)] * 3,
        out_specs=[spec(pltpu.VMEM)] * 3,
        compiler_params=grant(4),
    )(place, tokens, ids, after, total, first, second)


def split_three(x):
    high = x.astype(jnp.bfloat16)
    rest = x - high.astype(jnp.float32)
    middle = rest.astype(jnp.bfloat16)
    low = (rest - middle.astype(jnp.float32)).astype(jnp.bfloat16)
    return high, middle, low


def score_kernel(core_ref, own, other, eigen, other_eigen, block, other_block, out):
    first = core_ref[0] == 0
    half, ka = eigen.shape
    examples, factor_rows, width = block.shape
    ks = width - ka
    coords = (
        jnp.where(first, own[...], other[...]),
        jnp.where(first, other[...], own[...]),
    )
    eigens = (
        jnp.where(first, eigen[...], other_eigen[...]),
        jnp.where(first, other_eigen[...], eigen[...]),
    )
    scales = [1.0 / (e + damping) for e in eigens]
    act = jnp.concatenate([v[:, half : half + ka // 2] for v in coords], axis=1)
    act_terms = split_three(act)
    out_terms = [split_three(v[:, :half]) for v in coords]
    order = ((0, 0), (0, 1), (1, 0), (1, 1), (0, 2), (2, 0))
    weights, hot, flat = [], [], []
    lane = lax.broadcasted_iota(jnp.int32, (examples, LANES), 1).astype(jnp.float32)
    row = lax.broadcasted_iota(jnp.int32, (examples, factor_rows, ka), 1).astype(jnp.float32)
    for facts, rows in ((own, block), (other, other_block)):
        facts = facts[:, facts.shape[1] - LANES :]
        hot.append(lane == facts[:, :1])
        keep = row < facts[:, LANES // 2 : LANES // 2 + 1][:, :, None]
        weights.append(jnp.where(keep, rows[:, :, ks:].astype(jnp.float32), 0.0))
        flat.append(rows[:, :, :ks].reshape(examples * factor_rows, ks))
    for q in range(out.shape[0]):
        cut = slice(q * RQ, (q + 1) * RQ)
        right = jnp.concatenate([act_terms[b][cut] for _, b in order], axis=0)
        precond = []
        for part in range(2):
            left = jnp.concatenate([out_terms[part][a][cut] for a, _ in order], axis=0)
            numer = lax.dot_general(
                left, right, (((0,), (0,)), ((), ())), preferred_element_type=jnp.float32
            )
            precond.append((numer * scales[part]).astype(jnp.bfloat16))
        precond = jnp.concatenate(precond, axis=0)
        scores = 0.0
        for side in range(2):
            projected = jnp.dot(flat[side], precond, preferred_element_type=jnp.float32)
            terms = projected.reshape(examples, factor_rows, ka) * weights[side]
            per_example = jnp.sum(jnp.sum(terms, axis=1), axis=1, keepdims=True)
            scores += jnp.sum(jnp.where(hot[side], per_example, 0.0), axis=0, keepdims=True)
        out[q : q + 1, :] = scores[:, : out.shape[1]]


def score(core, own, other, eigen, other_eigen, block, other_block):
    return pl.pallas_call(
        score_kernel,
        out_shape=jax.ShapeDtypeStruct(
            (own.shape[0] // RQ, block.shape[0] + other_block.shape[0]), jnp.float32
        ),
        in_specs=[spec(pltpu.SMEM)] + [spec(pltpu.VMEM)] * 6,
        out_specs=spec(pltpu.VMEM),
        compiler_params=grant(12),
    )(core, own, other, eigen, other_eigen, block, other_block)


def direct(
    query_out,
    query_act,
    out_basis,
    act_basis,
    eigenvalues,
    train_out,
    train_act,
    train_tokens,
    train_ids,
):
    parts = lax.axis_size("blk")
    steps = parts.bit_length() - 1
    swap = [(0, 1), (1, 0)]

    def across(x, i):
        return lax.ppermute(x, "blk", [(s, s ^ (1 << i)) for s in range(parts)])

    place = lax.axis_index("blk").reshape(1)
    core = lax.axis_index("fsdp").reshape(1)
    other_eigen = lax.ppermute(eigenvalues, "fsdp", swap)
    block = pack(train_out, train_act)
    arrived = across(block, steps - 1)
    total = project(query_out.T, query_act.T, out_basis, act_basis)
    kept, moved, block = spread(
        place, train_tokens, train_ids, other_eigen, total, block, arrived, parts
    )
    second = across(block, 1)
    third = across(block, 0)
    kept, moved = fold(block, kept, across(moved, 0))
    fourth = across(relay(kept, second), 0)
    kept, moved = fold(second, kept, across(moved, 1))
    own, block = finish(kept[0], across(moved[0], 2), (block, second, third, fourth))
    other = lax.ppermute(own, "fsdp", swap)
    other_block = lax.ppermute(block, "fsdp", swap)
    return score(core, own, other, eigenvalues, other_eigen, block, other_block)


def score_block(precond, out_rows, act_rows, token_counts):
    factor_rows = out_rows.shape[1]
    valid = (
        lax.broadcasted_iota(jnp.int32, (out_rows.shape[0], factor_rows), 1) < token_counts[:, None]
    ).astype(jnp.float32)
    projected = jnp.einsum("nri,qij->nrqj", out_rows, precond, preferred_element_type=jnp.float32)
    weights = act_rows.astype(jnp.float32) * valid[:, :, None]
    return jnp.einsum("nrqj,nrj->qn", projected, weights, precision=lax.Precision.HIGHEST)


def gathered(
    query_out,
    query_act,
    out_basis,
    act_basis,
    eigenvalues,
    train_out,
    train_act,
    train_tokens,
    train_ids,
):
    half_ks = out_basis.shape[1]
    local_rows = query_out.shape[1] // lax.axis_size("blk")
    out_part = lax.dot_general(
        query_out, out_basis, (((0,), (0,)), ((), ())), preferred_element_type=jnp.float32
    )
    act_part = lax.dot_general(
        query_act, act_basis, (((0,), (0,)), ((), ())), preferred_element_type=jnp.float32
    )
    rotated = lax.psum_scatter(
        jnp.concatenate([out_part, act_part], axis=1), "blk", scatter_dimension=0, tiled=True
    )
    out_coords = rotated[:, :half_ks]
    act_half = rotated[:, half_ks:]
    act_coords = lax.all_gather(act_half, "fsdp", axis=1, tiled=True)
    queries = local_rows // RQ
    out_three = out_coords.reshape(queries, RQ, half_ks)
    act_three = act_coords.reshape(queries, RQ, act_coords.shape[1])
    numer = jnp.einsum("qri,qrj->qij", out_three, act_three, precision=lax.Precision.HIGHEST)
    precond = (numer / (eigenvalues + damping)).astype(jnp.bfloat16)
    train_total = train_out.shape[0] * lax.axis_size("blk") * lax.axis_size("fsdp")
    empty = jnp.zeros((queries, train_total), jnp.float32)
    full_precond = lax.all_gather(precond, "fsdp", axis=1, tiled=True)
    out_rows = lax.all_gather(train_out, "blk", axis=0, tiled=True)
    act_rows = lax.all_gather(train_act, "blk", axis=0, tiled=True)
    token_counts = lax.all_gather(train_tokens, "blk", axis=0, tiled=True)
    column_ids = lax.all_gather(train_ids, "blk", axis=0, tiled=True)
    scores = empty.at[:, column_ids].add(
        score_block(full_precond, out_rows, act_rows, token_counts)
    )
    return lax.psum(scores, "fsdp")


def solution(mesh):
    parts = mesh.shape["blk"]
    few = parts == DIRECT_PARTS and mesh.shape["fsdp"] == 2
    return jax.shard_map(
        direct if few else gathered,
        mesh=mesh,
        in_specs=(
            P("blk", None),
            P("blk", None),
            P("blk", "fsdp"),
            P("blk", "fsdp"),
            P("fsdp", None),
            P(("groups", "blk", "fsdp"), None, None),
            P(("groups", "blk", "fsdp"), None, None),
            P(("groups", "blk", "fsdp")),
            P(("groups", "blk", "fsdp")),
        ),
        out_specs=P("blk", "groups"),
        check_vma=False,
    )
```

```python
import functools

import jax
import jax.numpy as jnp
from jax import lax
from jax.experimental import pallas as pl
from jax.experimental.pallas import tpu as pltpu
from jax.sharding import PartitionSpec as P

RQ = 4
LANES = 128
DIRECT_PARTS = 8


damping = 0.1


def chunk_count(rows):
    for chunks in (4, 2):
        if rows % (chunks * LANES) == 0:
            return chunks
    return 1


def pinned(x):
    return pltpu.with_memory_space_constraint(x, pltpu.HBM)


def grant(mebibytes):
    return pltpu.CompilerParams(vmem_limit_bytes=mebibytes * 2**20)


def spec(space):
    return pl.BlockSpec(memory_space=space)


def pack_kernel(train_out, train_act, packed, sems):
    ks = train_out.shape[2]
    copies = (
        pltpu.make_async_copy(train_out, packed.at[:, :, :ks], sems.at[0]),
        pltpu.make_async_copy(train_act, packed.at[:, :, ks:], sems.at[1]),
    )
    for copy in copies:
        copy.start()
    for copy in copies:
        copy.wait()


def pack(train_out, train_act):
    examples, rows, ks = train_out.shape
    shape = (examples, rows, ks + train_act.shape[2])
    return pl.pallas_call(
        pack_kernel,
        out_shape=jax.ShapeDtypeStruct(shape, train_out.dtype),
        in_specs=[spec(pltpu.HBM)] * 2,
        out_specs=spec(pltpu.VMEM),
        scratch_shapes=[pltpu.SemaphoreType.DMA((2,))],
        compiler_params=grant(2),
    )(pinned(train_out), pinned(train_act))


def join_kernel(after, first, second, joined):
    del after
    count = first.shape[0]
    joined[:count] = first[...]
    joined[count:] = second[...]


def joined_shape(first, second):
    return jax.ShapeDtypeStruct(
        (first.shape[0] + second.shape[0],) + first.shape[1:], first.dtype
    )


def join(after, first, second):
    return pl.pallas_call(
        join_kernel,
        out_shape=joined_shape(first, second),
        in_specs=[spec(pl.ANY)] + [spec(pltpu.VMEM)] * 2,
        out_specs=spec(pltpu.VMEM),
        compiler_params=grant(4),
    )(after, first, second)


def project_kernel(
    chunks, query_out, query_act, out_basis, act_basis, total, q_out, q_act, b_out, b_act, sems
):
    rows = query_out.shape[1] // chunks
    copies = []
    for c in range(chunks):
        cut = pl.ds(c * rows, rows)
        copies.append(
            (
                pltpu.make_async_copy(query_out.at[:, cut], q_out.at[:, cut], sems.at[2 * c]),
                pltpu.make_async_copy(out_basis.at[cut, :], b_out.at[cut, :], sems.at[2 * c + 1]),
            )
        )
    copies.append(
        (
            pltpu.make_async_copy(query_act, q_act, sems.at[2 * chunks]),
            pltpu.make_async_copy(act_basis, b_act, sems.at[2 * chunks + 1]),
        )
    )
    for pair in copies:
        for copy in pair:
            copy.start()
    half_ks = b_out.shape[1]
    out_part = None
    for c in range(chunks):
        for copy in copies[c]:
            copy.wait()
        cut = pl.ds(c * rows, rows)
        term = jnp.dot(q_out[:, cut], b_out[cut, :], preferred_element_type=jnp.float32)
        out_part = term if out_part is None else out_part + term
    total[:, :half_ks] = out_part
    for copy in copies[chunks]:
        copy.wait()
    total[:, half_ks:] = jnp.dot(q_act[...], b_act[...], preferred_element_type=jnp.float32)


def project(query_out, query_act, out_basis, act_basis):
    columns = query_out.shape[0]
    width = out_basis.shape[1] + act_basis.shape[1]
    chunks = chunk_count(query_out.shape[1])
    operands = (query_out, query_act, out_basis, act_basis)
    return pl.pallas_call(
        functools.partial(project_kernel, chunks),
        out_shape=jax.ShapeDtypeStruct((columns, width), jnp.float32),
        in_specs=[spec(pltpu.HBM)] * len(operands),
        out_specs=spec(pltpu.VMEM),
        scratch_shapes=[pltpu.VMEM(x.shape, x.dtype) for x in operands]
        + [pltpu.SemaphoreType.DMA((2 * chunks + 2,))],
        compiler_params=grant(8),
        cost_estimate=pl.CostEstimate(
            flops=2 * columns * (out_basis.size + act_basis.size),
            bytes_accessed=2 * sum(x.size for x in operands),
            transcendentals=0,
        ),
    )(*[pinned(x) for x in operands])


def doubling_slot(distance, parts):
    bits = parts.bit_length() - 1
    return sum(1 << (bits - 1 - i) for i in range(bits) if distance >> i & 1)


def spread_kernel(
    place_ref, tokens_ref, ids_ref, after, total, first, second, kept, moved, joined
):
    del after
    parts = 2 * kept.shape[0]
    local_rows = kept.shape[1]
    width = total.shape[1]
    row = lax.broadcasted_iota(jnp.int32, (local_rows, LANES), 0)
    lane = lax.broadcasted_iota(jnp.int32, (local_rows, LANES), 1)
    facts = jnp.where(lane < LANES // 2, ids_ref[0], tokens_ref[0]).astype(jnp.float32)
    for part in range(parts):
        start = pl.multiple_of((place_ref[0] ^ part) * local_rows, local_rows)
        piece = (moved if part % 2 else kept).at[part // 2]
        piece[:, :width] = total[pl.ds(start, local_rows), :]
        piece[:, width:] = jnp.where(row == doubling_slot(part, parts), facts, 0.0)
    join_kernel(None, first, second, joined)


def spread(place, tokens, ids, after, total, first, second, parts):
    half = jax.ShapeDtypeStruct(
        (parts // 2, total.shape[0] // parts, total.shape[1] + LANES), jnp.float32
    )
    return pl.pallas_call(
        spread_kernel,
        out_shape=[half, half, joined_shape(first, second)],
        in_specs=[spec(pltpu.SMEM)] * 3 + [spec(pl.ANY)] + [spec(pltpu.VMEM)] * 3,
        out_specs=[spec(pltpu.VMEM)] * 3,
        compiler_params=grant(4),
    )(place, tokens, ids, after, total, first, second)


def split_three(x):
    high = x.astype(jnp.bfloat16)
    rest = x - high.astype(jnp.float32)
    middle = rest.astype(jnp.bfloat16)
    low = (rest - middle.astype(jnp.float32)).astype(jnp.bfloat16)
    return high, middle, low


def score_kernel(core_ref, own, other, eigen, other_eigen, *rest):
    out = rest[-1]
    pairs = (rest[: len(rest) // 2], rest[len(rest) // 2 : -1])
    first = core_ref[0] == 0
    half, ka = eigen.shape
    examples = sum(x.shape[0] for x in pairs[0])
    _, factor_rows, width = pairs[0][0].shape
    ks = width - ka
    coords = (
        jnp.where(first, own[...], other[...]),
        jnp.where(first, other[...], own[...]),
    )
    eigens = (
        jnp.where(first, eigen[...], other_eigen[...]),
        jnp.where(first, other_eigen[...], eigen[...]),
    )
    scales = [1.0 / (e + damping) for e in eigens]
    act = jnp.concatenate([v[:, half : half + ka // 2] for v in coords], axis=1)
    act_terms = split_three(act)
    out_terms = [split_three(v[:, :half]) for v in coords]
    order = ((0, 0), (0, 1), (1, 0), (1, 1), (0, 2), (2, 0))
    weights, hot, flat = [], [], []
    lane = lax.broadcasted_iota(jnp.int32, (examples, LANES), 1).astype(jnp.float32)
    row = lax.broadcasted_iota(jnp.int32, (examples, factor_rows, ka), 1).astype(jnp.float32)
    for facts, blocks in zip((own, other), pairs):
        rows = jnp.concatenate([x[...] for x in blocks], axis=0)
        facts = facts[:, facts.shape[1] - LANES :]
        hot.append(lane == facts[:, :1])
        keep = row < facts[:, LANES // 2 : LANES // 2 + 1][:, :, None]
        weights.append(jnp.where(keep, rows[:, :, ks:].astype(jnp.float32), 0.0))
        flat.append(rows[:, :, :ks].reshape(examples * factor_rows, ks))
    for q in range(out.shape[0]):
        cut = slice(q * RQ, (q + 1) * RQ)
        right = jnp.concatenate([act_terms[b][cut] for _, b in order], axis=0)
        precond = []
        for part in range(2):
            left = jnp.concatenate([out_terms[part][a][cut] for a, _ in order], axis=0)
            numer = lax.dot_general(
                left, right, (((0,), (0,)), ((), ())), preferred_element_type=jnp.float32
            )
            precond.append((numer * scales[part]).astype(jnp.bfloat16))
        precond = jnp.concatenate(precond, axis=0)
        scores = 0.0
        for side in range(2):
            projected = jnp.dot(flat[side], precond, preferred_element_type=jnp.float32)
            terms = projected.reshape(examples, factor_rows, ka) * weights[side]
            per_example = jnp.sum(jnp.sum(terms, axis=1), axis=1, keepdims=True)
            scores += jnp.sum(jnp.where(hot[side], per_example, 0.0), axis=0, keepdims=True)
        out[q : q + 1, :] = scores[:, : out.shape[1]]


def score(core, own, other, eigen, other_eigen, blocks, other_blocks):
    examples = sum(x.shape[0] for x in blocks + other_blocks)
    return pl.pallas_call(
        score_kernel,
        out_shape=jax.ShapeDtypeStruct((own.shape[0] // RQ, examples), jnp.float32),
        in_specs=[spec(pltpu.SMEM)] + [spec(pltpu.VMEM)] * (4 + len(blocks + other_blocks)),
        out_specs=spec(pltpu.VMEM),
        compiler_params=grant(12),
    )(core, own, other, eigen, other_eigen, *blocks, *other_blocks)


def direct(
    query_out,
    query_act,
    out_basis,
    act_basis,
    eigenvalues,
    train_out,
    train_act,
    train_tokens,
    train_ids,
):
    parts = lax.axis_size("blk")
    steps = parts.bit_length() - 1
    swap = [(0, 1), (1, 0)]

    def across(x, i):
        return lax.ppermute(x, "blk", [(s, s ^ (1 << i)) for s in range(parts)])

    place = lax.axis_index("blk").reshape(1)
    core = lax.axis_index("fsdp").reshape(1)
    other_eigen = lax.ppermute(eigenvalues, "fsdp", swap)
    block = pack(train_out, train_act)
    arrived = across(block, steps - 1)
    total = project(query_out.T, query_act.T, out_basis, act_basis)
    kept, moved, block = spread(
        place, train_tokens, train_ids, other_eigen, total, block, arrived, parts
    )
    sums = (kept + across(moved, 0)).reshape((2, 2) + kept.shape[1:])
    arrived = across(block, 1)
    kept, moved = sums[:, 0], sums[:, 1]
    near = join(kept, block, arrived)
    far = across(near, 0)
    other_near = lax.ppermute(near, "fsdp", swap)
    other_far = lax.ppermute(far, "fsdp", swap)
    sums = kept + across(moved, 1)
    own = sums[0] + across(sums[1], 2)
    other = lax.ppermute(own, "fsdp", swap)
    return score(
        core, own, other, eigenvalues, other_eigen, (near, far), (other_near, other_far)
    )


def score_block(precond, out_rows, act_rows, token_counts):
    factor_rows = out_rows.shape[1]
    valid = (
        lax.broadcasted_iota(jnp.int32, (out_rows.shape[0], factor_rows), 1) < token_counts[:, None]
    ).astype(jnp.float32)
    projected = jnp.einsum("nri,qij->nrqj", out_rows, precond, preferred_element_type=jnp.float32)
    weights = act_rows.astype(jnp.float32) * valid[:, :, None]
    return jnp.einsum("nrqj,nrj->qn", projected, weights, precision=lax.Precision.HIGHEST)


def gathered(
    query_out,
    query_act,
    out_basis,
    act_basis,
    eigenvalues,
    train_out,
    train_act,
    train_tokens,
    train_ids,
):
    half_ks = out_basis.shape[1]
    local_rows = query_out.shape[1] // lax.axis_size("blk")
    out_part = lax.dot_general(
        query_out, out_basis, (((0,), (0,)), ((), ())), preferred_element_type=jnp.float32
    )
    act_part = lax.dot_general(
        query_act, act_basis, (((0,), (0,)), ((), ())), preferred_element_type=jnp.float32
    )
    rotated = lax.psum_scatter(
        jnp.concatenate([out_part, act_part], axis=1), "blk", scatter_dimension=0, tiled=True
    )
    out_coords = rotated[:, :half_ks]
    act_half = rotated[:, half_ks:]
    act_coords = lax.all_gather(act_half, "fsdp", axis=1, tiled=True)
    queries = local_rows // RQ
    out_three = out_coords.reshape(queries, RQ, half_ks)
    act_three = act_coords.reshape(queries, RQ, act_coords.shape[1])
    numer = jnp.einsum("qri,qrj->qij", out_three, act_three, precision=lax.Precision.HIGHEST)
    precond = (numer / (eigenvalues + damping)).astype(jnp.bfloat16)
    train_total = train_out.shape[0] * lax.axis_size("blk") * lax.axis_size("fsdp")
    empty = jnp.zeros((queries, train_total), jnp.float32)
    full_precond = lax.all_gather(precond, "fsdp", axis=1, tiled=True)
    out_rows = lax.all_gather(train_out, "blk", axis=0, tiled=True)
    act_rows = lax.all_gather(train_act, "blk", axis=0, tiled=True)
    token_counts = lax.all_gather(train_tokens, "blk", axis=0, tiled=True)
    column_ids = lax.all_gather(train_ids, "blk", axis=0, tiled=True)
    scores = empty.at[:, column_ids].add(
        score_block(full_precond, out_rows, act_rows, token_counts)
    )
    return lax.psum(scores, "fsdp")


def solution(mesh):
    parts = mesh.shape["blk"]
    few = parts == DIRECT_PARTS and mesh.shape["fsdp"] == 2
    return jax.shard_map(
        direct if few else gathered,
        mesh=mesh,
        in_specs=(
            P("blk", None),
            P("blk", None),
            P("blk", "fsdp"),
            P("blk", "fsdp"),
            P("fsdp", None),
            P(("groups", "blk", "fsdp"), None, None),
            P(("groups", "blk", "fsdp"), None, None),
            P(("groups", "blk", "fsdp")),
            P(("groups", "blk", "fsdp")),
        ),
        out_specs=P("blk", "groups"),
        check_vma=False,
    )
```

```python
import functools

import jax
import jax.numpy as jnp
from jax import lax
from jax.experimental import pallas as pl
from jax.experimental.pallas import tpu as pltpu
from jax.sharding import PartitionSpec as P

RQ = 4
LANES = 128
DIRECT_PARTS = 8


damping = 0.1


def chunk_count(rows):
    for chunks in (4, 2):
        if rows % (chunks * LANES) == 0:
            return chunks
    return 1


def pinned(x):
    return pltpu.with_memory_space_constraint(x, pltpu.HBM)


def grant(mebibytes):
    return pltpu.CompilerParams(vmem_limit_bytes=mebibytes * 2**20)


def spec(space):
    return pl.BlockSpec(memory_space=space)


def pack_kernel(train_out, train_act, packed, sems):
    ks = train_out.shape[2]
    copies = (
        pltpu.make_async_copy(train_out, packed.at[:, :, :ks], sems.at[0]),
        pltpu.make_async_copy(train_act, packed.at[:, :, ks:], sems.at[1]),
    )
    for copy in copies:
        copy.start()
    for copy in copies:
        copy.wait()


def pack(train_out, train_act):
    examples, rows, ks = train_out.shape
    shape = (examples, rows, ks + train_act.shape[2])
    return pl.pallas_call(
        pack_kernel,
        out_shape=jax.ShapeDtypeStruct(shape, train_out.dtype),
        in_specs=[spec(pltpu.HBM)] * 2,
        out_specs=spec(pltpu.VMEM),
        scratch_shapes=[pltpu.SemaphoreType.DMA((2,))],
        compiler_params=grant(2),
    )(pinned(train_out), pinned(train_act))


def join_kernel(after, first, second, joined):
    del after
    count = first.shape[0]
    joined[:count] = first[...]
    joined[count:] = second[...]


def joined_shape(first, second):
    return jax.ShapeDtypeStruct(
        (first.shape[0] + second.shape[0],) + first.shape[1:], first.dtype
    )


def join(after, first, second):
    return pl.pallas_call(
        join_kernel,
        out_shape=joined_shape(first, second),
        in_specs=[spec(pl.ANY)] + [spec(pltpu.VMEM)] * 2,
        out_specs=spec(pltpu.VMEM),
        compiler_params=grant(4),
    )(after, first, second)


def project_kernel(
    chunks, query_out, query_act, out_basis, act_basis, total, q_out, q_act, b_out, b_act, sems
):
    rows = query_out.shape[1] // chunks
    copies = []
    for c in range(chunks):
        cut = pl.ds(c * rows, rows)
        copies.append(
            (
                pltpu.make_async_copy(query_out.at[:, cut], q_out.at[:, cut], sems.at[2 * c]),
                pltpu.make_async_copy(out_basis.at[cut, :], b_out.at[cut, :], sems.at[2 * c + 1]),
            )
        )
    copies.append(
        (
            pltpu.make_async_copy(query_act, q_act, sems.at[2 * chunks]),
            pltpu.make_async_copy(act_basis, b_act, sems.at[2 * chunks + 1]),
        )
    )
    for pair in copies:
        for copy in pair:
            copy.start()
    half_ks = b_out.shape[1]
    out_part = None
    for c in range(chunks):
        for copy in copies[c]:
            copy.wait()
        cut = pl.ds(c * rows, rows)
        term = jnp.dot(q_out[:, cut], b_out[cut, :], preferred_element_type=jnp.float32)
        out_part = term if out_part is None else out_part + term
    total[:, :half_ks] = out_part
    for copy in copies[chunks]:
        copy.wait()
    total[:, half_ks:] = jnp.dot(q_act[...], b_act[...], preferred_element_type=jnp.float32)


def project(query_out, query_act, out_basis, act_basis):
    columns = query_out.shape[0]
    width = out_basis.shape[1] + act_basis.shape[1]
    chunks = chunk_count(query_out.shape[1])
    operands = (query_out, query_act, out_basis, act_basis)
    return pl.pallas_call(
        functools.partial(project_kernel, chunks),
        out_shape=jax.ShapeDtypeStruct((columns, width), jnp.float32),
        in_specs=[spec(pltpu.HBM)] * len(operands),
        out_specs=spec(pltpu.VMEM),
        scratch_shapes=[pltpu.VMEM(x.shape, x.dtype) for x in operands]
        + [pltpu.SemaphoreType.DMA((2 * chunks + 2,))],
        compiler_params=grant(8),
        cost_estimate=pl.CostEstimate(
            flops=2 * columns * (out_basis.size + act_basis.size),
            bytes_accessed=2 * sum(x.size for x in operands),
            transcendentals=0,
        ),
    )(*[pinned(x) for x in operands])


def doubling_slot(distance, parts):
    bits = parts.bit_length() - 1
    return sum(1 << (bits - 1 - i) for i in range(bits) if distance >> i & 1)


def spread_kernel(
    place_ref, tokens_ref, ids_ref, total, first, second, kept, moved, joined
):
    parts = 2 * kept.shape[0]
    local_rows = kept.shape[1]
    width = total.shape[1]
    row = lax.broadcasted_iota(jnp.int32, (local_rows, LANES), 0)
    lane = lax.broadcasted_iota(jnp.int32, (local_rows, LANES), 1)
    facts = jnp.where(lane < LANES // 2, ids_ref[0], tokens_ref[0]).astype(jnp.float32)
    for part in range(parts):
        start = pl.multiple_of((place_ref[0] ^ part) * local_rows, local_rows)
        piece = (moved if part % 2 else kept).at[part // 2]
        piece[:, :width] = total[pl.ds(start, local_rows), :]
        piece[:, width:] = jnp.where(row == doubling_slot(part, parts), facts, 0.0)
    join_kernel(None, first, second, joined)


def spread(place, tokens, ids, total, first, second, parts):
    half = jax.ShapeDtypeStruct(
        (parts // 2, total.shape[0] // parts, total.shape[1] + LANES), jnp.float32
    )
    return pl.pallas_call(
        spread_kernel,
        out_shape=[half, half, joined_shape(first, second)],
        in_specs=[spec(pltpu.SMEM)] * 3 + [spec(pltpu.VMEM)] * 3,
        out_specs=[spec(pltpu.VMEM)] * 3,
        compiler_params=grant(4),
    )(place, tokens, ids, total, first, second)


def split_three(x):
    high = x.astype(jnp.bfloat16)
    rest = x - high.astype(jnp.float32)
    middle = rest.astype(jnp.bfloat16)
    low = (rest - middle.astype(jnp.float32)).astype(jnp.bfloat16)
    return high, middle, low


def score_kernel(core_ref, own, other, eigen, other_eigen, *rest):
    out = rest[-1]
    pairs = (rest[: len(rest) // 2], rest[len(rest) // 2 : -1])
    first = core_ref[0] == 0
    half, ka = eigen.shape
    examples = sum(x.shape[0] for x in pairs[0])
    _, factor_rows, width = pairs[0][0].shape
    ks = width - ka
    coords = (
        jnp.where(first, own[...], other[...]),
        jnp.where(first, other[...], own[...]),
    )
    eigens = (
        jnp.where(first, eigen[...], other_eigen[...]),
        jnp.where(first, other_eigen[...], eigen[...]),
    )
    scales = [1.0 / (e + damping) for e in eigens]
    act = jnp.concatenate([v[:, half : half + ka // 2] for v in coords], axis=1)
    act_terms = split_three(act)
    out_terms = [split_three(v[:, :half]) for v in coords]
    order = ((0, 0), (0, 1), (1, 0), (1, 1), (0, 2), (2, 0))
    weights, hot, flat = [], [], []
    lane = lax.broadcasted_iota(jnp.int32, (examples, LANES), 1).astype(jnp.float32)
    row = lax.broadcasted_iota(jnp.int32, (examples, factor_rows, ka), 1).astype(jnp.float32)
    for facts, blocks in zip((own, other), pairs):
        rows = jnp.concatenate([x[...] for x in blocks], axis=0)
        facts = facts[:, facts.shape[1] - LANES :]
        hot.append(lane == facts[:, :1])
        keep = row < facts[:, LANES // 2 : LANES // 2 + 1][:, :, None]
        weights.append(jnp.where(keep, rows[:, :, ks:].astype(jnp.float32), 0.0))
        flat.append(rows[:, :, :ks].reshape(examples * factor_rows, ks))
    for q in range(out.shape[0]):
        cut = slice(q * RQ, (q + 1) * RQ)
        right = jnp.concatenate([act_terms[b][cut] for _, b in order], axis=0)
        precond = []
        for part in range(2):
            left = jnp.concatenate([out_terms[part][a][cut] for a, _ in order], axis=0)
            numer = lax.dot_general(
                left, right, (((0,), (0,)), ((), ())), preferred_element_type=jnp.float32
            )
            precond.append((numer * scales[part]).astype(jnp.bfloat16))
        precond = jnp.concatenate(precond, axis=0)
        scores = 0.0
        for side in range(2):
            projected = jnp.dot(flat[side], precond, preferred_element_type=jnp.float32)
            terms = projected.reshape(examples, factor_rows, ka) * weights[side]
            per_example = jnp.sum(jnp.sum(terms, axis=1), axis=1, keepdims=True)
            scores += jnp.sum(jnp.where(hot[side], per_example, 0.0), axis=0, keepdims=True)
        out[q : q + 1, :] = scores[:, : out.shape[1]]


def score(core, own, other, eigen, other_eigen, blocks, other_blocks):
    examples = sum(x.shape[0] for x in blocks + other_blocks)
    return pl.pallas_call(
        score_kernel,
        out_shape=jax.ShapeDtypeStruct((own.shape[0] // RQ, examples), jnp.float32),
        in_specs=[spec(pltpu.SMEM)] + [spec(pltpu.VMEM)] * (4 + len(blocks + other_blocks)),
        out_specs=spec(pltpu.VMEM),
        compiler_params=grant(12),
    )(core, own, other, eigen, other_eigen, *blocks, *other_blocks)


def direct(
    query_out,
    query_act,
    out_basis,
    act_basis,
    eigenvalues,
    train_out,
    train_act,
    train_tokens,
    train_ids,
):
    parts = lax.axis_size("blk")
    steps = parts.bit_length() - 1
    swap = [(0, 1), (1, 0)]

    def across(x, i):
        return lax.ppermute(x, "blk", [(s, s ^ (1 << i)) for s in range(parts)])

    place = lax.axis_index("blk").reshape(1)
    core = lax.axis_index("fsdp").reshape(1)
    other_eigen = lax.ppermute(eigenvalues, "fsdp", swap)
    block = pack(train_out, train_act)
    arrived = across(block, steps - 1)
    total = project(query_out.T, query_act.T, out_basis, act_basis)
    kept, moved, block = spread(
        place, train_tokens, train_ids, total, block, arrived, parts
    )
    sums = (kept + across(moved, 0)).reshape((2, 2) + kept.shape[1:])
    arrived = across(block, 1)
    kept, moved = sums[:, 0], sums[:, 1]
    near = join(kept, block, arrived)
    far = across(near, 0)
    other_near = lax.ppermute(near, "fsdp", swap)
    other_far = lax.ppermute(far, "fsdp", swap)
    sums = kept + across(moved, 1)
    own = sums[0] + across(sums[1], 2)
    other = lax.ppermute(own, "fsdp", swap)
    return score(
        core, own, other, eigenvalues, other_eigen, (near, far), (other_near, other_far)
    )


def score_block(precond, out_rows, act_rows, token_counts):
    factor_rows = out_rows.shape[1]
    valid = (
        lax.broadcasted_iota(jnp.int32, (out_rows.shape[0], factor_rows), 1) < token_counts[:, None]
    ).astype(jnp.float32)
    projected = jnp.einsum("nri,qij->nrqj", out_rows, precond, preferred_element_type=jnp.float32)
    weights = act_rows.astype(jnp.float32) * valid[:, :, None]
    return jnp.einsum("nrqj,nrj->qn", projected, weights, precision=lax.Precision.HIGHEST)


def gathered(
    query_out,
    query_act,
    out_basis,
    act_basis,
    eigenvalues,
    train_out,
    train_act,
    train_tokens,
    train_ids,
):
    half_ks = out_basis.shape[1]
    local_rows = query_out.shape[1] // lax.axis_size("blk")
    out_part = lax.dot_general(
        query_out, out_basis, (((0,), (0,)), ((), ())), preferred_element_type=jnp.float32
    )
    act_part = lax.dot_general(
        query_act, act_basis, (((0,), (0,)), ((), ())), preferred_element_type=jnp.float32
    )
    rotated = lax.psum_scatter(
        jnp.concatenate([out_part, act_part], axis=1), "blk", scatter_dimension=0, tiled=True
    )
    out_coords = rotated[:, :half_ks]
    act_half = rotated[:, half_ks:]
    act_coords = lax.all_gather(act_half, "fsdp", axis=1, tiled=True)
    queries = local_rows // RQ
    out_three = out_coords.reshape(queries, RQ, half_ks)
    act_three = act_coords.reshape(queries, RQ, act_coords.shape[1])
    numer = jnp.einsum("qri,qrj->qij", out_three, act_three, precision=lax.Precision.HIGHEST)
    precond = (numer / (eigenvalues + damping)).astype(jnp.bfloat16)
    train_total = train_out.shape[0] * lax.axis_size("blk") * lax.axis_size("fsdp")
    empty = jnp.zeros((queries, train_total), jnp.float32)
    full_precond = lax.all_gather(precond, "fsdp", axis=1, tiled=True)
    out_rows = lax.all_gather(train_out, "blk", axis=0, tiled=True)
    act_rows = lax.all_gather(train_act, "blk", axis=0, tiled=True)
    token_counts = lax.all_gather(train_tokens, "blk", axis=0, tiled=True)
    column_ids = lax.all_gather(train_ids, "blk", axis=0, tiled=True)
    scores = empty.at[:, column_ids].add(
        score_block(full_precond, out_rows, act_rows, token_counts)
    )
    return lax.psum(scores, "fsdp")


def solution(mesh):
    parts = mesh.shape["blk"]
    few = parts == DIRECT_PARTS and mesh.shape["fsdp"] == 2
    return jax.shard_map(
        direct if few else gathered,
        mesh=mesh,
        in_specs=(
            P("blk", None),
            P("blk", None),
            P("blk", "fsdp"),
            P("blk", "fsdp"),
            P("fsdp", None),
            P(("groups", "blk", "fsdp"), None, None),
            P(("groups", "blk", "fsdp"), None, None),
            P(("groups", "blk", "fsdp")),
            P(("groups", "blk", "fsdp")),
        ),
        out_specs=P("blk", "groups"),
        check_vma=False,
    )
```

```python
import functools

import jax
import jax.numpy as jnp
from jax import lax
from jax.experimental import pallas as pl
from jax.experimental.pallas import tpu as pltpu
from jax.sharding import PartitionSpec as P

RQ = 4
LANES = 128
DIRECT_PARTS = 8
WAIT_FLOPS = 10**9


damping = 0.1


def pinned(x):
    return pltpu.with_memory_space_constraint(x, pltpu.HBM)


def grant(mebibytes):
    return pltpu.CompilerParams(vmem_limit_bytes=mebibytes * 2**20)


def spec(space):
    return pl.BlockSpec(memory_space=space)


def pack_kernel(train_out, train_act, packed, sems):
    ks = train_out.shape[2]
    copies = (
        pltpu.make_async_copy(train_out, packed.at[:, :, :ks], sems.at[0]),
        pltpu.make_async_copy(train_act, packed.at[:, :, ks:], sems.at[1]),
    )
    for copy in copies:
        copy.start()
    for copy in copies:
        copy.wait()


def pack(train_out, train_act):
    examples, rows, ks = train_out.shape
    shape = (examples, rows, ks + train_act.shape[2])
    return pl.pallas_call(
        pack_kernel,
        out_shape=jax.ShapeDtypeStruct(shape, train_out.dtype),
        in_specs=[spec(pltpu.HBM)] * 2,
        out_specs=spec(pltpu.VMEM),
        scratch_shapes=[pltpu.SemaphoreType.DMA((2,))],
        compiler_params=grant(2),
        cost_estimate=pl.CostEstimate(flops=WAIT_FLOPS, bytes_accessed=0, transcendentals=0),
    )(pinned(train_out), pinned(train_act))


def join_kernel(after, first, second, joined):
    del after
    count = first.shape[0]
    joined[:count] = first[...]
    joined[count:] = second[...]


def joined_shape(first, second):
    return jax.ShapeDtypeStruct(
        (first.shape[0] + second.shape[0],) + first.shape[1:], first.dtype
    )


def join(after, first, second):
    return pl.pallas_call(
        join_kernel,
        out_shape=joined_shape(first, second),
        in_specs=[spec(pl.ANY)] + [spec(pltpu.VMEM)] * 2,
        out_specs=spec(pltpu.VMEM),
        compiler_params=grant(4),
    )(after, first, second)


def project_kernel(query_out, query_act, out_basis, act_basis, total):
    half_ks = out_basis.shape[1]
    total[:, :half_ks] = jnp.dot(
        query_out[...], out_basis[...], preferred_element_type=jnp.float32
    )
    total[:, half_ks:] = jnp.dot(
        query_act[...], act_basis[...], preferred_element_type=jnp.float32
    )


def project(query_out, query_act, out_basis, act_basis):
    columns = query_out.shape[0]
    width = out_basis.shape[1] + act_basis.shape[1]
    operands = (query_out, query_act, out_basis, act_basis)
    return pl.pallas_call(
        project_kernel,
        out_shape=jax.ShapeDtypeStruct((columns, width), jnp.float32),
        in_specs=[spec(pltpu.VMEM)] * len(operands),
        out_specs=spec(pltpu.VMEM),
        compiler_params=grant(8),
        cost_estimate=pl.CostEstimate(
            flops=2 * columns * (out_basis.size + act_basis.size),
            bytes_accessed=2 * sum(x.size for x in operands),
            transcendentals=0,
        ),
    )(*operands)


def doubling_slot(distance, parts):
    bits = parts.bit_length() - 1
    return sum(1 << (bits - 1 - i) for i in range(bits) if distance >> i & 1)


def spread_kernel(
    place_ref, tokens_ref, ids_ref, after, total, first, second, kept, moved, joined
):
    del after
    parts = 2 * kept.shape[0]
    local_rows = kept.shape[1]
    width = total.shape[1]
    row = lax.broadcasted_iota(jnp.int32, (local_rows, LANES), 0)
    lane = lax.broadcasted_iota(jnp.int32, (local_rows, LANES), 1)
    facts = jnp.where(lane < LANES // 2, ids_ref[0], tokens_ref[0]).astype(jnp.float32)
    for part in range(parts):
        start = pl.multiple_of((place_ref[0] ^ part) * local_rows, local_rows)
        piece = (moved if part % 2 else kept).at[part // 2]
        piece[:, :width] = total[pl.ds(start, local_rows), :]
        piece[:, width:] = jnp.where(row == doubling_slot(part, parts), facts, 0.0)
    join_kernel(None, first, second, joined)


def spread(place, tokens, ids, after, total, first, second, parts):
    half = jax.ShapeDtypeStruct(
        (parts // 2, total.shape[0] // parts, total.shape[1] + LANES), jnp.float32
    )
    return pl.pallas_call(
        spread_kernel,
        out_shape=[half, half, joined_shape(first, second)],
        in_specs=[spec(pltpu.SMEM)] * 3 + [spec(pl.ANY)] + [spec(pltpu.VMEM)] * 3,
        out_specs=[spec(pltpu.VMEM)] * 3,
        compiler_params=grant(4),
    )(place, tokens, ids, after, total, first, second)


def split_three(x):
    high = x.astype(jnp.bfloat16)
    rest = x - high.astype(jnp.float32)
    middle = rest.astype(jnp.bfloat16)
    low = (rest - middle.astype(jnp.float32)).astype(jnp.bfloat16)
    return high, middle, low


def score_kernel(core_ref, own, other, eigen, other_eigen, *rest):
    out = rest[-1]
    pairs = (rest[: len(rest) // 2], rest[len(rest) // 2 : -1])
    first = core_ref[0] == 0
    half, ka = eigen.shape
    examples = sum(x.shape[0] for x in pairs[0])
    _, factor_rows, width = pairs[0][0].shape
    ks = width - ka
    coords = (
        jnp.where(first, own[...], other[...]),
        jnp.where(first, other[...], own[...]),
    )
    eigens = (
        jnp.where(first, eigen[...], other_eigen[...]),
        jnp.where(first, other_eigen[...], eigen[...]),
    )
    scales = [1.0 / (e + damping) for e in eigens]
    act = jnp.concatenate([v[:, half : half + ka // 2] for v in coords], axis=1)
    act_terms = split_three(act)
    out_terms = [split_three(v[:, :half]) for v in coords]
    order = ((0, 0), (0, 1), (1, 0), (1, 1), (0, 2), (2, 0))
    weights, hot, flat = [], [], []
    lane = lax.broadcasted_iota(jnp.int32, (examples, LANES), 1).astype(jnp.float32)
    row = lax.broadcasted_iota(jnp.int32, (examples, factor_rows, ka), 1).astype(jnp.float32)
    for facts, blocks in zip((own, other), pairs):
        rows = jnp.concatenate([x[...] for x in blocks], axis=0)
        facts = facts[:, facts.shape[1] - LANES :]
        hot.append(lane == facts[:, :1])
        keep = row < facts[:, LANES // 2 : LANES // 2 + 1][:, :, None]
        weights.append(jnp.where(keep, rows[:, :, ks:].astype(jnp.float32), 0.0))
        flat.append(rows[:, :, :ks].reshape(examples * factor_rows, ks))
    for q in range(out.shape[0]):
        cut = slice(q * RQ, (q + 1) * RQ)
        right = jnp.concatenate([act_terms[b][cut] for _, b in order], axis=0)
        precond = []
        for part in range(2):
            left = jnp.concatenate([out_terms[part][a][cut] for a, _ in order], axis=0)
            numer = lax.dot_general(
                left, right, (((0,), (0,)), ((), ())), preferred_element_type=jnp.float32
            )
            precond.append((numer * scales[part]).astype(jnp.bfloat16))
        precond = jnp.concatenate(precond, axis=0)
        scores = 0.0
        for side in range(2):
            projected = jnp.dot(flat[side], precond, preferred_element_type=jnp.float32)
            terms = projected.reshape(examples, factor_rows, ka) * weights[side]
            per_example = jnp.sum(jnp.sum(terms, axis=1), axis=1, keepdims=True)
            scores += jnp.sum(jnp.where(hot[side], per_example, 0.0), axis=0, keepdims=True)
        out[q : q + 1, :] = scores[:, : out.shape[1]]


def score(core, own, other, eigen, other_eigen, blocks, other_blocks):
    examples = sum(x.shape[0] for x in blocks + other_blocks)
    return pl.pallas_call(
        score_kernel,
        out_shape=jax.ShapeDtypeStruct((own.shape[0] // RQ, examples), jnp.float32),
        in_specs=[spec(pltpu.SMEM)] + [spec(pltpu.VMEM)] * (4 + len(blocks + other_blocks)),
        out_specs=spec(pltpu.VMEM),
        compiler_params=grant(12),
    )(core, own, other, eigen, other_eigen, *blocks, *other_blocks)


def direct(
    query_out,
    query_act,
    out_basis,
    act_basis,
    eigenvalues,
    train_out,
    train_act,
    train_tokens,
    train_ids,
):
    parts = lax.axis_size("blk")
    steps = parts.bit_length() - 1
    swap = [(0, 1), (1, 0)]

    def across(x, i):
        return lax.ppermute(x, "blk", [(s, s ^ (1 << i)) for s in range(parts)])

    place = lax.axis_index("blk").reshape(1)
    core = lax.axis_index("fsdp").reshape(1)
    other_eigen = lax.ppermute(eigenvalues, "fsdp", swap)
    block = pack(train_out, train_act)
    arrived = across(block, steps - 1)
    total = project(query_out.T, query_act.T, out_basis, act_basis)
    kept, moved, block = spread(
        place, train_tokens, train_ids, other_eigen, total, block, arrived, parts
    )
    sums = (kept + across(moved, 0)).reshape((2, 2) + kept.shape[1:])
    arrived = across(block, 1)
    kept, moved = sums[:, 0], sums[:, 1]
    near = join(kept, block, arrived)
    far = across(near, 0)
    other_near = lax.ppermute(near, "fsdp", swap)
    other_far = lax.ppermute(far, "fsdp", swap)
    sums = kept + across(moved, 1)
    own = sums[0] + across(sums[1], 2)
    other = lax.ppermute(own, "fsdp", swap)
    return score(
        core, own, other, eigenvalues, other_eigen, (near, far), (other_near, other_far)
    )


def score_block(precond, out_rows, act_rows, token_counts):
    factor_rows = out_rows.shape[1]
    valid = (
        lax.broadcasted_iota(jnp.int32, (out_rows.shape[0], factor_rows), 1) < token_counts[:, None]
    ).astype(jnp.float32)
    projected = jnp.einsum("nri,qij->nrqj", out_rows, precond, preferred_element_type=jnp.float32)
    weights = act_rows.astype(jnp.float32) * valid[:, :, None]
    return jnp.einsum("nrqj,nrj->qn", projected, weights, precision=lax.Precision.HIGHEST)


def gathered(
    query_out,
    query_act,
    out_basis,
    act_basis,
    eigenvalues,
    train_out,
    train_act,
    train_tokens,
    train_ids,
):
    half_ks = out_basis.shape[1]
    local_rows = query_out.shape[1] // lax.axis_size("blk")
    out_part = lax.dot_general(
        query_out, out_basis, (((0,), (0,)), ((), ())), preferred_element_type=jnp.float32
    )
    act_part = lax.dot_general(
        query_act, act_basis, (((0,), (0,)), ((), ())), preferred_element_type=jnp.float32
    )
    rotated = lax.psum_scatter(
        jnp.concatenate([out_part, act_part], axis=1), "blk", scatter_dimension=0, tiled=True
    )
    out_coords = rotated[:, :half_ks]
    act_half = rotated[:, half_ks:]
    act_coords = lax.all_gather(act_half, "fsdp", axis=1, tiled=True)
    queries = local_rows // RQ
    out_three = out_coords.reshape(queries, RQ, half_ks)
    act_three = act_coords.reshape(queries, RQ, act_coords.shape[1])
    numer = jnp.einsum("qri,qrj->qij", out_three, act_three, precision=lax.Precision.HIGHEST)
    precond = (numer / (eigenvalues + damping)).astype(jnp.bfloat16)
    train_total = train_out.shape[0] * lax.axis_size("blk") * lax.axis_size("fsdp")
    empty = jnp.zeros((queries, train_total), jnp.float32)
    full_precond = lax.all_gather(precond, "fsdp", axis=1, tiled=True)
    out_rows = lax.all_gather(train_out, "blk", axis=0, tiled=True)
    act_rows = lax.all_gather(train_act, "blk", axis=0, tiled=True)
    token_counts = lax.all_gather(train_tokens, "blk", axis=0, tiled=True)
    column_ids = lax.all_gather(train_ids, "blk", axis=0, tiled=True)
    scores = empty.at[:, column_ids].add(
        score_block(full_precond, out_rows, act_rows, token_counts)
    )
    return lax.psum(scores, "fsdp")


def solution(mesh):
    parts = mesh.shape["blk"]
    few = parts == DIRECT_PARTS and mesh.shape["fsdp"] == 2
    return jax.shard_map(
        direct if few else gathered,
        mesh=mesh,
        in_specs=(
            P("blk", None),
            P("blk", None),
            P("blk", "fsdp"),
            P("blk", "fsdp"),
            P("fsdp", None),
            P(("groups", "blk", "fsdp"), None, None),
            P(("groups", "blk", "fsdp"), None, None),
            P(("groups", "blk", "fsdp")),
            P(("groups", "blk", "fsdp")),
        ),
        out_specs=P("blk", "groups"),
        check_vma=False,
    )
```

```python
import functools

import jax
import jax.numpy as jnp
from jax import lax
from jax.experimental import pallas as pl
from jax.experimental.pallas import tpu as pltpu
from jax.sharding import PartitionSpec as P

RQ = 4
LANES = 128
DIRECT_PARTS = 8
WAIT_FLOPS = 10**9


damping = 0.1


def pinned(x):
    return pltpu.with_memory_space_constraint(x, pltpu.HBM)


def grant(mebibytes):
    return pltpu.CompilerParams(vmem_limit_bytes=mebibytes * 2**20)


def spec(space):
    return pl.BlockSpec(memory_space=space)


def pack_kernel(train_out, train_act, packed, sems):
    ks = train_out.shape[2]
    copies = (
        pltpu.make_async_copy(train_out, packed.at[:, :, :ks], sems.at[0]),
        pltpu.make_async_copy(train_act, packed.at[:, :, ks:], sems.at[1]),
    )
    for copy in copies:
        copy.start()
    for copy in copies:
        copy.wait()


def pack(train_out, train_act):
    examples, rows, ks = train_out.shape
    shape = (examples, rows, ks + train_act.shape[2])
    return pl.pallas_call(
        pack_kernel,
        out_shape=jax.ShapeDtypeStruct(shape, train_out.dtype),
        in_specs=[spec(pltpu.HBM)] * 2,
        out_specs=spec(pltpu.VMEM),
        scratch_shapes=[pltpu.SemaphoreType.DMA((2,))],
        compiler_params=grant(2),
        cost_estimate=pl.CostEstimate(flops=WAIT_FLOPS, bytes_accessed=0, transcendentals=0),
    )(pinned(train_out), pinned(train_act))


def join_kernel(after, first, second, joined):
    del after
    count = first.shape[0]
    joined[:count] = first[...]
    joined[count:] = second[...]


def joined_shape(first, second):
    return jax.ShapeDtypeStruct(
        (first.shape[0] + second.shape[0],) + first.shape[1:], first.dtype
    )


def join(after, first, second):
    return pl.pallas_call(
        join_kernel,
        out_shape=joined_shape(first, second),
        in_specs=[spec(pl.ANY)] + [spec(pltpu.VMEM)] * 2,
        out_specs=spec(pltpu.VMEM),
        compiler_params=grant(4),
    )(after, first, second)


def project_kernel(after, query_out, query_act, out_basis, act_basis, total):
    del after
    half_ks = out_basis.shape[1]
    total[:, :half_ks] = jnp.dot(
        query_out[...], out_basis[...], preferred_element_type=jnp.float32
    )
    total[:, half_ks:] = jnp.dot(
        query_act[...], act_basis[...], preferred_element_type=jnp.float32
    )


def project(after, query_out, query_act, out_basis, act_basis):
    columns = query_out.shape[0]
    width = out_basis.shape[1] + act_basis.shape[1]
    operands = (query_out, query_act, out_basis, act_basis)
    return pl.pallas_call(
        project_kernel,
        out_shape=jax.ShapeDtypeStruct((columns, width), jnp.float32),
        in_specs=[spec(pl.ANY)] + [spec(pltpu.VMEM)] * len(operands),
        out_specs=spec(pltpu.VMEM),
        compiler_params=grant(8),
        cost_estimate=pl.CostEstimate(
            flops=2 * columns * (out_basis.size + act_basis.size),
            bytes_accessed=2 * sum(x.size for x in operands),
            transcendentals=0,
        ),
    )(after, *operands)


def doubling_slot(distance, parts):
    bits = parts.bit_length() - 1
    return sum(1 << (bits - 1 - i) for i in range(bits) if distance >> i & 1)


def spread_kernel(place_ref, tokens_ref, ids_ref, after, total, kept, moved):
    del after
    lines, rows, _ = kept.shape
    lines = 2 * lines
    width = total.shape[1]
    line = place_ref[0] // 2
    row = lax.broadcasted_iota(jnp.int32, (rows, LANES), 0)
    lane = lax.broadcasted_iota(jnp.int32, (rows, LANES), 1)
    facts = jnp.where(lane < LANES // 2, ids_ref[0], tokens_ref[0]).astype(jnp.float32)
    for k in range(lines):
        start = pl.multiple_of((line ^ k) * rows, rows)
        piece = (moved if k % 2 else kept).at[k // 2]
        piece[:, :width] = total[pl.ds(start, rows), :]
        piece[:, width:] = jnp.where(row == doubling_slot(k, lines), facts, 0.0)


def spread(place, tokens, ids, after, total, lines):
    half = jax.ShapeDtypeStruct(
        (lines // 2, total.shape[0] // lines, total.shape[1] + LANES), jnp.float32
    )
    return pl.pallas_call(
        spread_kernel,
        out_shape=[half, half],
        in_specs=[spec(pltpu.SMEM)] * 3 + [spec(pl.ANY), spec(pltpu.VMEM)],
        out_specs=[spec(pltpu.VMEM)] * 2,
        compiler_params=grant(4),
    )(place, tokens, ids, after, total)


def split_three(x):
    high = x.astype(jnp.bfloat16)
    rest = x - high.astype(jnp.float32)
    middle = rest.astype(jnp.bfloat16)
    low = (rest - middle.astype(jnp.float32)).astype(jnp.bfloat16)
    return high, middle, low


def score_kernel(
    core_ref, place_ref, own, other, eigen, other_eigen, block, other_block, mine, theirs
):
    first = core_ref[0] == 0
    half, ka = eigen.shape
    examples, factor_rows, width = block.shape
    ks = width - ka
    coords = (
        jnp.where(first, own[...], other[...]),
        jnp.where(first, other[...], own[...]),
    )
    eigens = (
        jnp.where(first, eigen[...], other_eigen[...]),
        jnp.where(first, other_eigen[...], eigen[...]),
    )
    scales = [1.0 / (e + damping) for e in eigens]
    act = jnp.concatenate([v[:, half : half + ka // 2] for v in coords], axis=1)
    act_terms = split_three(act)
    out_terms = [split_three(v[:, :half]) for v in coords]
    order = ((0, 0), (0, 1), (1, 0), (1, 1), (0, 2), (2, 0))
    facts = jnp.concatenate([v[:examples, v.shape[1] - LANES :] for v in (own, other)], axis=0)
    rows = jnp.concatenate([block[...], other_block[...]], axis=0)
    examples = rows.shape[0]
    lane = lax.broadcasted_iota(jnp.int32, (examples, LANES), 1).astype(jnp.float32)
    row = lax.broadcasted_iota(jnp.int32, (examples, factor_rows, ka), 1).astype(jnp.float32)
    hot = lane == facts[:, :1]
    keep = row < facts[:, LANES // 2 : LANES // 2 + 1][:, :, None]
    weights = jnp.where(keep, rows[:, :, ks:].astype(jnp.float32), 0.0)
    flat = rows[:, :, :ks].reshape(examples * factor_rows, ks)
    results = []
    for q in range(act.shape[0] // RQ):
        cut = slice(q * RQ, (q + 1) * RQ)
        right = jnp.concatenate([act_terms[b][cut] for _, b in order], axis=0)
        precond = []
        for part in range(2):
            left = jnp.concatenate([out_terms[part][a][cut] for a, _ in order], axis=0)
            numer = lax.dot_general(
                left, right, (((0,), (0,)), ((), ())), preferred_element_type=jnp.float32
            )
            precond.append((numer * scales[part]).astype(jnp.bfloat16))
        precond = jnp.concatenate(precond, axis=0)
        projected = jnp.dot(flat, precond, preferred_element_type=jnp.float32)
        terms = projected.reshape(examples, factor_rows, ka) * weights
        per_example = jnp.sum(jnp.sum(terms, axis=1), axis=1, keepdims=True)
        results.append(jnp.sum(jnp.where(hot, per_example, 0.0), axis=0, keepdims=True))
    queries, total = mine.shape
    low = place_ref[0] % 2 == 0
    for q in range(queries):
        here, there = results[q][:, :total], results[queries + q][:, :total]
        mine[q : q + 1, :] = jnp.where(low, here, there)
        theirs[q : q + 1, :] = jnp.where(low, there, here)


def score(core, place, own, other, eigen, other_eigen, block, other_block, total):
    half = jax.ShapeDtypeStruct((own.shape[0] // (2 * RQ), total), jnp.float32)
    return pl.pallas_call(
        score_kernel,
        out_shape=[half, half],
        in_specs=[spec(pltpu.SMEM)] * 2 + [spec(pltpu.VMEM)] * 6,
        out_specs=[spec(pltpu.VMEM)] * 2,
        compiler_params=grant(12),
    )(core, place, own, other, eigen, other_eigen, block, other_block)


def direct(
    query_out,
    query_act,
    out_basis,
    act_basis,
    eigenvalues,
    train_out,
    train_act,
    train_tokens,
    train_ids,
):
    parts = lax.axis_size("blk")
    lines = parts // 2
    swap = [(0, 1), (1, 0)]

    def across(x, distance):
        return lax.ppermute(x, "blk", [(s, s ^ distance) for s in range(parts)])

    place = lax.axis_index("blk").reshape(1)
    core = lax.axis_index("fsdp").reshape(1)
    other_eigen = lax.ppermute(eigenvalues, "fsdp", swap)
    block = pack(train_out, train_act)
    total = project(block, query_out.T, query_act.T, out_basis, act_basis)
    kept, moved = spread(place, train_tokens, train_ids, other_eigen, total, lines)
    block = join(kept, block, across(block, 4))
    sums = kept + across(moved, 2)
    block = join(sums, block, across(block, 2))
    other_block = lax.ppermute(block, "fsdp", swap)
    sums = sums[0] + across(sums[1], 4)
    shared = sums.shape[1] - LANES
    coords = sums[:, :shared] + across(sums[:, :shared], 1)
    own = jnp.concatenate([coords, sums[:, shared:]], axis=1)
    other = lax.ppermute(own, "fsdp", swap)
    mine, theirs = score(
        core,
        place,
        own,
        other,
        eigenvalues,
        other_eigen,
        block,
        other_block,
        parts * 2 * train_out.shape[0],
    )
    return mine + across(theirs, 1)


def score_block(precond, out_rows, act_rows, token_counts):
    factor_rows = out_rows.shape[1]
    valid = (
        lax.broadcasted_iota(jnp.int32, (out_rows.shape[0], factor_rows), 1) < token_counts[:, None]
    ).astype(jnp.float32)
    projected = jnp.einsum("nri,qij->nrqj", out_rows, precond, preferred_element_type=jnp.float32)
    weights = act_rows.astype(jnp.float32) * valid[:, :, None]
    return jnp.einsum("nrqj,nrj->qn", projected, weights, precision=lax.Precision.HIGHEST)


def gathered(
    query_out,
    query_act,
    out_basis,
    act_basis,
    eigenvalues,
    train_out,
    train_act,
    train_tokens,
    train_ids,
):
    half_ks = out_basis.shape[1]
    local_rows = query_out.shape[1] // lax.axis_size("blk")
    out_part = lax.dot_general(
        query_out, out_basis, (((0,), (0,)), ((), ())), preferred_element_type=jnp.float32
    )
    act_part = lax.dot_general(
        query_act, act_basis, (((0,), (0,)), ((), ())), preferred_element_type=jnp.float32
    )
    rotated = lax.psum_scatter(
        jnp.concatenate([out_part, act_part], axis=1), "blk", scatter_dimension=0, tiled=True
    )
    out_coords = rotated[:, :half_ks]
    act_half = rotated[:, half_ks:]
    act_coords = lax.all_gather(act_half, "fsdp", axis=1, tiled=True)
    queries = local_rows // RQ
    out_three = out_coords.reshape(queries, RQ, half_ks)
    act_three = act_coords.reshape(queries, RQ, act_coords.shape[1])
    numer = jnp.einsum("qri,qrj->qij", out_three, act_three, precision=lax.Precision.HIGHEST)
    precond = (numer / (eigenvalues + damping)).astype(jnp.bfloat16)
    train_total = train_out.shape[0] * lax.axis_size("blk") * lax.axis_size("fsdp")
    empty = jnp.zeros((queries, train_total), jnp.float32)
    full_precond = lax.all_gather(precond, "fsdp", axis=1, tiled=True)
    out_rows = lax.all_gather(train_out, "blk", axis=0, tiled=True)
    act_rows = lax.all_gather(train_act, "blk", axis=0, tiled=True)
    token_counts = lax.all_gather(train_tokens, "blk", axis=0, tiled=True)
    column_ids = lax.all_gather(train_ids, "blk", axis=0, tiled=True)
    scores = empty.at[:, column_ids].add(
        score_block(full_precond, out_rows, act_rows, token_counts)
    )
    return lax.psum(scores, "fsdp")


def solution(mesh):
    parts = mesh.shape["blk"]
    few = parts == DIRECT_PARTS and mesh.shape["fsdp"] == 2
    return jax.shard_map(
        direct if few else gathered,
        mesh=mesh,
        in_specs=(
            P("blk", None),
            P("blk", None),
            P("blk", "fsdp"),
            P("blk", "fsdp"),
            P("fsdp", None),
            P(("groups", "blk", "fsdp"), None, None),
            P(("groups", "blk", "fsdp"), None, None),
            P(("groups", "blk", "fsdp")),
            P(("groups", "blk", "fsdp")),
        ),
        out_specs=P("blk", "groups"),
        check_vma=False,
    )
```

```python
import functools

import jax
import jax.numpy as jnp
from jax import lax
from jax.experimental import pallas as pl
from jax.experimental.pallas import tpu as pltpu
from jax.sharding import PartitionSpec as P

RQ = 4
LANES = 128
DIRECT_PARTS = 8
WAIT_FLOPS = 10**9


damping = 0.1


def pinned(x):
    return pltpu.with_memory_space_constraint(x, pltpu.HBM)


def grant(mebibytes):
    return pltpu.CompilerParams(vmem_limit_bytes=mebibytes * 2**20)


def spec(space):
    return pl.BlockSpec(memory_space=space)


def pack_kernel(train_out, train_act, packed, sems):
    ks = train_out.shape[2]
    copies = (
        pltpu.make_async_copy(train_out, packed.at[:, :, :ks], sems.at[0]),
        pltpu.make_async_copy(train_act, packed.at[:, :, ks:], sems.at[1]),
    )
    for copy in copies:
        copy.start()
    for copy in copies:
        copy.wait()


def pack(train_out, train_act):
    examples, rows, ks = train_out.shape
    shape = (examples, rows, ks + train_act.shape[2])
    return pl.pallas_call(
        pack_kernel,
        out_shape=jax.ShapeDtypeStruct(shape, train_out.dtype),
        in_specs=[spec(pltpu.HBM)] * 2,
        out_specs=spec(pltpu.VMEM),
        scratch_shapes=[pltpu.SemaphoreType.DMA((2,))],
        compiler_params=grant(2),
        cost_estimate=pl.CostEstimate(flops=WAIT_FLOPS, bytes_accessed=0, transcendentals=0),
    )(pinned(train_out), pinned(train_act))


def join_kernel(after, first, second, joined):
    del after
    count = first.shape[0]
    joined[:count] = first[...]
    joined[count:] = second[...]


def joined_shape(first, second):
    return jax.ShapeDtypeStruct(
        (first.shape[0] + second.shape[0],) + first.shape[1:], first.dtype
    )


def join(after, first, second):
    return pl.pallas_call(
        join_kernel,
        out_shape=joined_shape(first, second),
        in_specs=[spec(pl.ANY)] + [spec(pltpu.VMEM)] * 2,
        out_specs=spec(pltpu.VMEM),
        compiler_params=grant(4),
    )(after, first, second)


def project_kernel(after, query_out, query_act, out_basis, act_basis, total):
    del after
    half_ks = out_basis.shape[1]
    total[:, :half_ks] = jnp.dot(
        query_out[...], out_basis[...], preferred_element_type=jnp.float32
    )
    total[:, half_ks:] = jnp.dot(
        query_act[...], act_basis[...], preferred_element_type=jnp.float32
    )


def project(after, query_out, query_act, out_basis, act_basis):
    columns = query_out.shape[0]
    width = out_basis.shape[1] + act_basis.shape[1]
    operands = (query_out, query_act, out_basis, act_basis)
    return pl.pallas_call(
        project_kernel,
        out_shape=jax.ShapeDtypeStruct((columns, width), jnp.float32),
        in_specs=[spec(pl.ANY)] + [spec(pltpu.VMEM)] * len(operands),
        out_specs=spec(pltpu.VMEM),
        compiler_params=grant(8),
        cost_estimate=pl.CostEstimate(
            flops=2 * columns * (out_basis.size + act_basis.size),
            bytes_accessed=2 * sum(x.size for x in operands),
            transcendentals=0,
        ),
    )(after, *operands)


def doubling_slot(distance, parts):
    bits = parts.bit_length() - 1
    return sum(1 << (bits - 1 - i) for i in range(bits) if distance >> i & 1)


def spread_kernel(place_ref, tokens_ref, ids_ref, after, total, kept, moved):
    del after
    lines, rows, _ = kept.shape
    lines = 2 * lines
    width = total.shape[1]
    line = place_ref[0] // 2
    row = lax.broadcasted_iota(jnp.int32, (rows, LANES), 0)
    lane = lax.broadcasted_iota(jnp.int32, (rows, LANES), 1)
    facts = jnp.where(lane < LANES // 2, ids_ref[0], tokens_ref[0]).astype(jnp.float32)
    for k in range(lines):
        start = pl.multiple_of((line ^ k) * rows, rows)
        piece = (moved if k % 2 else kept).at[k // 2]
        piece[:, :width] = total[pl.ds(start, rows), :]
        piece[:, width:] = jnp.where(row == doubling_slot(k, lines), facts, 0.0)


def spread(place, tokens, ids, after, total, lines):
    half = jax.ShapeDtypeStruct(
        (lines // 2, total.shape[0] // lines, total.shape[1] + LANES), jnp.float32
    )
    return pl.pallas_call(
        spread_kernel,
        out_shape=[half, half],
        in_specs=[spec(pltpu.SMEM)] * 3 + [spec(pl.ANY), spec(pltpu.VMEM)],
        out_specs=[spec(pltpu.VMEM)] * 2,
        compiler_params=grant(4),
    )(place, tokens, ids, after, total)


def split_three(x):
    high = x.astype(jnp.bfloat16)
    rest = x - high.astype(jnp.float32)
    middle = rest.astype(jnp.bfloat16)
    low = (rest - middle.astype(jnp.float32)).astype(jnp.bfloat16)
    return high, middle, low


def score_kernel(
    core_ref, place_ref, own, other, eigen, other_eigen, blocks, handed, mine, theirs
):
    first = core_ref[0] == 0
    half, ka = eigen.shape
    examples, factor_rows, width = blocks.shape
    ks = width - ka
    coords = (
        jnp.where(first, own[...], other[...]),
        jnp.where(first, other[...], own[...]),
    )
    eigens = (
        jnp.where(first, eigen[...], other_eigen[...]),
        jnp.where(first, other_eigen[...], eigen[...]),
    )
    scales = [1.0 / (e + damping) for e in eigens]
    act = jnp.concatenate([v[:, half : half + ka // 2] for v in coords], axis=1)
    act_terms = split_three(act)
    out_terms = [split_three(v[:, :half]) for v in coords]
    order = ((0, 0), (0, 1), (1, 0), (1, 1), (0, 2), (2, 0))
    facts = [v[: examples // 2, v.shape[1] - LANES :] for v in coords]
    facts = jnp.concatenate(facts, axis=0)
    rows = jnp.where(first, handed[...], blocks[...])
    rows = rows.reshape(examples // 2, 2, factor_rows, width)
    rows = jnp.concatenate([rows[:, 0], rows[:, 1]], axis=0)
    lane = lax.broadcasted_iota(jnp.int32, (examples, LANES), 1).astype(jnp.float32)
    row = lax.broadcasted_iota(jnp.int32, (examples, factor_rows, ka), 1).astype(jnp.float32)
    hot = lane == facts[:, :1]
    keep = row < facts[:, LANES // 2 : LANES // 2 + 1][:, :, None]
    weights = jnp.where(keep, rows[:, :, ks:].astype(jnp.float32), 0.0)
    flat = rows[:, :, :ks].reshape(examples * factor_rows, ks)
    results = []
    for q in range(act.shape[0] // RQ):
        cut = slice(q * RQ, (q + 1) * RQ)
        right = jnp.concatenate([act_terms[b][cut] for _, b in order], axis=0)
        precond = []
        for part in range(2):
            left = jnp.concatenate([out_terms[part][a][cut] for a, _ in order], axis=0)
            numer = lax.dot_general(
                left, right, (((0,), (0,)), ((), ())), preferred_element_type=jnp.float32
            )
            precond.append((numer * scales[part]).astype(jnp.bfloat16))
        precond = jnp.concatenate(precond, axis=0)
        projected = jnp.dot(flat, precond, preferred_element_type=jnp.float32)
        terms = projected.reshape(examples, factor_rows, ka) * weights
        per_example = jnp.sum(jnp.sum(terms, axis=1), axis=1, keepdims=True)
        results.append(jnp.sum(jnp.where(hot, per_example, 0.0), axis=0, keepdims=True))
    queries, total = mine.shape
    low = place_ref[0] % 2 == 0
    for q in range(queries):
        here, there = results[q][:, :total], results[queries + q][:, :total]
        mine[q : q + 1, :] = jnp.where(low, here, there)
        theirs[q : q + 1, :] = jnp.where(low, there, here)


def score(core, place, own, other, eigen, other_eigen, blocks, handed, total):
    half = jax.ShapeDtypeStruct((own.shape[0] // (2 * RQ), total), jnp.float32)
    return pl.pallas_call(
        score_kernel,
        out_shape=[half, half],
        in_specs=[spec(pltpu.SMEM)] * 2 + [spec(pltpu.VMEM)] * 6,
        out_specs=[spec(pltpu.VMEM)] * 2,
        compiler_params=grant(12),
    )(core, place, own, other, eigen, other_eigen, blocks, handed)


def direct(
    query_out,
    query_act,
    out_basis,
    act_basis,
    eigenvalues,
    train_out,
    train_act,
    train_tokens,
    train_ids,
):
    parts = lax.axis_size("blk")
    lines = parts // 2
    swap = [(0, 1), (1, 0)]

    def across(x, distance):
        return lax.ppermute(x, "blk", [(s, s ^ distance) for s in range(parts)])

    def second_core(x, distance):
        pairs = [(2 * s + 1, 2 * (s ^ distance) + 1) for s in range(parts)]
        return lax.ppermute(x, ("blk", "fsdp"), pairs)

    place = lax.axis_index("blk").reshape(1)
    core = lax.axis_index("fsdp").reshape(1)
    other_eigen = lax.ppermute(eigenvalues, "fsdp", swap)
    block = pack(train_out, train_act)
    pair = join(block, lax.ppermute(block, "fsdp", [(0, 1)]), block)
    total = project(pair, query_out.T, query_act.T, out_basis, act_basis)
    kept, moved = spread(place, train_tokens, train_ids, other_eigen, total, lines)
    pairs = join(kept, pair, second_core(pair, 4))
    sums = kept + across(moved, 2)
    blocks = join(sums, pairs, second_core(pairs, 2))
    handed = lax.ppermute(blocks, "fsdp", [(1, 0)])
    sums = sums[0] + across(sums[1], 4)
    shared = sums.shape[1] - LANES
    coords = sums[:, :shared] + across(sums[:, :shared], 1)
    own = jnp.concatenate([coords, sums[:, shared:]], axis=1)
    other = lax.ppermute(own, "fsdp", swap)
    mine, theirs = score(
        core,
        place,
        own,
        other,
        eigenvalues,
        other_eigen,
        blocks,
        handed,
        parts * 2 * train_out.shape[0],
    )
    return mine + across(theirs, 1)


def score_block(precond, out_rows, act_rows, token_counts):
    factor_rows = out_rows.shape[1]
    valid = (
        lax.broadcasted_iota(jnp.int32, (out_rows.shape[0], factor_rows), 1) < token_counts[:, None]
    ).astype(jnp.float32)
    projected = jnp.einsum("nri,qij->nrqj", out_rows, precond, preferred_element_type=jnp.float32)
    weights = act_rows.astype(jnp.float32) * valid[:, :, None]
    return jnp.einsum("nrqj,nrj->qn", projected, weights, precision=lax.Precision.HIGHEST)


def gathered(
    query_out,
    query_act,
    out_basis,
    act_basis,
    eigenvalues,
    train_out,
    train_act,
    train_tokens,
    train_ids,
):
    half_ks = out_basis.shape[1]
    local_rows = query_out.shape[1] // lax.axis_size("blk")
    out_part = lax.dot_general(
        query_out, out_basis, (((0,), (0,)), ((), ())), preferred_element_type=jnp.float32
    )
    act_part = lax.dot_general(
        query_act, act_basis, (((0,), (0,)), ((), ())), preferred_element_type=jnp.float32
    )
    rotated = lax.psum_scatter(
        jnp.concatenate([out_part, act_part], axis=1), "blk", scatter_dimension=0, tiled=True
    )
    out_coords = rotated[:, :half_ks]
    act_half = rotated[:, half_ks:]
    act_coords = lax.all_gather(act_half, "fsdp", axis=1, tiled=True)
    queries = local_rows // RQ
    out_three = out_coords.reshape(queries, RQ, half_ks)
    act_three = act_coords.reshape(queries, RQ, act_coords.shape[1])
    numer = jnp.einsum("qri,qrj->qij", out_three, act_three, precision=lax.Precision.HIGHEST)
    precond = (numer / (eigenvalues + damping)).astype(jnp.bfloat16)
    train_total = train_out.shape[0] * lax.axis_size("blk") * lax.axis_size("fsdp")
    empty = jnp.zeros((queries, train_total), jnp.float32)
    full_precond = lax.all_gather(precond, "fsdp", axis=1, tiled=True)
    out_rows = lax.all_gather(train_out, "blk", axis=0, tiled=True)
    act_rows = lax.all_gather(train_act, "blk", axis=0, tiled=True)
    token_counts = lax.all_gather(train_tokens, "blk", axis=0, tiled=True)
    column_ids = lax.all_gather(train_ids, "blk", axis=0, tiled=True)
    scores = empty.at[:, column_ids].add(
        score_block(full_precond, out_rows, act_rows, token_counts)
    )
    return lax.psum(scores, "fsdp")


def solution(mesh):
    parts = mesh.shape["blk"]
    few = parts == DIRECT_PARTS and mesh.shape["fsdp"] == 2
    return jax.shard_map(
        direct if few else gathered,
        mesh=mesh,
        in_specs=(
            P("blk", None),
            P("blk", None),
            P("blk", "fsdp"),
            P("blk", "fsdp"),
            P("fsdp", None),
            P(("groups", "blk", "fsdp"), None, None),
            P(("groups", "blk", "fsdp"), None, None),
            P(("groups", "blk", "fsdp")),
            P(("groups", "blk", "fsdp")),
        ),
        out_specs=P("blk", "groups"),
        check_vma=False,
    )
```

```python
import functools

import jax
import jax.numpy as jnp
from jax import lax
from jax.experimental import pallas as pl
from jax.experimental.pallas import tpu as pltpu
from jax.sharding import PartitionSpec as P

RQ = 4
LANES = 128
DIRECT_PARTS = 8
WAIT_FLOPS = 10**9


damping = 0.1


def pinned(x):
    return pltpu.with_memory_space_constraint(x, pltpu.HBM)


def grant(mebibytes):
    return pltpu.CompilerParams(vmem_limit_bytes=mebibytes * 2**20)


def spec(space):
    return pl.BlockSpec(memory_space=space)


def pack_kernel(train_out, train_act, packed, sems):
    ks = train_out.shape[2]
    copies = (
        pltpu.make_async_copy(train_out, packed.at[:, :, :ks], sems.at[0]),
        pltpu.make_async_copy(train_act, packed.at[:, :, ks:], sems.at[1]),
    )
    for copy in copies:
        copy.start()
    for copy in copies:
        copy.wait()


def pack(train_out, train_act):
    examples, rows, ks = train_out.shape
    shape = (examples, rows, ks + train_act.shape[2])
    return pl.pallas_call(
        pack_kernel,
        out_shape=jax.ShapeDtypeStruct(shape, train_out.dtype),
        in_specs=[spec(pltpu.HBM)] * 2,
        out_specs=spec(pltpu.VMEM),
        scratch_shapes=[pltpu.SemaphoreType.DMA((2,))],
        compiler_params=grant(2),
        cost_estimate=pl.CostEstimate(flops=WAIT_FLOPS, bytes_accessed=0, transcendentals=0),
    )(pinned(train_out), pinned(train_act))


def join_kernel(after, first, second, joined):
    del after
    count = first.shape[0]
    joined[:count] = first[...]
    joined[count:] = second[...]


def joined_shape(first, second):
    return jax.ShapeDtypeStruct(
        (first.shape[0] + second.shape[0],) + first.shape[1:], first.dtype
    )


def join(after, first, second):
    return pl.pallas_call(
        join_kernel,
        out_shape=joined_shape(first, second),
        in_specs=[spec(pl.ANY)] + [spec(pltpu.VMEM)] * 2,
        out_specs=spec(pltpu.VMEM),
        compiler_params=grant(4),
    )(after, first, second)


def relay_kernel(after, source, target):
    del after
    target[...] = source[...]


def relay(after, source):
    return pl.pallas_call(
        relay_kernel,
        out_shape=jax.ShapeDtypeStruct(source.shape, source.dtype),
        in_specs=[spec(pl.ANY), spec(pltpu.VMEM)],
        out_specs=spec(pltpu.VMEM),
        compiler_params=grant(2),
    )(after, source)


def project_kernel(after, query_out, query_act, out_basis, act_basis, total):
    del after
    half_ks = out_basis.shape[1]
    total[:, :half_ks] = jnp.dot(
        query_out[...], out_basis[...], preferred_element_type=jnp.float32
    )
    total[:, half_ks:] = jnp.dot(
        query_act[...], act_basis[...], preferred_element_type=jnp.float32
    )


def project(after, query_out, query_act, out_basis, act_basis):
    columns = query_out.shape[0]
    width = out_basis.shape[1] + act_basis.shape[1]
    operands = (query_out, query_act, out_basis, act_basis)
    return pl.pallas_call(
        project_kernel,
        out_shape=jax.ShapeDtypeStruct((columns, width), jnp.float32),
        in_specs=[spec(pl.ANY)] + [spec(pltpu.VMEM)] * len(operands),
        out_specs=spec(pltpu.VMEM),
        compiler_params=grant(8),
        cost_estimate=pl.CostEstimate(
            flops=2 * columns * (out_basis.size + act_basis.size),
            bytes_accessed=2 * sum(x.size for x in operands),
            transcendentals=0,
        ),
    )(after, *operands)


def doubling_slot(distance, parts):
    bits = parts.bit_length() - 1
    return sum(1 << (bits - 1 - i) for i in range(bits) if distance >> i & 1)


def spread_kernel(place_ref, tokens_ref, ids_ref, after, total, kept, moved):
    del after
    lines, rows, _ = kept.shape
    lines = 2 * lines
    width = total.shape[1]
    line = place_ref[0] // 2
    row = lax.broadcasted_iota(jnp.int32, (rows, LANES), 0)
    lane = lax.broadcasted_iota(jnp.int32, (rows, LANES), 1)
    facts = jnp.where(lane < LANES // 2, ids_ref[0], tokens_ref[0]).astype(jnp.float32)
    for k in range(lines):
        start = pl.multiple_of((line ^ k) * rows, rows)
        piece = (moved if k % 2 else kept).at[k // 2]
        piece[:, :width] = total[pl.ds(start, rows), :]
        piece[:, width:] = jnp.where(row == doubling_slot(k, lines), facts, 0.0)


def spread(place, tokens, ids, after, total, lines):
    half = jax.ShapeDtypeStruct(
        (lines // 2, total.shape[0] // lines, total.shape[1] + LANES), jnp.float32
    )
    return pl.pallas_call(
        spread_kernel,
        out_shape=[half, half],
        in_specs=[spec(pltpu.SMEM)] * 3 + [spec(pl.ANY), spec(pltpu.VMEM)],
        out_specs=[spec(pltpu.VMEM)] * 2,
        compiler_params=grant(4),
    )(place, tokens, ids, after, total)


def split_three(x):
    high = x.astype(jnp.bfloat16)
    rest = x - high.astype(jnp.float32)
    middle = rest.astype(jnp.bfloat16)
    low = (rest - middle.astype(jnp.float32)).astype(jnp.bfloat16)
    return high, middle, low


def score_kernel(
    core_ref, place_ref, own, other, eigen, other_eigen, block, other_block, mine, theirs
):
    first = core_ref[0] == 0
    half, ka = eigen.shape
    examples, factor_rows, width = block.shape
    ks = width - ka
    shared = half + ka // 2
    far = shared + LANES
    near = own[:, :shared] + other[:, far:]
    away = other[:, :shared] + own[:, far:]
    coords = (jnp.where(first, near, away), jnp.where(first, away, near))
    eigens = (
        jnp.where(first, eigen[...], other_eigen[...]),
        jnp.where(first, other_eigen[...], eigen[...]),
    )
    scales = [1.0 / (e + damping) for e in eigens]
    act = jnp.concatenate([v[:, half:] for v in coords], axis=1)
    act_terms = split_three(act)
    out_terms = [split_three(v[:, :half]) for v in coords]
    order = ((0, 0), (0, 1), (1, 0), (1, 1), (0, 2), (2, 0))
    facts = jnp.concatenate([v[:examples, shared:far] for v in (own, other)], axis=0)
    rows = jnp.concatenate([block[...], other_block[...]], axis=0)
    examples = rows.shape[0]
    lane = lax.broadcasted_iota(jnp.int32, (examples, LANES), 1).astype(jnp.float32)
    row = lax.broadcasted_iota(jnp.int32, (examples, factor_rows, ka), 1).astype(jnp.float32)
    hot = lane == facts[:, :1]
    keep = row < facts[:, LANES // 2 : LANES // 2 + 1][:, :, None]
    weights = jnp.where(keep, rows[:, :, ks:].astype(jnp.float32), 0.0)
    flat = rows[:, :, :ks].reshape(examples * factor_rows, ks)
    results = []
    for q in range(act.shape[0] // RQ):
        cut = slice(q * RQ, (q + 1) * RQ)
        right = jnp.concatenate([act_terms[b][cut] for _, b in order], axis=0)
        precond = []
        for part in range(2):
            left = jnp.concatenate([out_terms[part][a][cut] for a, _ in order], axis=0)
            numer = lax.dot_general(
                left, right, (((0,), (0,)), ((), ())), preferred_element_type=jnp.float32
            )
            precond.append((numer * scales[part]).astype(jnp.bfloat16))
        precond = jnp.concatenate(precond, axis=0)
        projected = jnp.dot(flat, precond, preferred_element_type=jnp.float32)
        terms = projected.reshape(examples, factor_rows, ka) * weights
        per_example = jnp.sum(jnp.sum(terms, axis=1), axis=1, keepdims=True)
        results.append(jnp.sum(jnp.where(hot, per_example, 0.0), axis=0, keepdims=True))
    queries, total = mine.shape
    low = place_ref[0] % 2 == 0
    for q in range(queries):
        here, there = results[q][:, :total], results[queries + q][:, :total]
        mine[q : q + 1, :] = jnp.where(low, here, there)
        theirs[q : q + 1, :] = jnp.where(low, there, here)


def score(core, place, own, other, eigen, other_eigen, block, other_block, total):
    half = jax.ShapeDtypeStruct((own.shape[0] // (2 * RQ), total), jnp.float32)
    return pl.pallas_call(
        score_kernel,
        out_shape=[half, half],
        in_specs=[spec(pltpu.SMEM)] * 2 + [spec(pltpu.VMEM)] * 6,
        out_specs=[spec(pltpu.VMEM)] * 2,
        compiler_params=grant(12),
    )(core, place, own, other, eigen, other_eigen, block, other_block)


def direct(
    query_out,
    query_act,
    out_basis,
    act_basis,
    eigenvalues,
    train_out,
    train_act,
    train_tokens,
    train_ids,
):
    parts = lax.axis_size("blk")
    lines = parts // 2
    swap = [(0, 1), (1, 0)]

    def across(x, distance):
        return lax.ppermute(x, "blk", [(s, s ^ distance) for s in range(parts)])

    def crossed(x):
        pairs = [(2 * s + f, 2 * (s ^ 1) + 1 - f) for s in range(parts) for f in range(2)]
        return lax.ppermute(x, ("blk", "fsdp"), pairs)

    place = lax.axis_index("blk").reshape(1)
    core = lax.axis_index("fsdp").reshape(1)
    block = pack(train_out, train_act)
    other_eigen = lax.ppermute(relay(block, eigenvalues), "fsdp", swap)
    total = project(block, query_out.T, query_act.T, out_basis, act_basis)
    kept, moved = spread(place, train_tokens, train_ids, other_eigen, total, lines)
    arrived = across(block, 4)
    sums = kept + across(moved, 2)
    block = join(sums, block, arrived)
    arrived = across(block, 2)
    sums = sums[0] + across(sums[1], 4)
    sums = jnp.concatenate([sums, crossed(sums[:, : sums.shape[1] - LANES])], axis=1)
    block = join(sums, block, arrived)
    other_block = lax.ppermute(block, "fsdp", swap)
    other = lax.ppermute(sums, "fsdp", swap)
    mine, theirs = score(
        core,
        place,
        sums,
        other,
        eigenvalues,
        other_eigen,
        block,
        other_block,
        parts * 2 * train_out.shape[0],
    )
    return mine + crossed(theirs)


def score_block(precond, out_rows, act_rows, token_counts):
    factor_rows = out_rows.shape[1]
    valid = (
        lax.broadcasted_iota(jnp.int32, (out_rows.shape[0], factor_rows), 1) < token_counts[:, None]
    ).astype(jnp.float32)
    projected = jnp.einsum("nri,qij->nrqj", out_rows, precond, preferred_element_type=jnp.float32)
    weights = act_rows.astype(jnp.float32) * valid[:, :, None]
    return jnp.einsum("nrqj,nrj->qn", projected, weights, precision=lax.Precision.HIGHEST)


def gathered(
    query_out,
    query_act,
    out_basis,
    act_basis,
    eigenvalues,
    train_out,
    train_act,
    train_tokens,
    train_ids,
):
    half_ks = out_basis.shape[1]
    local_rows = query_out.shape[1] // lax.axis_size("blk")
    out_part = lax.dot_general(
        query_out, out_basis, (((0,), (0,)), ((), ())), preferred_element_type=jnp.float32
    )
    act_part = lax.dot_general(
        query_act, act_basis, (((0,), (0,)), ((), ())), preferred_element_type=jnp.float32
    )
    rotated = lax.psum_scatter(
        jnp.concatenate([out_part, act_part], axis=1), "blk", scatter_dimension=0, tiled=True
    )
    out_coords = rotated[:, :half_ks]
    act_half = rotated[:, half_ks:]
    act_coords = lax.all_gather(act_half, "fsdp", axis=1, tiled=True)
    queries = local_rows // RQ
    out_three = out_coords.reshape(queries, RQ, half_ks)
    act_three = act_coords.reshape(queries, RQ, act_coords.shape[1])
    numer = jnp.einsum("qri,qrj->qij", out_three, act_three, precision=lax.Precision.HIGHEST)
    precond = (numer / (eigenvalues + damping)).astype(jnp.bfloat16)
    train_total = train_out.shape[0] * lax.axis_size("blk") * lax.axis_size("fsdp")
    empty = jnp.zeros((queries, train_total), jnp.float32)
    full_precond = lax.all_gather(precond, "fsdp", axis=1, tiled=True)
    out_rows = lax.all_gather(train_out, "blk", axis=0, tiled=True)
    act_rows = lax.all_gather(train_act, "blk", axis=0, tiled=True)
    token_counts = lax.all_gather(train_tokens, "blk", axis=0, tiled=True)
    column_ids = lax.all_gather(train_ids, "blk", axis=0, tiled=True)
    scores = empty.at[:, column_ids].add(
        score_block(full_precond, out_rows, act_rows, token_counts)
    )
    return lax.psum(scores, "fsdp")


def solution(mesh):
    parts = mesh.shape["blk"]
    few = parts == DIRECT_PARTS and mesh.shape["fsdp"] == 2
    return jax.shard_map(
        direct if few else gathered,
        mesh=mesh,
        in_specs=(
            P("blk", None),
            P("blk", None),
            P("blk", "fsdp"),
            P("blk", "fsdp"),
            P("fsdp", None),
            P(("groups", "blk", "fsdp"), None, None),
            P(("groups", "blk", "fsdp"), None, None),
            P(("groups", "blk", "fsdp")),
            P(("groups", "blk", "fsdp")),
        ),
        out_specs=P("blk", "groups"),
        check_vma=False,
    )
```

```python
import functools

import jax
import jax.numpy as jnp
from jax import lax
from jax.experimental import pallas as pl
from jax.experimental.pallas import tpu as pltpu
from jax.sharding import PartitionSpec as P

RQ = 4
LANES = 128
DIRECT_PARTS = 8
WAIT_FLOPS = 10**9


damping = 0.1


def pinned(x):
    return pltpu.with_memory_space_constraint(x, pltpu.HBM)


def grant(mebibytes):
    return pltpu.CompilerParams(vmem_limit_bytes=mebibytes * 2**20)


def spec(space):
    return pl.BlockSpec(memory_space=space)


def pack_kernel(train_out, train_act, packed, sems):
    ks = train_out.shape[2]
    copies = (
        pltpu.make_async_copy(train_out, packed.at[:, :, :ks], sems.at[0]),
        pltpu.make_async_copy(train_act, packed.at[:, :, ks:], sems.at[1]),
    )
    for copy in copies:
        copy.start()
    for copy in copies:
        copy.wait()


def pack(train_out, train_act):
    examples, rows, ks = train_out.shape
    shape = (examples, rows, ks + train_act.shape[2])
    return pl.pallas_call(
        pack_kernel,
        out_shape=jax.ShapeDtypeStruct(shape, train_out.dtype),
        in_specs=[spec(pltpu.HBM)] * 2,
        out_specs=spec(pltpu.VMEM),
        scratch_shapes=[pltpu.SemaphoreType.DMA((2,))],
        compiler_params=grant(2),
        cost_estimate=pl.CostEstimate(flops=WAIT_FLOPS, bytes_accessed=0, transcendentals=0),
    )(pinned(train_out), pinned(train_act))


def join_kernel(after, first, second, joined):
    del after
    count = first.shape[0]
    joined[:count] = first[...]
    joined[count:] = second[...]


def joined_shape(first, second):
    return jax.ShapeDtypeStruct(
        (first.shape[0] + second.shape[0],) + first.shape[1:], first.dtype
    )


def join(after, first, second):
    return pl.pallas_call(
        join_kernel,
        out_shape=joined_shape(first, second),
        in_specs=[spec(pl.ANY)] + [spec(pltpu.VMEM)] * 2,
        out_specs=spec(pltpu.VMEM),
        compiler_params=grant(4),
    )(after, first, second)


def project_kernel(query_out, query_act, out_basis, act_basis, total):
    half_ks = out_basis.shape[1]
    total[:, :half_ks] = jnp.dot(
        query_out[...], out_basis[...], preferred_element_type=jnp.float32
    )
    total[:, half_ks:] = jnp.dot(
        query_act[...], act_basis[...], preferred_element_type=jnp.float32
    )


def project(query_out, query_act, out_basis, act_basis):
    columns = query_out.shape[0]
    width = out_basis.shape[1] + act_basis.shape[1]
    operands = (query_out, query_act, out_basis, act_basis)
    return pl.pallas_call(
        project_kernel,
        out_shape=jax.ShapeDtypeStruct((columns, width), jnp.float32),
        in_specs=[spec(pltpu.VMEM)] * len(operands),
        out_specs=spec(pltpu.VMEM),
        compiler_params=grant(8),
        cost_estimate=pl.CostEstimate(
            flops=2 * columns * (out_basis.size + act_basis.size),
            bytes_accessed=2 * sum(x.size for x in operands),
            transcendentals=0,
        ),
    )(*operands)


def doubling_slot(distance, parts):
    bits = parts.bit_length() - 1
    return sum(1 << (bits - 1 - i) for i in range(bits) if distance >> i & 1)


def spread_kernel(
    place_ref, tokens_ref, ids_ref, after, total, first, second, kept, moved, joined
):
    del after
    parts = 2 * kept.shape[0]
    local_rows = kept.shape[1]
    width = total.shape[1]
    row = lax.broadcasted_iota(jnp.int32, (local_rows, LANES), 0)
    lane = lax.broadcasted_iota(jnp.int32, (local_rows, LANES), 1)
    facts = jnp.where(lane < LANES // 2, ids_ref[0], tokens_ref[0]).astype(jnp.float32)
    for part in range(parts):
        start = pl.multiple_of((place_ref[0] ^ part) * local_rows, local_rows)
        piece = (moved if part % 2 else kept).at[part // 2]
        piece[:, :width] = total[pl.ds(start, local_rows), :]
        piece[:, width:] = jnp.where(row == doubling_slot(part, parts), facts, 0.0)
    join_kernel(None, first, second, joined)


def spread(place, tokens, ids, after, total, first, second, parts):
    half = jax.ShapeDtypeStruct(
        (parts // 2, total.shape[0] // parts, total.shape[1] + LANES), jnp.float32
    )
    return pl.pallas_call(
        spread_kernel,
        out_shape=[half, half, joined_shape(first, second)],
        in_specs=[spec(pltpu.SMEM)] * 3 + [spec(pl.ANY)] + [spec(pltpu.VMEM)] * 3,
        out_specs=[spec(pltpu.VMEM)] * 3,
        compiler_params=grant(4),
    )(place, tokens, ids, after, total, first, second)


def split_three(x):
    high = x.astype(jnp.bfloat16)
    rest = x - high.astype(jnp.float32)
    middle = rest.astype(jnp.bfloat16)
    low = (rest - middle.astype(jnp.float32)).astype(jnp.bfloat16)
    return high, middle, low


def score_kernel(core_ref, own, other, eigen, other_eigen, *rest):
    blocks, out = rest[:-1], rest[-1]
    first = core_ref[0] == 0
    half, ka = eigen.shape
    factor_rows, width = blocks[0].shape[1:]
    ks = width - ka
    shared = own.shape[1] - LANES
    mine, theirs = own[...], other[...]
    coords = (jnp.where(first, mine, theirs), jnp.where(first, theirs, mine))
    eigens = (
        jnp.where(first, eigen[...], other_eigen[...]),
        jnp.where(first, other_eigen[...], eigen[...]),
    )
    scales = [1.0 / (e + damping) for e in eigens]
    act = jnp.concatenate([v[:, half:shared] for v in coords], axis=1)
    act_terms = split_three(act)
    out_terms = [split_three(v[:, :half]) for v in coords]
    order = ((0, 0), (0, 1), (1, 0), (1, 1), (0, 2), (2, 0))
    slot = lax.broadcasted_iota(jnp.int32, (mine.shape[0], LANES), 0)
    even = (slot // 4 + slot // 2 + slot) % 2 == 0
    facts = (mine[:, shared:], theirs[:, shared:])
    facts = jnp.concatenate(
        [jnp.where(even, facts[0], facts[1]), jnp.where(even, facts[1], facts[0])], axis=0
    )
    rows = jnp.concatenate([x[...] for x in blocks], axis=0)
    examples = rows.shape[0]
    lane = lax.broadcasted_iota(jnp.int32, (examples, LANES), 1).astype(jnp.float32)
    row = lax.broadcasted_iota(jnp.int32, (examples, factor_rows, ka), 1).astype(jnp.float32)
    hot = lane == facts[:, :1]
    keep = row < facts[:, LANES // 2 : LANES // 2 + 1][:, :, None]
    weights = jnp.where(keep, rows[:, :, ks:].astype(jnp.float32), 0.0)
    flat = rows[:, :, :ks].reshape(examples * factor_rows, ks)
    for q in range(out.shape[0]):
        cut = slice(q * RQ, (q + 1) * RQ)
        right = jnp.concatenate([act_terms[b][cut] for _, b in order], axis=0)
        precond = []
        for part in range(2):
            left = jnp.concatenate([out_terms[part][a][cut] for a, _ in order], axis=0)
            numer = lax.dot_general(
                left, right, (((0,), (0,)), ((), ())), preferred_element_type=jnp.float32
            )
            precond.append((numer * scales[part]).astype(jnp.bfloat16))
        precond = jnp.concatenate(precond, axis=0)
        projected = jnp.dot(flat, precond, preferred_element_type=jnp.float32)
        terms = projected.reshape(examples, factor_rows, ka) * weights
        per_example = jnp.sum(jnp.sum(terms, axis=1), axis=1, keepdims=True)
        scores = jnp.sum(jnp.where(hot, per_example, 0.0), axis=0, keepdims=True)
        out[q : q + 1, :] = scores[:, : out.shape[1]]


def score(core, own, other, eigen, other_eigen, blocks):
    examples = sum(x.shape[0] for x in blocks)
    return pl.pallas_call(
        score_kernel,
        out_shape=jax.ShapeDtypeStruct((own.shape[0] // RQ, examples), jnp.float32),
        in_specs=[spec(pltpu.SMEM)] + [spec(pltpu.VMEM)] * (4 + len(blocks)),
        out_specs=spec(pltpu.VMEM),
        compiler_params=grant(12),
    )(core, own, other, eigen, other_eigen, *blocks)


def direct(
    query_out,
    query_act,
    out_basis,
    act_basis,
    eigenvalues,
    train_out,
    train_act,
    train_tokens,
    train_ids,
):
    parts = lax.axis_size("blk")
    steps = parts.bit_length() - 1
    swap = [(0, 1), (1, 0)]

    def across(x, i):
        return lax.ppermute(x, "blk", [(s, s ^ (1 << i)) for s in range(parts)])

    def crossed(x, i):
        pairs = [
            (2 * s + f, 2 * (s ^ (1 << i)) + 1 - f) for s in range(parts) for f in range(2)
        ]
        return lax.ppermute(x, ("blk", "fsdp"), pairs)

    place = lax.axis_index("blk").reshape(1)
    core = lax.axis_index("fsdp").reshape(1)
    other_eigen = lax.ppermute(eigenvalues, "fsdp", swap)
    block = pack(train_out, train_act)
    arrived = crossed(block, 2)
    total = project(query_out.T, query_act.T, out_basis, act_basis)
    kept, moved, block = spread(
        place, train_tokens, train_ids, other_eigen, total, block, arrived, parts
    )
    sums = (kept + across(moved, 0)).reshape((2, 2) + kept.shape[1:])
    arrived = crossed(block, 1)
    kept, moved = sums[:, 0], sums[:, 1]
    near = join(kept, block, arrived)
    far = crossed(near, 0)
    other_near = lax.ppermute(near, "fsdp", swap)
    other_far = lax.ppermute(far, "fsdp", swap)
    sums = kept + across(moved, 1)
    own = sums[0] + across(sums[1], 2)
    other = lax.ppermute(own, "fsdp", swap)
    return score(
        core, own, other, eigenvalues, other_eigen, (near, far, other_near, other_far)
    )


def score_block(precond, out_rows, act_rows, token_counts):
    factor_rows = out_rows.shape[1]
    valid = (
        lax.broadcasted_iota(jnp.int32, (out_rows.shape[0], factor_rows), 1) < token_counts[:, None]
    ).astype(jnp.float32)
    projected = jnp.einsum("nri,qij->nrqj", out_rows, precond, preferred_element_type=jnp.float32)
    weights = act_rows.astype(jnp.float32) * valid[:, :, None]
    return jnp.einsum("nrqj,nrj->qn", projected, weights, precision=lax.Precision.HIGHEST)


def gathered(
    query_out,
    query_act,
    out_basis,
    act_basis,
    eigenvalues,
    train_out,
    train_act,
    train_tokens,
    train_ids,
):
    half_ks = out_basis.shape[1]
    local_rows = query_out.shape[1] // lax.axis_size("blk")
    out_part = lax.dot_general(
        query_out, out_basis, (((0,), (0,)), ((), ())), preferred_element_type=jnp.float32
    )
    act_part = lax.dot_general(
        query_act, act_basis, (((0,), (0,)), ((), ())), preferred_element_type=jnp.float32
    )
    rotated = lax.psum_scatter(
        jnp.concatenate([out_part, act_part], axis=1), "blk", scatter_dimension=0, tiled=True
    )
    out_coords = rotated[:, :half_ks]
    act_half = rotated[:, half_ks:]
    act_coords = lax.all_gather(act_half, "fsdp", axis=1, tiled=True)
    queries = local_rows // RQ
    out_three = out_coords.reshape(queries, RQ, half_ks)
    act_three = act_coords.reshape(queries, RQ, act_coords.shape[1])
    numer = jnp.einsum("qri,qrj->qij", out_three, act_three, precision=lax.Precision.HIGHEST)
    precond = (numer / (eigenvalues + damping)).astype(jnp.bfloat16)
    train_total = train_out.shape[0] * lax.axis_size("blk") * lax.axis_size("fsdp")
    empty = jnp.zeros((queries, train_total), jnp.float32)
    full_precond = lax.all_gather(precond, "fsdp", axis=1, tiled=True)
    out_rows = lax.all_gather(train_out, "blk", axis=0, tiled=True)
    act_rows = lax.all_gather(train_act, "blk", axis=0, tiled=True)
    token_counts = lax.all_gather(train_tokens, "blk", axis=0, tiled=True)
    column_ids = lax.all_gather(train_ids, "blk", axis=0, tiled=True)
    scores = empty.at[:, column_ids].add(
        score_block(full_precond, out_rows, act_rows, token_counts)
    )
    return lax.psum(scores, "fsdp")


def solution(mesh):
    parts = mesh.shape["blk"]
    few = parts == DIRECT_PARTS and mesh.shape["fsdp"] == 2
    return jax.shard_map(
        direct if few else gathered,
        mesh=mesh,
        in_specs=(
            P("blk", None),
            P("blk", None),
            P("blk", "fsdp"),
            P("blk", "fsdp"),
            P("fsdp", None),
            P(("groups", "blk", "fsdp"), None, None),
            P(("groups", "blk", "fsdp"), None, None),
            P(("groups", "blk", "fsdp")),
            P(("groups", "blk", "fsdp")),
        ),
        out_specs=P("blk", "groups"),
        check_vma=False,
    )
```

```python
import functools

import jax
import jax.numpy as jnp
from jax import lax
from jax.experimental import pallas as pl
from jax.experimental.pallas import tpu as pltpu
from jax.sharding import PartitionSpec as P

RQ = 4
LANES = 128
DIRECT_PARTS = 8
WAIT_FLOPS = 10**9


damping = 0.1


def pinned(x):
    return pltpu.with_memory_space_constraint(x, pltpu.HBM)


def grant(mebibytes):
    return pltpu.CompilerParams(vmem_limit_bytes=mebibytes * 2**20)


def spec(space):
    return pl.BlockSpec(memory_space=space)


def pack_kernel(train_out, train_act, packed, sems):
    ks = train_out.shape[2]
    copies = (
        pltpu.make_async_copy(train_out, packed.at[:, :, :ks], sems.at[0]),
        pltpu.make_async_copy(train_act, packed.at[:, :, ks:], sems.at[1]),
    )
    for copy in copies:
        copy.start()
    for copy in copies:
        copy.wait()


def pack(train_out, train_act):
    examples, rows, ks = train_out.shape
    shape = (examples, rows, ks + train_act.shape[2])
    return pl.pallas_call(
        pack_kernel,
        out_shape=jax.ShapeDtypeStruct(shape, train_out.dtype),
        in_specs=[spec(pltpu.HBM)] * 2,
        out_specs=spec(pltpu.VMEM),
        scratch_shapes=[pltpu.SemaphoreType.DMA((2,))],
        compiler_params=grant(2),
    )(pinned(train_out), pinned(train_act))


def join_kernel(after, first, second, joined):
    del after
    count = first.shape[0]
    joined[:count] = first[...]
    joined[count:] = second[...]


def joined_shape(first, second):
    return jax.ShapeDtypeStruct(
        (first.shape[0] + second.shape[0],) + first.shape[1:], first.dtype
    )


def join(after, first, second):
    return pl.pallas_call(
        join_kernel,
        out_shape=joined_shape(first, second),
        in_specs=[spec(pl.ANY)] + [spec(pltpu.VMEM)] * 2,
        out_specs=spec(pltpu.VMEM),
        compiler_params=grant(4),
    )(after, first, second)


def relay_kernel(source, target):
    target[...] = source[...]


def relay(source):
    return pl.pallas_call(
        relay_kernel,
        out_shape=jax.ShapeDtypeStruct(source.shape, source.dtype),
        in_specs=[spec(pltpu.VMEM)],
        out_specs=spec(pltpu.VMEM),
        compiler_params=grant(2),
        cost_estimate=pl.CostEstimate(flops=WAIT_FLOPS, bytes_accessed=0, transcendentals=0),
    )(source)


def gather_sum_kernel(after, *refs):
    del after
    total = refs[0][...]
    for term in refs[1:-1]:
        total = total + term[...]
    refs[-1][...] = total


def gather_sum(after, terms):
    return pl.pallas_call(
        gather_sum_kernel,
        out_shape=jax.ShapeDtypeStruct(terms[0].shape, terms[0].dtype),
        in_specs=[spec(pl.ANY)] + [spec(pltpu.VMEM)] * len(terms),
        out_specs=spec(pltpu.VMEM),
        compiler_params=grant(4),
    )(after, *terms)


def project_kernel(query_out, query_act, out_basis, act_basis, total):
    half_ks = out_basis.shape[1]
    total[:, :half_ks] = jnp.dot(
        query_out[...], out_basis[...], preferred_element_type=jnp.float32
    )
    total[:, half_ks:] = jnp.dot(
        query_act[...], act_basis[...], preferred_element_type=jnp.float32
    )


def project(query_out, query_act, out_basis, act_basis):
    columns = query_out.shape[0]
    width = out_basis.shape[1] + act_basis.shape[1]
    operands = (query_out, query_act, out_basis, act_basis)
    return pl.pallas_call(
        project_kernel,
        out_shape=jax.ShapeDtypeStruct((columns, width), jnp.float32),
        in_specs=[spec(pltpu.VMEM)] * len(operands),
        out_specs=spec(pltpu.VMEM),
        compiler_params=grant(8),
        cost_estimate=pl.CostEstimate(
            flops=2 * columns * (out_basis.size + act_basis.size),
            bytes_accessed=2 * sum(x.size for x in operands),
            transcendentals=0,
        ),
    )(*operands)


def doubling_slot(distance, parts):
    bits = parts.bit_length() - 1
    return sum(1 << (bits - 1 - i) for i in range(bits) if distance >> i & 1)


def spread_kernel(place_ref, tokens_ref, ids_ref, after, total, first, second, *rest):
    del after
    pieces, joined = rest[:-1], rest[-1]
    groups = len(pieces)
    each, local_rows, _ = pieces[0].shape
    parts = groups * each
    width = total.shape[1]
    row = lax.broadcasted_iota(jnp.int32, (local_rows, LANES), 0)
    lane = lax.broadcasted_iota(jnp.int32, (local_rows, LANES), 1)
    facts = jnp.where(lane < LANES // 2, ids_ref[0], tokens_ref[0]).astype(jnp.float32)
    for part in range(parts):
        start = pl.multiple_of((place_ref[0] ^ part) * local_rows, local_rows)
        piece = pieces[part % groups].at[part // groups]
        piece[:, :width] = total[pl.ds(start, local_rows), :]
        piece[:, width:] = jnp.where(row == doubling_slot(part, parts), facts, 0.0)
    join_kernel(None, first, second, joined)


def spread(place, tokens, ids, after, total, first, second, parts, groups):
    piece = jax.ShapeDtypeStruct(
        (parts // groups, total.shape[0] // parts, total.shape[1] + LANES), jnp.float32
    )
    joined = jax.ShapeDtypeStruct(
        (first.shape[0] + second.shape[0],) + first.shape[1:], first.dtype
    )
    return pl.pallas_call(
        spread_kernel,
        out_shape=[piece] * groups + [joined],
        in_specs=[spec(pltpu.SMEM)] * 3 + [spec(pl.ANY)] + [spec(pltpu.VMEM)] * 3,
        out_specs=[spec(pltpu.VMEM)] * (groups + 1),
        compiler_params=grant(4),
    )(place, tokens, ids, after, total, first, second)


def split_three(x):
    high = x.astype(jnp.bfloat16)
    rest = x - high.astype(jnp.float32)
    middle = rest.astype(jnp.bfloat16)
    low = (rest - middle.astype(jnp.float32)).astype(jnp.bfloat16)
    return high, middle, low


def score_kernel(core_ref, own, other, eigen, other_eigen, *rest):
    blocks, out = rest[:-1], rest[-1]
    first = core_ref[0] == 0
    half, ka = eigen.shape
    factor_rows, width = blocks[0].shape[1:]
    ks = width - ka
    shared = own.shape[1] - LANES
    mine, theirs = own[...], other[...]
    coords = (jnp.where(first, mine, theirs), jnp.where(first, theirs, mine))
    eigens = (
        jnp.where(first, eigen[...], other_eigen[...]),
        jnp.where(first, other_eigen[...], eigen[...]),
    )
    scales = [1.0 / (e + damping) for e in eigens]
    act = jnp.concatenate([v[:, half:shared] for v in coords], axis=1)
    act_terms = split_three(act)
    out_terms = [split_three(v[:, :half]) for v in coords]
    order = ((0, 0), (0, 1), (1, 0), (1, 1), (0, 2), (2, 0))
    slot = lax.broadcasted_iota(jnp.int32, (mine.shape[0], LANES), 0)
    even = (slot // 4 + slot // 2 + slot) % 2 == 0
    facts = (mine[:, shared:], theirs[:, shared:])
    facts = jnp.concatenate(
        [jnp.where(even, facts[0], facts[1]), jnp.where(even, facts[1], facts[0])], axis=0
    )
    rows = jnp.concatenate([x[...] for x in blocks], axis=0)
    examples = rows.shape[0]
    lane = lax.broadcasted_iota(jnp.int32, (examples, LANES), 1).astype(jnp.float32)
    row = lax.broadcasted_iota(jnp.int32, (examples, factor_rows, ka), 1).astype(jnp.float32)
    hot = lane == facts[:, :1]
    keep = row < facts[:, LANES // 2 : LANES // 2 + 1][:, :, None]
    weights = jnp.where(keep, rows[:, :, ks:].astype(jnp.float32), 0.0)
    flat = rows[:, :, :ks].reshape(examples * factor_rows, ks)
    for q in range(out.shape[0]):
        cut = slice(q * RQ, (q + 1) * RQ)
        right = jnp.concatenate([act_terms[b][cut] for _, b in order], axis=0)
        precond = []
        for part in range(2):
            left = jnp.concatenate([out_terms[part][a][cut] for a, _ in order], axis=0)
            numer = lax.dot_general(
                left, right, (((0,), (0,)), ((), ())), preferred_element_type=jnp.float32
            )
            precond.append((numer * scales[part]).astype(jnp.bfloat16))
        precond = jnp.concatenate(precond, axis=0)
        projected = jnp.dot(flat, precond, preferred_element_type=jnp.float32)
        terms = projected.reshape(examples, factor_rows, ka) * weights
        per_example = jnp.sum(jnp.sum(terms, axis=1), axis=1, keepdims=True)
        scores = jnp.sum(jnp.where(hot, per_example, 0.0), axis=0, keepdims=True)
        out[q : q + 1, :] = scores[:, : out.shape[1]]


def score(core, own, other, eigen, other_eigen, blocks):
    examples = sum(x.shape[0] for x in blocks)
    return pl.pallas_call(
        score_kernel,
        out_shape=jax.ShapeDtypeStruct((own.shape[0] // RQ, examples), jnp.float32),
        in_specs=[spec(pltpu.SMEM)] + [spec(pltpu.VMEM)] * (4 + len(blocks)),
        out_specs=spec(pltpu.VMEM),
        compiler_params=grant(12),
    )(core, own, other, eigen, other_eigen, *blocks)


def direct(
    query_out,
    query_act,
    out_basis,
    act_basis,
    eigenvalues,
    train_out,
    train_act,
    train_tokens,
    train_ids,
):
    parts = lax.axis_size("blk")
    steps = parts.bit_length() - 1
    swap = [(0, 1), (1, 0)]

    def apart(x, distance):
        return lax.ppermute(x, "blk", [(s, s ^ distance) for s in range(parts)])

    def crossed(x, i):
        pairs = [
            (2 * s + f, 2 * (s ^ (1 << i)) + 1 - f) for s in range(parts) for f in range(2)
        ]
        return lax.ppermute(x, ("blk", "fsdp"), pairs)

    place = lax.axis_index("blk").reshape(1)
    core = lax.axis_index("fsdp").reshape(1)
    other_eigen = lax.ppermute(eigenvalues, "fsdp", swap)
    block = relay(pack(train_out, train_act))
    arrived = crossed(block, 2)
    total = project(query_out.T, query_act.T, out_basis, act_basis)
    *pieces, block = spread(
        place, train_tokens, train_ids, other_eigen, total, block, arrived, parts, parts // 2
    )
    near = join(pieces[0], block, crossed(block, 1))
    sums = gather_sum(near, [pieces[0]] + [apart(pieces[d], d) for d in range(1, len(pieces))])
    far = crossed(near, 0)
    other_near = lax.ppermute(near, "fsdp", swap)
    other_far = lax.ppermute(far, "fsdp", swap)
    own = sums[0] + apart(sums[1], 4)
    other = lax.ppermute(own, "fsdp", swap)
    return score(
        core, own, other, eigenvalues, other_eigen, (near, far, other_near, other_far)
    )


def score_block(precond, out_rows, act_rows, token_counts):
    factor_rows = out_rows.shape[1]
    valid = (
        lax.broadcasted_iota(jnp.int32, (out_rows.shape[0], factor_rows), 1) < token_counts[:, None]
    ).astype(jnp.float32)
    projected = jnp.einsum("nri,qij->nrqj", out_rows, precond, preferred_element_type=jnp.float32)
    weights = act_rows.astype(jnp.float32) * valid[:, :, None]
    return jnp.einsum("nrqj,nrj->qn", projected, weights, precision=lax.Precision.HIGHEST)


def gathered(
    query_out,
    query_act,
    out_basis,
    act_basis,
    eigenvalues,
    train_out,
    train_act,
    train_tokens,
    train_ids,
):
    half_ks = out_basis.shape[1]
    local_rows = query_out.shape[1] // lax.axis_size("blk")
    out_part = lax.dot_general(
        query_out, out_basis, (((0,), (0,)), ((), ())), preferred_element_type=jnp.float32
    )
    act_part = lax.dot_general(
        query_act, act_basis, (((0,), (0,)), ((), ())), preferred_element_type=jnp.float32
    )
    rotated = lax.psum_scatter(
        jnp.concatenate([out_part, act_part], axis=1), "blk", scatter_dimension=0, tiled=True
    )
    out_coords = rotated[:, :half_ks]
    act_half = rotated[:, half_ks:]
    act_coords = lax.all_gather(act_half, "fsdp", axis=1, tiled=True)
    queries = local_rows // RQ
    out_three = out_coords.reshape(queries, RQ, half_ks)
    act_three = act_coords.reshape(queries, RQ, act_coords.shape[1])
    numer = jnp.einsum("qri,qrj->qij", out_three, act_three, precision=lax.Precision.HIGHEST)
    precond = (numer / (eigenvalues + damping)).astype(jnp.bfloat16)
    train_total = train_out.shape[0] * lax.axis_size("blk") * lax.axis_size("fsdp")
    empty = jnp.zeros((queries, train_total), jnp.float32)
    full_precond = lax.all_gather(precond, "fsdp", axis=1, tiled=True)
    out_rows = lax.all_gather(train_out, "blk", axis=0, tiled=True)
    act_rows = lax.all_gather(train_act, "blk", axis=0, tiled=True)
    token_counts = lax.all_gather(train_tokens, "blk", axis=0, tiled=True)
    column_ids = lax.all_gather(train_ids, "blk", axis=0, tiled=True)
    scores = empty.at[:, column_ids].add(
        score_block(full_precond, out_rows, act_rows, token_counts)
    )
    return lax.psum(scores, "fsdp")


def solution(mesh):
    parts = mesh.shape["blk"]
    few = parts == DIRECT_PARTS and mesh.shape["fsdp"] == 2
    return jax.shard_map(
        direct if few else gathered,
        mesh=mesh,
        in_specs=(
            P("blk", None),
            P("blk", None),
            P("blk", "fsdp"),
            P("blk", "fsdp"),
            P("fsdp", None),
            P(("groups", "blk", "fsdp"), None, None),
            P(("groups", "blk", "fsdp"), None, None),
            P(("groups", "blk", "fsdp")),
            P(("groups", "blk", "fsdp")),
        ),
        out_specs=P("blk", "groups"),
        check_vma=False,
    )
```

```python
import functools

import jax
import jax.numpy as jnp
from jax import lax
from jax.experimental import pallas as pl
from jax.experimental.pallas import tpu as pltpu
from jax.sharding import PartitionSpec as P

RQ = 4
LANES = 128
DIRECT_PARTS = 8
WAIT_FLOPS = 10**9


damping = 0.1


def pinned(x):
    return pltpu.with_memory_space_constraint(x, pltpu.HBM)


def grant(mebibytes):
    return pltpu.CompilerParams(vmem_limit_bytes=mebibytes * 2**20)


def spec(space):
    return pl.BlockSpec(memory_space=space)


def pack_kernel(train_out, train_act, packed, sems):
    ks = train_out.shape[2]
    copies = (
        pltpu.make_async_copy(train_out, packed.at[:, :, :ks], sems.at[0]),
        pltpu.make_async_copy(train_act, packed.at[:, :, ks:], sems.at[1]),
    )
    for copy in copies:
        copy.start()
    for copy in copies:
        copy.wait()


def pack(train_out, train_act):
    examples, rows, ks = train_out.shape
    shape = (examples, rows, ks + train_act.shape[2])
    return pl.pallas_call(
        pack_kernel,
        out_shape=jax.ShapeDtypeStruct(shape, train_out.dtype),
        in_specs=[spec(pltpu.HBM)] * 2,
        out_specs=spec(pltpu.VMEM),
        scratch_shapes=[pltpu.SemaphoreType.DMA((2,))],
        compiler_params=grant(2),
    )(pinned(train_out), pinned(train_act))


def join_kernel(after, first, second, joined):
    del after
    count = first.shape[0]
    joined[:count] = first[...]
    joined[count:] = second[...]


def joined_shape(first, second):
    return jax.ShapeDtypeStruct(
        (first.shape[0] + second.shape[0],) + first.shape[1:], first.dtype
    )


def join(after, first, second):
    return pl.pallas_call(
        join_kernel,
        out_shape=joined_shape(first, second),
        in_specs=[spec(pl.ANY)] + [spec(pltpu.VMEM)] * 2,
        out_specs=spec(pltpu.VMEM),
        compiler_params=grant(4),
    )(after, first, second)


def relay_kernel(source, target):
    target[...] = source[...]


def relay(source):
    return pl.pallas_call(
        relay_kernel,
        out_shape=jax.ShapeDtypeStruct(source.shape, source.dtype),
        in_specs=[spec(pltpu.VMEM)],
        out_specs=spec(pltpu.VMEM),
        compiler_params=grant(2),
        cost_estimate=pl.CostEstimate(flops=WAIT_FLOPS, bytes_accessed=0, transcendentals=0),
    )(source)


def gather_sum_kernel(after, *refs):
    del after
    total = refs[0][...]
    for term in refs[1:-1]:
        total = total + term[...]
    refs[-1][...] = total


def gather_sum(after, terms):
    return pl.pallas_call(
        gather_sum_kernel,
        out_shape=jax.ShapeDtypeStruct(terms[0].shape, terms[0].dtype),
        in_specs=[spec(pl.ANY)] + [spec(pltpu.VMEM)] * len(terms),
        out_specs=spec(pltpu.VMEM),
        compiler_params=grant(4),
    )(after, *terms)


def project_kernel(query_out, query_act, out_basis, act_basis, total):
    half_ks = out_basis.shape[1]
    total[:, :half_ks] = jnp.dot(
        query_out[...], out_basis[...], preferred_element_type=jnp.float32
    )
    total[:, half_ks:] = jnp.dot(
        query_act[...], act_basis[...], preferred_element_type=jnp.float32
    )


def project(query_out, query_act, out_basis, act_basis):
    columns = query_out.shape[0]
    width = out_basis.shape[1] + act_basis.shape[1]
    operands = (query_out, query_act, out_basis, act_basis)
    return pl.pallas_call(
        project_kernel,
        out_shape=jax.ShapeDtypeStruct((columns, width), jnp.float32),
        in_specs=[spec(pltpu.VMEM)] * len(operands),
        out_specs=spec(pltpu.VMEM),
        compiler_params=grant(8),
        cost_estimate=pl.CostEstimate(
            flops=2 * columns * (out_basis.size + act_basis.size),
            bytes_accessed=2 * sum(x.size for x in operands),
            transcendentals=0,
        ),
    )(*operands)


def doubling_slot(distance, parts):
    bits = parts.bit_length() - 1
    return sum(1 << (bits - 1 - i) for i in range(bits) if distance >> i & 1)


def spread_kernel(place_ref, tokens_ref, ids_ref, after, total, first, second, *rest):
    del after
    pieces, joined = rest[:-1], rest[-1]
    groups = len(pieces)
    each, local_rows, _ = pieces[0].shape
    parts = groups * each
    width = total.shape[1]
    row = lax.broadcasted_iota(jnp.int32, (local_rows, LANES), 0)
    lane = lax.broadcasted_iota(jnp.int32, (local_rows, LANES), 1)
    facts = jnp.where(lane < LANES // 2, ids_ref[0], tokens_ref[0]).astype(jnp.float32)
    for part in range(parts):
        start = pl.multiple_of((place_ref[0] ^ part) * local_rows, local_rows)
        piece = pieces[part % groups].at[part // groups]
        piece[:, :width] = total[pl.ds(start, local_rows), :]
        piece[:, width:] = jnp.where(row == doubling_slot(part, parts), facts, 0.0)
    join_kernel(None, first, second, joined)


def spread(place, tokens, ids, after, total, first, second, parts, groups):
    piece = jax.ShapeDtypeStruct(
        (parts // groups, total.shape[0] // parts, total.shape[1] + LANES), jnp.float32
    )
    joined = jax.ShapeDtypeStruct(
        (first.shape[0] + second.shape[0],) + first.shape[1:], first.dtype
    )
    return pl.pallas_call(
        spread_kernel,
        out_shape=[piece] * groups + [joined],
        in_specs=[spec(pltpu.SMEM)] * 3 + [spec(pl.ANY)] + [spec(pltpu.VMEM)] * 3,
        out_specs=[spec(pltpu.VMEM)] * (groups + 1),
        compiler_params=grant(4),
    )(place, tokens, ids, after, total, first, second)


def split_three(x):
    high = x.astype(jnp.bfloat16)
    rest = x - high.astype(jnp.float32)
    middle = rest.astype(jnp.bfloat16)
    low = (rest - middle.astype(jnp.float32)).astype(jnp.bfloat16)
    return high, middle, low


def score_kernel(core_ref, own, other, eigen, other_eigen, *rest):
    blocks, out = rest[:-1], rest[-1]
    first = core_ref[0] == 0
    half, ka = eigen.shape
    factor_rows, width = blocks[0].shape[1:]
    ks = width - ka
    shared = own.shape[1] - LANES
    mine, theirs = own[...], other[...]
    coords = (jnp.where(first, mine, theirs), jnp.where(first, theirs, mine))
    eigens = (
        jnp.where(first, eigen[...], other_eigen[...]),
        jnp.where(first, other_eigen[...], eigen[...]),
    )
    scales = [1.0 / (e + damping) for e in eigens]
    act = jnp.concatenate([v[:, half:shared] for v in coords], axis=1)
    act_terms = split_three(act)
    out_terms = [split_three(v[:, :half]) for v in coords]
    order = ((0, 0), (0, 1), (1, 0), (1, 1), (0, 2), (2, 0))
    slot = lax.broadcasted_iota(jnp.int32, (mine.shape[0], LANES), 0)
    even = (slot // 4 + slot // 2 + slot) % 2 == 0
    facts = (mine[:, shared:], theirs[:, shared:])
    facts = jnp.concatenate(
        [jnp.where(even, facts[0], facts[1]), jnp.where(even, facts[1], facts[0])], axis=0
    )
    rows = jnp.concatenate([x[...] for x in blocks], axis=0)
    examples = rows.shape[0]
    lane = lax.broadcasted_iota(jnp.int32, (examples, LANES), 1).astype(jnp.float32)
    row = lax.broadcasted_iota(jnp.int32, (examples, factor_rows, ka), 1).astype(jnp.float32)
    hot = lane == facts[:, :1]
    keep = row < facts[:, LANES // 2 : LANES // 2 + 1][:, :, None]
    weights = jnp.where(keep, rows[:, :, ks:].astype(jnp.float32), 0.0)
    flat = rows[:, :, :ks].reshape(examples * factor_rows, ks)
    for q in range(out.shape[0]):
        cut = slice(q * RQ, (q + 1) * RQ)
        right = jnp.concatenate([act_terms[b][cut] for _, b in order], axis=0)
        precond = []
        for part in range(2):
            left = jnp.concatenate([out_terms[part][a][cut] for a, _ in order], axis=0)
            numer = lax.dot_general(
                left, right, (((0,), (0,)), ((), ())), preferred_element_type=jnp.float32
            )
            precond.append((numer * scales[part]).astype(jnp.bfloat16))
        precond = jnp.concatenate(precond, axis=0)
        projected = jnp.dot(flat, precond, preferred_element_type=jnp.float32)
        terms = projected.reshape(examples, factor_rows, ka) * weights
        per_example = jnp.sum(jnp.sum(terms, axis=1), axis=1, keepdims=True)
        scores = jnp.sum(jnp.where(hot, per_example, 0.0), axis=0, keepdims=True)
        out[q : q + 1, :] = scores[:, : out.shape[1]]


def score(core, own, other, eigen, other_eigen, blocks):
    examples = sum(x.shape[0] for x in blocks)
    return pl.pallas_call(
        score_kernel,
        out_shape=jax.ShapeDtypeStruct((own.shape[0] // RQ, examples), jnp.float32),
        in_specs=[spec(pltpu.SMEM)] + [spec(pltpu.VMEM)] * (4 + len(blocks)),
        out_specs=spec(pltpu.VMEM),
        compiler_params=grant(12),
    )(core, own, other, eigen, other_eigen, *blocks)


def direct(
    query_out,
    query_act,
    out_basis,
    act_basis,
    eigenvalues,
    train_out,
    train_act,
    train_tokens,
    train_ids,
):
    parts = lax.axis_size("blk")
    steps = parts.bit_length() - 1
    swap = [(0, 1), (1, 0)]

    def apart(x, distance):
        return lax.ppermute(x, "blk", [(s, s ^ distance) for s in range(parts)])

    def crossed(x, i):
        pairs = [
            (2 * s + f, 2 * (s ^ (1 << i)) + 1 - f) for s in range(parts) for f in range(2)
        ]
        return lax.ppermute(x, ("blk", "fsdp"), pairs)

    place = lax.axis_index("blk").reshape(1)
    core = lax.axis_index("fsdp").reshape(1)
    other_eigen = lax.ppermute(eigenvalues, "fsdp", swap)
    block = relay(pack(train_out, train_act))
    arrived = crossed(block, 2)
    total = project(query_out.T, query_act.T, out_basis, act_basis)
    *pieces, block = spread(
        place, train_tokens, train_ids, other_eigen, total, block, arrived, parts, parts // 2
    )
    near = join(pieces[0], block, crossed(block, 1))
    far_first = reversed(range(1, len(pieces)))
    terms = [pieces[0]] + [apart(pieces[d], d) for d in far_first]
    sums = gather_sum(near, terms)
    far = crossed(near, 0)
    other_near = lax.ppermute(near, "fsdp", swap)
    other_far = lax.ppermute(far, "fsdp", swap)
    own = sums[0] + apart(sums[1], 4)
    other = lax.ppermute(own, "fsdp", swap)
    return score(
        core, own, other, eigenvalues, other_eigen, (near, far, other_near, other_far)
    )


def score_block(precond, out_rows, act_rows, token_counts):
    factor_rows = out_rows.shape[1]
    valid = (
        lax.broadcasted_iota(jnp.int32, (out_rows.shape[0], factor_rows), 1) < token_counts[:, None]
    ).astype(jnp.float32)
    projected = jnp.einsum("nri,qij->nrqj", out_rows, precond, preferred_element_type=jnp.float32)
    weights = act_rows.astype(jnp.float32) * valid[:, :, None]
    return jnp.einsum("nrqj,nrj->qn", projected, weights, precision=lax.Precision.HIGHEST)


def gathered(
    query_out,
    query_act,
    out_basis,
    act_basis,
    eigenvalues,
    train_out,
    train_act,
    train_tokens,
    train_ids,
):
    half_ks = out_basis.shape[1]
    local_rows = query_out.shape[1] // lax.axis_size("blk")
    out_part = lax.dot_general(
        query_out, out_basis, (((0,), (0,)), ((), ())), preferred_element_type=jnp.float32
    )
    act_part = lax.dot_general(
        query_act, act_basis, (((0,), (0,)), ((), ())), preferred_element_type=jnp.float32
    )
    rotated = lax.psum_scatter(
        jnp.concatenate([out_part, act_part], axis=1), "blk", scatter_dimension=0, tiled=True
    )
    out_coords = rotated[:, :half_ks]
    act_half = rotated[:, half_ks:]
    act_coords = lax.all_gather(act_half, "fsdp", axis=1, tiled=True)
    queries = local_rows // RQ
    out_three = out_coords.reshape(queries, RQ, half_ks)
    act_three = act_coords.reshape(queries, RQ, act_coords.shape[1])
    numer = jnp.einsum("qri,qrj->qij", out_three, act_three, precision=lax.Precision.HIGHEST)
    precond = (numer / (eigenvalues + damping)).astype(jnp.bfloat16)
    train_total = train_out.shape[0] * lax.axis_size("blk") * lax.axis_size("fsdp")
    empty = jnp.zeros((queries, train_total), jnp.float32)
    full_precond = lax.all_gather(precond, "fsdp", axis=1, tiled=True)
    out_rows = lax.all_gather(train_out, "blk", axis=0, tiled=True)
    act_rows = lax.all_gather(train_act, "blk", axis=0, tiled=True)
    token_counts = lax.all_gather(train_tokens, "blk", axis=0, tiled=True)
    column_ids = lax.all_gather(train_ids, "blk", axis=0, tiled=True)
    scores = empty.at[:, column_ids].add(
        score_block(full_precond, out_rows, act_rows, token_counts)
    )
    return lax.psum(scores, "fsdp")


def solution(mesh):
    parts = mesh.shape["blk"]
    few = parts == DIRECT_PARTS and mesh.shape["fsdp"] == 2
    return jax.shard_map(
        direct if few else gathered,
        mesh=mesh,
        in_specs=(
            P("blk", None),
            P("blk", None),
            P("blk", "fsdp"),
            P("blk", "fsdp"),
            P("fsdp", None),
            P(("groups", "blk", "fsdp"), None, None),
            P(("groups", "blk", "fsdp"), None, None),
            P(("groups", "blk", "fsdp")),
            P(("groups", "blk", "fsdp")),
        ),
        out_specs=P("blk", "groups"),
        check_vma=False,
    )
```

```python
import functools

import jax
import jax.numpy as jnp
from jax import lax
from jax.experimental import pallas as pl
from jax.experimental.pallas import tpu as pltpu
from jax.sharding import PartitionSpec as P

RQ = 4
LANES = 128
DIRECT_PARTS = 8
DIRECT_STEPS = (0, 5, 4, 1)
LAST_STEP = 2
WAIT_FLOPS = 10**9


damping = 0.1


def pinned(x):
    return pltpu.with_memory_space_constraint(x, pltpu.HBM)


def grant(mebibytes):
    return pltpu.CompilerParams(vmem_limit_bytes=mebibytes * 2**20)


def spec(space):
    return pl.BlockSpec(memory_space=space)


def pack_kernel(train_out, train_act, packed, sems):
    ks = train_out.shape[2]
    copies = (
        pltpu.make_async_copy(train_out, packed.at[:, :, :ks], sems.at[0]),
        pltpu.make_async_copy(train_act, packed.at[:, :, ks:], sems.at[1]),
    )
    for copy in copies:
        copy.start()
    for copy in copies:
        copy.wait()


def pack(train_out, train_act):
    examples, rows, ks = train_out.shape
    shape = (examples, rows, ks + train_act.shape[2])
    return pl.pallas_call(
        pack_kernel,
        out_shape=jax.ShapeDtypeStruct(shape, train_out.dtype),
        in_specs=[spec(pltpu.HBM)] * 2,
        out_specs=spec(pltpu.VMEM),
        scratch_shapes=[pltpu.SemaphoreType.DMA((2,))],
        compiler_params=grant(2),
    )(pinned(train_out), pinned(train_act))


def join_kernel(after, first, second, joined):
    del after
    count = first.shape[0]
    joined[:count] = first[...]
    joined[count:] = second[...]


def joined_shape(first, second):
    return jax.ShapeDtypeStruct(
        (first.shape[0] + second.shape[0],) + first.shape[1:], first.dtype
    )


def join(after, first, second):
    return pl.pallas_call(
        join_kernel,
        out_shape=joined_shape(first, second),
        in_specs=[spec(pl.ANY)] + [spec(pltpu.VMEM)] * 2,
        out_specs=spec(pltpu.VMEM),
        compiler_params=grant(4),
    )(after, first, second)


def relay_kernel(source, target):
    target[...] = source[...]


def relay(source):
    return pl.pallas_call(
        relay_kernel,
        out_shape=jax.ShapeDtypeStruct(source.shape, source.dtype),
        in_specs=[spec(pltpu.VMEM)],
        out_specs=spec(pltpu.VMEM),
        compiler_params=grant(2),
        cost_estimate=pl.CostEstimate(flops=WAIT_FLOPS, bytes_accessed=0, transcendentals=0),
    )(source)


def gather_sum_kernel(after, *refs):
    del after
    total = refs[0][...]
    for term in refs[1:-1]:
        total = total + term[...]
    refs[-1][...] = total


def gather_sum(after, terms):
    return pl.pallas_call(
        gather_sum_kernel,
        out_shape=jax.ShapeDtypeStruct(terms[0].shape, terms[0].dtype),
        in_specs=[spec(pl.ANY)] + [spec(pltpu.VMEM)] * len(terms),
        out_specs=spec(pltpu.VMEM),
        compiler_params=grant(4),
    )(after, *terms)


def project_kernel(query_out, query_act, out_basis, act_basis, total):
    half_ks = out_basis.shape[1]
    total[:, :half_ks] = jnp.dot(
        query_out[...], out_basis[...], preferred_element_type=jnp.float32
    )
    total[:, half_ks:] = jnp.dot(
        query_act[...], act_basis[...], preferred_element_type=jnp.float32
    )


def project(query_out, query_act, out_basis, act_basis):
    columns = query_out.shape[0]
    width = out_basis.shape[1] + act_basis.shape[1]
    operands = (query_out, query_act, out_basis, act_basis)
    return pl.pallas_call(
        project_kernel,
        out_shape=jax.ShapeDtypeStruct((columns, width), jnp.float32),
        in_specs=[spec(pltpu.VMEM)] * len(operands),
        out_specs=spec(pltpu.VMEM),
        compiler_params=grant(8),
        cost_estimate=pl.CostEstimate(
            flops=2 * columns * (out_basis.size + act_basis.size),
            bytes_accessed=2 * sum(x.size for x in operands),
            transcendentals=0,
        ),
    )(*operands)


def doubling_slot(distance, parts):
    bits = parts.bit_length() - 1
    return sum(1 << (bits - 1 - i) for i in range(bits) if distance >> i & 1)


def spread_kernel(place_ref, tokens_ref, ids_ref, after, total, first, second, *rest):
    del after
    pieces, joined = rest[:-1], rest[-1]
    each, local_rows, _ = pieces[0].shape
    parts = each * len(pieces)
    width = total.shape[1]
    row = lax.broadcasted_iota(jnp.int32, (local_rows, LANES), 0)
    lane = lax.broadcasted_iota(jnp.int32, (local_rows, LANES), 1)
    facts = jnp.where(lane < LANES // 2, ids_ref[0], tokens_ref[0]).astype(jnp.float32)
    for part in range(parts):
        start = pl.multiple_of((place_ref[0] ^ part) * local_rows, local_rows)
        piece = pieces[DIRECT_STEPS.index(part & DIRECT_STEPS[1])].at[int(part & LAST_STEP > 0)]
        piece[:, :width] = total[pl.ds(start, local_rows), :]
        piece[:, width:] = jnp.where(row == doubling_slot(part, parts), facts, 0.0)
    join_kernel(None, first, second, joined)


def spread(place, tokens, ids, after, total, first, second, parts):
    piece = jax.ShapeDtypeStruct(
        (parts // len(DIRECT_STEPS), total.shape[0] // parts, total.shape[1] + LANES), jnp.float32
    )
    joined = jax.ShapeDtypeStruct(
        (first.shape[0] + second.shape[0],) + first.shape[1:], first.dtype
    )
    return pl.pallas_call(
        spread_kernel,
        out_shape=[piece] * len(DIRECT_STEPS) + [joined],
        in_specs=[spec(pltpu.SMEM)] * 3 + [spec(pl.ANY)] + [spec(pltpu.VMEM)] * 3,
        out_specs=[spec(pltpu.VMEM)] * (len(DIRECT_STEPS) + 1),
        compiler_params=grant(4),
    )(place, tokens, ids, after, total, first, second)


def split_three(x):
    high = x.astype(jnp.bfloat16)
    rest = x - high.astype(jnp.float32)
    middle = rest.astype(jnp.bfloat16)
    low = (rest - middle.astype(jnp.float32)).astype(jnp.bfloat16)
    return high, middle, low


def score_kernel(core_ref, own, other, eigen, other_eigen, *rest):
    blocks, out = rest[:-1], rest[-1]
    first = core_ref[0] == 0
    half, ka = eigen.shape
    factor_rows, width = blocks[0].shape[1:]
    ks = width - ka
    shared = own.shape[1] - LANES
    mine, theirs = own[...], other[...]
    coords = (jnp.where(first, mine, theirs), jnp.where(first, theirs, mine))
    eigens = (
        jnp.where(first, eigen[...], other_eigen[...]),
        jnp.where(first, other_eigen[...], eigen[...]),
    )
    scales = [1.0 / (e + damping) for e in eigens]
    act = jnp.concatenate([v[:, half:shared] for v in coords], axis=1)
    act_terms = split_three(act)
    out_terms = [split_three(v[:, :half]) for v in coords]
    order = ((0, 0), (0, 1), (1, 0), (1, 1), (0, 2), (2, 0))
    slot = lax.broadcasted_iota(jnp.int32, (mine.shape[0], LANES), 0)
    even = (slot // 4 + slot // 2 + slot) % 2 == 0
    facts = (mine[:, shared:], theirs[:, shared:])
    facts = jnp.concatenate(
        [jnp.where(even, facts[0], facts[1]), jnp.where(even, facts[1], facts[0])], axis=0
    )
    rows = jnp.concatenate([x[...] for x in blocks], axis=0)
    examples = rows.shape[0]
    lane = lax.broadcasted_iota(jnp.int32, (examples, LANES), 1).astype(jnp.float32)
    row = lax.broadcasted_iota(jnp.int32, (examples, factor_rows, ka), 1).astype(jnp.float32)
    hot = lane == facts[:, :1]
    keep = row < facts[:, LANES // 2 : LANES // 2 + 1][:, :, None]
    weights = jnp.where(keep, rows[:, :, ks:].astype(jnp.float32), 0.0)
    flat = rows[:, :, :ks].reshape(examples * factor_rows, ks)
    for q in range(out.shape[0]):
        cut = slice(q * RQ, (q + 1) * RQ)
        right = jnp.concatenate([act_terms[b][cut] for _, b in order], axis=0)
        precond = []
        for part in range(2):
            left = jnp.concatenate([out_terms[part][a][cut] for a, _ in order], axis=0)
            numer = lax.dot_general(
                left, right, (((0,), (0,)), ((), ())), preferred_element_type=jnp.float32
            )
            precond.append((numer * scales[part]).astype(jnp.bfloat16))
        precond = jnp.concatenate(precond, axis=0)
        projected = jnp.dot(flat, precond, preferred_element_type=jnp.float32)
        terms = projected.reshape(examples, factor_rows, ka) * weights
        per_example = jnp.sum(jnp.sum(terms, axis=1), axis=1, keepdims=True)
        scores = jnp.sum(jnp.where(hot, per_example, 0.0), axis=0, keepdims=True)
        out[q : q + 1, :] = scores[:, : out.shape[1]]


def score(core, own, other, eigen, other_eigen, blocks):
    examples = sum(x.shape[0] for x in blocks)
    return pl.pallas_call(
        score_kernel,
        out_shape=jax.ShapeDtypeStruct((own.shape[0] // RQ, examples), jnp.float32),
        in_specs=[spec(pltpu.SMEM)] + [spec(pltpu.VMEM)] * (4 + len(blocks)),
        out_specs=spec(pltpu.VMEM),
        compiler_params=grant(12),
    )(core, own, other, eigen, other_eigen, *blocks)


def direct(
    query_out,
    query_act,
    out_basis,
    act_basis,
    eigenvalues,
    train_out,
    train_act,
    train_tokens,
    train_ids,
):
    parts = lax.axis_size("blk")
    steps = parts.bit_length() - 1
    swap = [(0, 1), (1, 0)]

    def apart(x, distance):
        return lax.ppermute(x, "blk", [(s, s ^ distance) for s in range(parts)])

    def crossed(x, i):
        pairs = [
            (2 * s + f, 2 * (s ^ (1 << i)) + 1 - f) for s in range(parts) for f in range(2)
        ]
        return lax.ppermute(x, ("blk", "fsdp"), pairs)

    place = lax.axis_index("blk").reshape(1)
    core = lax.axis_index("fsdp").reshape(1)
    other_eigen = lax.ppermute(eigenvalues, "fsdp", swap)
    block = relay(pack(train_out, train_act))
    arrived = crossed(block, 2)
    total = project(query_out.T, query_act.T, out_basis, act_basis)
    *pieces, block = spread(
        place, train_tokens, train_ids, other_eigen, total, block, arrived, parts
    )
    near = join(pieces[0], block, crossed(block, 1))
    terms = [apart(piece, step) for piece, step in zip(pieces[1:], DIRECT_STEPS[1:])]
    sums = gather_sum(near, [pieces[0]] + terms)
    far = crossed(near, 0)
    other_near = lax.ppermute(near, "fsdp", swap)
    other_far = lax.ppermute(far, "fsdp", swap)
    own = sums[0] + apart(sums[1], LAST_STEP)
    other = lax.ppermute(own, "fsdp", swap)
    return score(
        core, own, other, eigenvalues, other_eigen, (near, far, other_near, other_far)
    )


def score_block(precond, out_rows, act_rows, token_counts):
    factor_rows = out_rows.shape[1]
    valid = (
        lax.broadcasted_iota(jnp.int32, (out_rows.shape[0], factor_rows), 1) < token_counts[:, None]
    ).astype(jnp.float32)
    projected = jnp.einsum("nri,qij->nrqj", out_rows, precond, preferred_element_type=jnp.float32)
    weights = act_rows.astype(jnp.float32) * valid[:, :, None]
    return jnp.einsum("nrqj,nrj->qn", projected, weights, precision=lax.Precision.HIGHEST)


def gathered(
    query_out,
    query_act,
    out_basis,
    act_basis,
    eigenvalues,
    train_out,
    train_act,
    train_tokens,
    train_ids,
):
    half_ks = out_basis.shape[1]
    local_rows = query_out.shape[1] // lax.axis_size("blk")
    out_part = lax.dot_general(
        query_out, out_basis, (((0,), (0,)), ((), ())), preferred_element_type=jnp.float32
    )
    act_part = lax.dot_general(
        query_act, act_basis, (((0,), (0,)), ((), ())), preferred_element_type=jnp.float32
    )
    rotated = lax.psum_scatter(
        jnp.concatenate([out_part, act_part], axis=1), "blk", scatter_dimension=0, tiled=True
    )
    out_coords = rotated[:, :half_ks]
    act_half = rotated[:, half_ks:]
    act_coords = lax.all_gather(act_half, "fsdp", axis=1, tiled=True)
    queries = local_rows // RQ
    out_three = out_coords.reshape(queries, RQ, half_ks)
    act_three = act_coords.reshape(queries, RQ, act_coords.shape[1])
    numer = jnp.einsum("qri,qrj->qij", out_three, act_three, precision=lax.Precision.HIGHEST)
    precond = (numer / (eigenvalues + damping)).astype(jnp.bfloat16)
    train_total = train_out.shape[0] * lax.axis_size("blk") * lax.axis_size("fsdp")
    empty = jnp.zeros((queries, train_total), jnp.float32)
    full_precond = lax.all_gather(precond, "fsdp", axis=1, tiled=True)
    out_rows = lax.all_gather(train_out, "blk", axis=0, tiled=True)
    act_rows = lax.all_gather(train_act, "blk", axis=0, tiled=True)
    token_counts = lax.all_gather(train_tokens, "blk", axis=0, tiled=True)
    column_ids = lax.all_gather(train_ids, "blk", axis=0, tiled=True)
    scores = empty.at[:, column_ids].add(
        score_block(full_precond, out_rows, act_rows, token_counts)
    )
    return lax.psum(scores, "fsdp")


def solution(mesh):
    parts = mesh.shape["blk"]
    few = parts == DIRECT_PARTS and mesh.shape["fsdp"] == 2
    return jax.shard_map(
        direct if few else gathered,
        mesh=mesh,
        in_specs=(
            P("blk", None),
            P("blk", None),
            P("blk", "fsdp"),
            P("blk", "fsdp"),
            P("fsdp", None),
            P(("groups", "blk", "fsdp"), None, None),
            P(("groups", "blk", "fsdp"), None, None),
            P(("groups", "blk", "fsdp")),
            P(("groups", "blk", "fsdp")),
        ),
        out_specs=P("blk", "groups"),
        check_vma=False,
    )
```

```python
import functools

import jax
import jax.numpy as jnp
from jax import lax
from jax.experimental import pallas as pl
from jax.experimental.pallas import tpu as pltpu
from jax.sharding import PartitionSpec as P

RQ = 4
LANES = 128
DIRECT_PARTS = 8
WAIT_FLOPS = 10**9


damping = 0.1


def pinned(x):
    return pltpu.with_memory_space_constraint(x, pltpu.HBM)


def grant(mebibytes):
    return pltpu.CompilerParams(vmem_limit_bytes=mebibytes * 2**20)


def spec(space):
    return pl.BlockSpec(memory_space=space)


def pack_kernel(train_out, train_act, packed, sems):
    ks = train_out.shape[2]
    copies = (
        pltpu.make_async_copy(train_out, packed.at[:, :, :ks], sems.at[0]),
        pltpu.make_async_copy(train_act, packed.at[:, :, ks:], sems.at[1]),
    )
    for copy in copies:
        copy.start()
    for copy in copies:
        copy.wait()


def pack(train_out, train_act):
    examples, rows, ks = train_out.shape
    shape = (examples, rows, ks + train_act.shape[2])
    return pl.pallas_call(
        pack_kernel,
        out_shape=jax.ShapeDtypeStruct(shape, train_out.dtype),
        in_specs=[spec(pltpu.HBM)] * 2,
        out_specs=spec(pltpu.VMEM),
        scratch_shapes=[pltpu.SemaphoreType.DMA((2,))],
        compiler_params=grant(2),
    )(pinned(train_out), pinned(train_act))


def join_kernel(after, first, second, joined):
    del after
    count = first.shape[0]
    joined[:count] = first[...]
    joined[count:] = second[...]


def joined_shape(first, second):
    return jax.ShapeDtypeStruct(
        (first.shape[0] + second.shape[0],) + first.shape[1:], first.dtype
    )


def join(after, first, second):
    return pl.pallas_call(
        join_kernel,
        out_shape=joined_shape(first, second),
        in_specs=[spec(pl.ANY)] + [spec(pltpu.VMEM)] * 2,
        out_specs=spec(pltpu.VMEM),
        compiler_params=grant(4),
    )(after, first, second)


def relay_kernel(source, target):
    target[...] = source[...]


def relay(source):
    return pl.pallas_call(
        relay_kernel,
        out_shape=jax.ShapeDtypeStruct(source.shape, source.dtype),
        in_specs=[spec(pltpu.VMEM)],
        out_specs=spec(pltpu.VMEM),
        compiler_params=grant(2),
        cost_estimate=pl.CostEstimate(flops=WAIT_FLOPS, bytes_accessed=0, transcendentals=0),
    )(source)


def gather_sum_kernel(after, *refs):
    del after
    total = refs[0][...]
    for term in refs[1:-1]:
        total = total + term[...]
    refs[-1][...] = total


def gather_sum(after, terms):
    return pl.pallas_call(
        gather_sum_kernel,
        out_shape=jax.ShapeDtypeStruct(terms[0].shape, terms[0].dtype),
        in_specs=[spec(pl.ANY)] + [spec(pltpu.VMEM)] * len(terms),
        out_specs=spec(pltpu.VMEM),
        compiler_params=grant(4),
    )(after, *terms)


def project_kernel(query_out, query_act, out_basis, act_basis, total):
    half_ks = out_basis.shape[1]
    total[:, :half_ks] = jnp.dot(
        query_out[...], out_basis[...], preferred_element_type=jnp.float32
    )
    total[:, half_ks:] = jnp.dot(
        query_act[...], act_basis[...], preferred_element_type=jnp.float32
    )


def project(query_out, query_act, out_basis, act_basis):
    columns = query_out.shape[0]
    width = out_basis.shape[1] + act_basis.shape[1]
    operands = (query_out, query_act, out_basis, act_basis)
    return pl.pallas_call(
        project_kernel,
        out_shape=jax.ShapeDtypeStruct((columns, width), jnp.float32),
        in_specs=[spec(pltpu.VMEM)] * len(operands),
        out_specs=spec(pltpu.VMEM),
        compiler_params=grant(8),
        cost_estimate=pl.CostEstimate(
            flops=2 * columns * (out_basis.size + act_basis.size),
            bytes_accessed=2 * sum(x.size for x in operands),
            transcendentals=0,
        ),
    )(*operands)


def doubling_slot(distance, parts):
    return distance // 2 + distance % 2 * (parts // 2)


def spread_kernel(place_ref, tokens_ref, ids_ref, after, total, first, second, *rest):
    del after
    pieces, joined = rest[:-1], rest[-1]
    groups = len(pieces)
    each, local_rows, _ = pieces[0].shape
    parts = groups * each
    width = total.shape[1]
    row = lax.broadcasted_iota(jnp.int32, (local_rows, LANES), 0)
    lane = lax.broadcasted_iota(jnp.int32, (local_rows, LANES), 1)
    facts = jnp.where(lane < LANES // 2, ids_ref[0], tokens_ref[0]).astype(jnp.float32)
    for part in range(parts):
        start = pl.multiple_of((place_ref[0] ^ part) * local_rows, local_rows)
        piece = pieces[part % groups].at[part // groups]
        piece[:, :width] = total[pl.ds(start, local_rows), :]
        piece[:, width:] = jnp.where(row == doubling_slot(part, parts), facts, 0.0)
    join_kernel(None, first, second, joined)


def spread(place, tokens, ids, after, total, first, second, parts, groups):
    piece = jax.ShapeDtypeStruct(
        (parts // groups, total.shape[0] // parts, total.shape[1] + LANES), jnp.float32
    )
    joined = jax.ShapeDtypeStruct(
        (first.shape[0] + second.shape[0],) + first.shape[1:], first.dtype
    )
    return pl.pallas_call(
        spread_kernel,
        out_shape=[piece] * groups + [joined],
        in_specs=[spec(pltpu.SMEM)] * 3 + [spec(pl.ANY)] + [spec(pltpu.VMEM)] * 3,
        out_specs=[spec(pltpu.VMEM)] * (groups + 1),
        compiler_params=grant(4),
    )(place, tokens, ids, after, total, first, second)


def split_three(x):
    high = x.astype(jnp.bfloat16)
    rest = x - high.astype(jnp.float32)
    middle = rest.astype(jnp.bfloat16)
    low = (rest - middle.astype(jnp.float32)).astype(jnp.bfloat16)
    return high, middle, low


def score_kernel(core_ref, own, other, eigen, other_eigen, *rest):
    blocks, out = rest[:-1], rest[-1]
    first = core_ref[0] == 0
    half, ka = eigen.shape
    factor_rows, width = blocks[0].shape[1:]
    ks = width - ka
    shared = own.shape[1] - LANES
    mine, theirs = own[...], other[...]
    coords = (jnp.where(first, mine, theirs), jnp.where(first, theirs, mine))
    eigens = (
        jnp.where(first, eigen[...], other_eigen[...]),
        jnp.where(first, other_eigen[...], eigen[...]),
    )
    scales = [1.0 / (e + damping) for e in eigens]
    act = jnp.concatenate([v[:, half:shared] for v in coords], axis=1)
    act_terms = split_three(act)
    out_terms = [split_three(v[:, :half]) for v in coords]
    order = ((0, 0), (0, 1), (1, 0), (1, 1), (0, 2), (2, 0))
    slot = lax.broadcasted_iota(jnp.int32, (mine.shape[0], LANES), 0)
    even = (slot // 4 + slot // 2 + slot) % 2 == 0
    facts = (mine[:, shared:], theirs[:, shared:])
    facts = jnp.concatenate(
        [jnp.where(even, facts[0], facts[1]), jnp.where(even, facts[1], facts[0])], axis=0
    )
    rows = jnp.concatenate([x[...] for x in blocks], axis=0)
    examples = rows.shape[0]
    lane = lax.broadcasted_iota(jnp.int32, (examples, LANES), 1).astype(jnp.float32)
    row = lax.broadcasted_iota(jnp.int32, (examples, factor_rows, ka), 1).astype(jnp.float32)
    hot = lane == facts[:, :1]
    keep = row < facts[:, LANES // 2 : LANES // 2 + 1][:, :, None]
    weights = jnp.where(keep, rows[:, :, ks:].astype(jnp.float32), 0.0)
    flat = rows[:, :, :ks].reshape(examples * factor_rows, ks)
    for q in range(out.shape[0]):
        cut = slice(q * RQ, (q + 1) * RQ)
        right = jnp.concatenate([act_terms[b][cut] for _, b in order], axis=0)
        precond = []
        for part in range(2):
            left = jnp.concatenate([out_terms[part][a][cut] for a, _ in order], axis=0)
            numer = lax.dot_general(
                left, right, (((0,), (0,)), ((), ())), preferred_element_type=jnp.float32
            )
            precond.append((numer * scales[part]).astype(jnp.bfloat16))
        precond = jnp.concatenate(precond, axis=0)
        projected = jnp.dot(flat, precond, preferred_element_type=jnp.float32)
        terms = projected.reshape(examples, factor_rows, ka) * weights
        per_example = jnp.sum(jnp.sum(terms, axis=1), axis=1, keepdims=True)
        scores = jnp.sum(jnp.where(hot, per_example, 0.0), axis=0, keepdims=True)
        out[q : q + 1, :] = scores[:, : out.shape[1]]


def score(core, own, other, eigen, other_eigen, blocks):
    examples = sum(x.shape[0] for x in blocks)
    return pl.pallas_call(
        score_kernel,
        out_shape=jax.ShapeDtypeStruct((own.shape[0] // RQ, examples), jnp.float32),
        in_specs=[spec(pltpu.SMEM)] + [spec(pltpu.VMEM)] * (4 + len(blocks)),
        out_specs=spec(pltpu.VMEM),
        compiler_params=grant(12),
    )(core, own, other, eigen, other_eigen, *blocks)


def direct(
    query_out,
    query_act,
    out_basis,
    act_basis,
    eigenvalues,
    train_out,
    train_act,
    train_tokens,
    train_ids,
):
    parts = lax.axis_size("blk")
    steps = parts.bit_length() - 1
    swap = [(0, 1), (1, 0)]

    def apart(x, distance):
        return lax.ppermute(x, "blk", [(s, s ^ distance) for s in range(parts)])

    def crossed(x, i):
        pairs = [
            (2 * s + f, 2 * (s ^ (1 << i)) + 1 - f) for s in range(parts) for f in range(2)
        ]
        return lax.ppermute(x, ("blk", "fsdp"), pairs)

    place = lax.axis_index("blk").reshape(1)
    core = lax.axis_index("fsdp").reshape(1)
    other_eigen = lax.ppermute(eigenvalues, "fsdp", swap)
    block = relay(pack(train_out, train_act))
    arrived = crossed(block, 1)
    total = project(query_out.T, query_act.T, out_basis, act_basis)
    *pieces, block = spread(
        place, train_tokens, train_ids, other_eigen, total, block, arrived, parts, parts // 2
    )
    near = join(pieces[0], block, crossed(block, 2))
    far_first = reversed(range(1, len(pieces)))
    terms = [pieces[0]] + [apart(pieces[d], d) for d in far_first]
    sums = gather_sum(near, terms)
    far = crossed(near, 0)
    other_near = lax.ppermute(near, "fsdp", swap)
    other_far = lax.ppermute(far, "fsdp", swap)
    own = sums[0] + apart(sums[1], 4)
    other = lax.ppermute(own, "fsdp", swap)
    return score(
        core, own, other, eigenvalues, other_eigen, (near, far, other_near, other_far)
    )


def score_block(precond, out_rows, act_rows, token_counts):
    factor_rows = out_rows.shape[1]
    valid = (
        lax.broadcasted_iota(jnp.int32, (out_rows.shape[0], factor_rows), 1) < token_counts[:, None]
    ).astype(jnp.float32)
    projected = jnp.einsum("nri,qij->nrqj", out_rows, precond, preferred_element_type=jnp.float32)
    weights = act_rows.astype(jnp.float32) * valid[:, :, None]
    return jnp.einsum("nrqj,nrj->qn", projected, weights, precision=lax.Precision.HIGHEST)


def gathered(
    query_out,
    query_act,
    out_basis,
    act_basis,
    eigenvalues,
    train_out,
    train_act,
    train_tokens,
    train_ids,
):
    half_ks = out_basis.shape[1]
    local_rows = query_out.shape[1] // lax.axis_size("blk")
    out_part = lax.dot_general(
        query_out, out_basis, (((0,), (0,)), ((), ())), preferred_element_type=jnp.float32
    )
    act_part = lax.dot_general(
        query_act, act_basis, (((0,), (0,)), ((), ())), preferred_element_type=jnp.float32
    )
    rotated = lax.psum_scatter(
        jnp.concatenate([out_part, act_part], axis=1), "blk", scatter_dimension=0, tiled=True
    )
    out_coords = rotated[:, :half_ks]
    act_half = rotated[:, half_ks:]
    act_coords = lax.all_gather(act_half, "fsdp", axis=1, tiled=True)
    queries = local_rows // RQ
    out_three = out_coords.reshape(queries, RQ, half_ks)
    act_three = act_coords.reshape(queries, RQ, act_coords.shape[1])
    numer = jnp.einsum("qri,qrj->qij", out_three, act_three, precision=lax.Precision.HIGHEST)
    precond = (numer / (eigenvalues + damping)).astype(jnp.bfloat16)
    train_total = train_out.shape[0] * lax.axis_size("blk") * lax.axis_size("fsdp")
    empty = jnp.zeros((queries, train_total), jnp.float32)
    full_precond = lax.all_gather(precond, "fsdp", axis=1, tiled=True)
    out_rows = lax.all_gather(train_out, "blk", axis=0, tiled=True)
    act_rows = lax.all_gather(train_act, "blk", axis=0, tiled=True)
    token_counts = lax.all_gather(train_tokens, "blk", axis=0, tiled=True)
    column_ids = lax.all_gather(train_ids, "blk", axis=0, tiled=True)
    scores = empty.at[:, column_ids].add(
        score_block(full_precond, out_rows, act_rows, token_counts)
    )
    return lax.psum(scores, "fsdp")


def solution(mesh):
    parts = mesh.shape["blk"]
    few = parts == DIRECT_PARTS and mesh.shape["fsdp"] == 2
    return jax.shard_map(
        direct if few else gathered,
        mesh=mesh,
        in_specs=(
            P("blk", None),
            P("blk", None),
            P("blk", "fsdp"),
            P("blk", "fsdp"),
            P("fsdp", None),
            P(("groups", "blk", "fsdp"), None, None),
            P(("groups", "blk", "fsdp"), None, None),
            P(("groups", "blk", "fsdp")),
            P(("groups", "blk", "fsdp")),
        ),
        out_specs=P("blk", "groups"),
        check_vma=False,
    )
```

```python
import functools

import jax
import jax.numpy as jnp
from jax import lax
from jax.experimental import pallas as pl
from jax.experimental.pallas import tpu as pltpu
from jax.sharding import PartitionSpec as P

RQ = 4
LANES = 128
DIRECT_PARTS = 8
WAIT_FLOPS = 10**9


damping = 0.1


def pinned(x):
    return pltpu.with_memory_space_constraint(x, pltpu.HBM)


def grant(mebibytes):
    return pltpu.CompilerParams(vmem_limit_bytes=mebibytes * 2**20)


def spec(space):
    return pl.BlockSpec(memory_space=space)


def pack_kernel(train_out, train_act, packed, sems):
    ks = train_out.shape[2]
    copies = (
        pltpu.make_async_copy(train_out, packed.at[:, :, :ks], sems.at[0]),
        pltpu.make_async_copy(train_act, packed.at[:, :, ks:], sems.at[1]),
    )
    for copy in copies:
        copy.start()
    for copy in copies:
        copy.wait()


def pack(train_out, train_act):
    examples, rows, ks = train_out.shape
    shape = (examples, rows, ks + train_act.shape[2])
    return pl.pallas_call(
        pack_kernel,
        out_shape=jax.ShapeDtypeStruct(shape, train_out.dtype),
        in_specs=[spec(pltpu.HBM)] * 2,
        out_specs=spec(pltpu.VMEM),
        scratch_shapes=[pltpu.SemaphoreType.DMA((2,))],
        compiler_params=grant(2),
    )(pinned(train_out), pinned(train_act))


def join_kernel(after, first, second, joined):
    del after
    count = first.shape[0]
    joined[:count] = first[...]
    joined[count:] = second[...]


def joined_shape(first, second):
    return jax.ShapeDtypeStruct(
        (first.shape[0] + second.shape[0],) + first.shape[1:], first.dtype
    )


def join(after, first, second):
    return pl.pallas_call(
        join_kernel,
        out_shape=joined_shape(first, second),
        in_specs=[spec(pl.ANY)] + [spec(pltpu.VMEM)] * 2,
        out_specs=spec(pltpu.VMEM),
        compiler_params=grant(4),
    )(after, first, second)


def relay_kernel(source, target):
    target[...] = source[...]


def relay(source):
    return pl.pallas_call(
        relay_kernel,
        out_shape=jax.ShapeDtypeStruct(source.shape, source.dtype),
        in_specs=[spec(pltpu.VMEM)],
        out_specs=spec(pltpu.VMEM),
        compiler_params=grant(2),
        cost_estimate=pl.CostEstimate(flops=WAIT_FLOPS, bytes_accessed=0, transcendentals=0),
    )(source)


def gather_sum_kernel(after, *refs):
    del after
    total = refs[0][...]
    for term in refs[1:-1]:
        total = total + term[...]
    refs[-1][...] = total


def gather_sum(after, terms):
    return pl.pallas_call(
        gather_sum_kernel,
        out_shape=jax.ShapeDtypeStruct(terms[0].shape, terms[0].dtype),
        in_specs=[spec(pl.ANY)] + [spec(pltpu.VMEM)] * len(terms),
        out_specs=spec(pltpu.VMEM),
        compiler_params=grant(4),
    )(after, *terms)


def hold_kernel(after, source, target):
    del after
    target[...] = source[...]


def hold(after, source):
    return pl.pallas_call(
        hold_kernel,
        out_shape=jax.ShapeDtypeStruct(source.shape, source.dtype),
        in_specs=[spec(pl.ANY), spec(pltpu.VMEM)],
        out_specs=spec(pltpu.VMEM),
        compiler_params=grant(2),
    )(after, source)


def project_kernel(query_out, query_act, out_basis, act_basis, total):
    half_ks = out_basis.shape[1]
    total[:, :half_ks] = jnp.dot(
        query_out[...], out_basis[...], preferred_element_type=jnp.float32
    )
    total[:, half_ks:] = jnp.dot(
        query_act[...], act_basis[...], preferred_element_type=jnp.float32
    )


def project(query_out, query_act, out_basis, act_basis):
    columns = query_out.shape[0]
    width = out_basis.shape[1] + act_basis.shape[1]
    operands = (query_out, query_act, out_basis, act_basis)
    return pl.pallas_call(
        project_kernel,
        out_shape=jax.ShapeDtypeStruct((columns, width), jnp.float32),
        in_specs=[spec(pltpu.VMEM)] * len(operands),
        out_specs=spec(pltpu.VMEM),
        compiler_params=grant(8),
        cost_estimate=pl.CostEstimate(
            flops=2 * columns * (out_basis.size + act_basis.size),
            bytes_accessed=2 * sum(x.size for x in operands),
            transcendentals=0,
        ),
    )(*operands)


def doubling_slot(distance, parts):
    bits = parts.bit_length() - 1
    return sum(1 << (bits - 1 - i) for i in range(bits) if distance >> i & 1)


def spread_kernel(place_ref, tokens_ref, ids_ref, total, first, second, *rest):
    pieces, joined = rest[:-1], rest[-1]
    groups = len(pieces)
    each, local_rows, _ = pieces[0].shape
    parts = groups * each
    width = total.shape[1]
    row = lax.broadcasted_iota(jnp.int32, (local_rows, LANES), 0)
    lane = lax.broadcasted_iota(jnp.int32, (local_rows, LANES), 1)
    facts = jnp.where(lane < LANES // 2, ids_ref[0], tokens_ref[0]).astype(jnp.float32)
    for part in range(parts):
        start = pl.multiple_of((place_ref[0] ^ part) * local_rows, local_rows)
        piece = pieces[part % groups].at[part // groups]
        piece[:, :width] = total[pl.ds(start, local_rows), :]
        piece[:, width:] = jnp.where(row == doubling_slot(part, parts), facts, 0.0)
    join_kernel(None, first, second, joined)


def spread(place, tokens, ids, total, first, second, parts, groups):
    piece = jax.ShapeDtypeStruct(
        (parts // groups, total.shape[0] // parts, total.shape[1] + LANES), jnp.float32
    )
    joined = jax.ShapeDtypeStruct(
        (first.shape[0] + second.shape[0],) + first.shape[1:], first.dtype
    )
    return pl.pallas_call(
        spread_kernel,
        out_shape=[piece] * groups + [joined],
        in_specs=[spec(pltpu.SMEM)] * 3 + [spec(pltpu.VMEM)] * 3,
        out_specs=[spec(pltpu.VMEM)] * (groups + 1),
        compiler_params=grant(4),
    )(place, tokens, ids, total, first, second)


def split_three(x):
    high = x.astype(jnp.bfloat16)
    rest = x - high.astype(jnp.float32)
    middle = rest.astype(jnp.bfloat16)
    low = (rest - middle.astype(jnp.float32)).astype(jnp.bfloat16)
    return high, middle, low


def score_kernel(core_ref, own, other, eigen, other_eigen, *rest):
    blocks, out = rest[:-1], rest[-1]
    first = core_ref[0] == 0
    half, ka = eigen.shape
    factor_rows, width = blocks[0].shape[1:]
    ks = width - ka
    shared = own.shape[1] - LANES
    mine, theirs = own[...], other[...]
    coords = (jnp.where(first, mine, theirs), jnp.where(first, theirs, mine))
    eigens = (
        jnp.where(first, eigen[...], other_eigen[...]),
        jnp.where(first, other_eigen[...], eigen[...]),
    )
    scales = [1.0 / (e + damping) for e in eigens]
    act = jnp.concatenate([v[:, half:shared] for v in coords], axis=1)
    act_terms = split_three(act)
    out_terms = [split_three(v[:, :half]) for v in coords]
    order = ((0, 0), (0, 1), (1, 0), (1, 1), (0, 2), (2, 0))
    slot = lax.broadcasted_iota(jnp.int32, (mine.shape[0], LANES), 0)
    even = (slot // 4 + slot // 2 + slot) % 2 == 0
    facts = (mine[:, shared:], theirs[:, shared:])
    facts = jnp.concatenate(
        [jnp.where(even, facts[0], facts[1]), jnp.where(even, facts[1], facts[0])], axis=0
    )
    rows = jnp.concatenate([x[...] for x in blocks], axis=0)
    examples = rows.shape[0]
    lane = lax.broadcasted_iota(jnp.int32, (examples, LANES), 1).astype(jnp.float32)
    row = lax.broadcasted_iota(jnp.int32, (examples, factor_rows, ka), 1).astype(jnp.float32)
    hot = lane == facts[:, :1]
    keep = row < facts[:, LANES // 2 : LANES // 2 + 1][:, :, None]
    weights = jnp.where(keep, rows[:, :, ks:].astype(jnp.float32), 0.0)
    flat = rows[:, :, :ks].reshape(examples * factor_rows, ks)
    for q in range(out.shape[0]):
        cut = slice(q * RQ, (q + 1) * RQ)
        right = jnp.concatenate([act_terms[b][cut] for _, b in order], axis=0)
        precond = []
        for part in range(2):
            left = jnp.concatenate([out_terms[part][a][cut] for a, _ in order], axis=0)
            numer = lax.dot_general(
                left, right, (((0,), (0,)), ((), ())), preferred_element_type=jnp.float32
            )
            precond.append((numer * scales[part]).astype(jnp.bfloat16))
        precond = jnp.concatenate(precond, axis=0)
        projected = jnp.dot(flat, precond, preferred_element_type=jnp.float32)
        terms = projected.reshape(examples, factor_rows, ka) * weights
        per_example = jnp.sum(jnp.sum(terms, axis=1), axis=1, keepdims=True)
        scores = jnp.sum(jnp.where(hot, per_example, 0.0), axis=0, keepdims=True)
        out[q : q + 1, :] = scores[:, : out.shape[1]]


def score(core, own, other, eigen, other_eigen, blocks):
    examples = sum(x.shape[0] for x in blocks)
    return pl.pallas_call(
        score_kernel,
        out_shape=jax.ShapeDtypeStruct((own.shape[0] // RQ, examples), jnp.float32),
        in_specs=[spec(pltpu.SMEM)] + [spec(pltpu.VMEM)] * (4 + len(blocks)),
        out_specs=spec(pltpu.VMEM),
        compiler_params=grant(12),
    )(core, own, other, eigen, other_eigen, *blocks)


def direct(
    query_out,
    query_act,
    out_basis,
    act_basis,
    eigenvalues,
    train_out,
    train_act,
    train_tokens,
    train_ids,
):
    parts = lax.axis_size("blk")
    steps = parts.bit_length() - 1
    swap = [(0, 1), (1, 0)]

    def apart(x, distance):
        return lax.ppermute(x, "blk", [(s, s ^ distance) for s in range(parts)])

    def crossed(x, i):
        pairs = [
            (2 * s + f, 2 * (s ^ (1 << i)) + 1 - f) for s in range(parts) for f in range(2)
        ]
        return lax.ppermute(x, ("blk", "fsdp"), pairs)

    place = lax.axis_index("blk").reshape(1)
    core = lax.axis_index("fsdp").reshape(1)
    block = relay(pack(train_out, train_act))
    arrived = crossed(block, 2)
    total = project(query_out.T, query_act.T, out_basis, act_basis)
    *pieces, block = spread(
        place, train_tokens, train_ids, total, block, arrived, parts, parts // 2
    )
    near = join(pieces[0], block, crossed(block, 1))
    far_first = reversed(range(1, len(pieces)))
    terms = [pieces[0]] + [apart(pieces[d], d) for d in far_first]
    sums = gather_sum(near, terms)
    far = crossed(near, 0)
    other_eigen = lax.ppermute(hold(near, eigenvalues), "fsdp", swap)
    other_near = lax.ppermute(near, "fsdp", swap)
    other_far = lax.ppermute(far, "fsdp", swap)
    own = sums[0] + apart(sums[1], 4)
    other = lax.ppermute(own, "fsdp", swap)
    return score(
        core, own, other, eigenvalues, other_eigen, (near, far, other_near, other_far)
    )


def score_block(precond, out_rows, act_rows, token_counts):
    factor_rows = out_rows.shape[1]
    valid = (
        lax.broadcasted_iota(jnp.int32, (out_rows.shape[0], factor_rows), 1) < token_counts[:, None]
    ).astype(jnp.float32)
    projected = jnp.einsum("nri,qij->nrqj", out_rows, precond, preferred_element_type=jnp.float32)
    weights = act_rows.astype(jnp.float32) * valid[:, :, None]
    return jnp.einsum("nrqj,nrj->qn", projected, weights, precision=lax.Precision.HIGHEST)


def gathered(
    query_out,
    query_act,
    out_basis,
    act_basis,
    eigenvalues,
    train_out,
    train_act,
    train_tokens,
    train_ids,
):
    half_ks = out_basis.shape[1]
    local_rows = query_out.shape[1] // lax.axis_size("blk")
    out_part = lax.dot_general(
        query_out, out_basis, (((0,), (0,)), ((), ())), preferred_element_type=jnp.float32
    )
    act_part = lax.dot_general(
        query_act, act_basis, (((0,), (0,)), ((), ())), preferred_element_type=jnp.float32
    )
    rotated = lax.psum_scatter(
        jnp.concatenate([out_part, act_part], axis=1), "blk", scatter_dimension=0, tiled=True
    )
    out_coords = rotated[:, :half_ks]
    act_half = rotated[:, half_ks:]
    act_coords = lax.all_gather(act_half, "fsdp", axis=1, tiled=True)
    queries = local_rows // RQ
    out_three = out_coords.reshape(queries, RQ, half_ks)
    act_three = act_coords.reshape(queries, RQ, act_coords.shape[1])
    numer = jnp.einsum("qri,qrj->qij", out_three, act_three, precision=lax.Precision.HIGHEST)
    precond = (numer / (eigenvalues + damping)).astype(jnp.bfloat16)
    train_total = train_out.shape[0] * lax.axis_size("blk") * lax.axis_size("fsdp")
    empty = jnp.zeros((queries, train_total), jnp.float32)
    full_precond = lax.all_gather(precond, "fsdp", axis=1, tiled=True)
    out_rows = lax.all_gather(train_out, "blk", axis=0, tiled=True)
    act_rows = lax.all_gather(train_act, "blk", axis=0, tiled=True)
    token_counts = lax.all_gather(train_tokens, "blk", axis=0, tiled=True)
    column_ids = lax.all_gather(train_ids, "blk", axis=0, tiled=True)
    scores = empty.at[:, column_ids].add(
        score_block(full_precond, out_rows, act_rows, token_counts)
    )
    return lax.psum(scores, "fsdp")


def solution(mesh):
    parts = mesh.shape["blk"]
    few = parts == DIRECT_PARTS and mesh.shape["fsdp"] == 2
    return jax.shard_map(
        direct if few else gathered,
        mesh=mesh,
        in_specs=(
            P("blk", None),
            P("blk", None),
            P("blk", "fsdp"),
            P("blk", "fsdp"),
            P("fsdp", None),
            P(("groups", "blk", "fsdp"), None, None),
            P(("groups", "blk", "fsdp"), None, None),
            P(("groups", "blk", "fsdp")),
            P(("groups", "blk", "fsdp")),
        ),
        out_specs=P("blk", "groups"),
        check_vma=False,
    )
```

```python
import functools

import jax
import jax.numpy as jnp
from jax import lax
from jax.experimental import pallas as pl
from jax.experimental.pallas import tpu as pltpu
from jax.sharding import PartitionSpec as P

RQ = 4
LANES = 128
DIRECT_PARTS = 8
WAIT_FLOPS = 10**9


damping = 0.1


def pinned(x):
    return pltpu.with_memory_space_constraint(x, pltpu.HBM)


def grant(mebibytes):
    return pltpu.CompilerParams(vmem_limit_bytes=mebibytes * 2**20)


def spec(space):
    return pl.BlockSpec(memory_space=space)


def pack_kernel(train_out, train_act, packed, sems):
    ks = train_out.shape[2]
    copies = (
        pltpu.make_async_copy(train_out, packed.at[:, :, :ks], sems.at[0]),
        pltpu.make_async_copy(train_act, packed.at[:, :, ks:], sems.at[1]),
    )
    for copy in copies:
        copy.start()
    for copy in copies:
        copy.wait()


def pack(train_out, train_act):
    examples, rows, ks = train_out.shape
    shape = (examples, rows, ks + train_act.shape[2])
    return pl.pallas_call(
        pack_kernel,
        out_shape=jax.ShapeDtypeStruct(shape, train_out.dtype),
        in_specs=[spec(pltpu.HBM)] * 2,
        out_specs=spec(pltpu.VMEM),
        scratch_shapes=[pltpu.SemaphoreType.DMA((2,))],
        compiler_params=grant(2),
    )(pinned(train_out), pinned(train_act))


def join_kernel(after, first, second, joined):
    del after
    count = first.shape[0]
    joined[:count] = first[...]
    joined[count:] = second[...]


def joined_shape(first, second):
    return jax.ShapeDtypeStruct(
        (first.shape[0] + second.shape[0],) + first.shape[1:], first.dtype
    )


def join(after, first, second):
    return pl.pallas_call(
        join_kernel,
        out_shape=joined_shape(first, second),
        in_specs=[spec(pl.ANY)] + [spec(pltpu.VMEM)] * 2,
        out_specs=spec(pltpu.VMEM),
        compiler_params=grant(4),
    )(after, first, second)


def relay_kernel(source, target):
    target[...] = source[...]


def relay(source):
    return pl.pallas_call(
        relay_kernel,
        out_shape=jax.ShapeDtypeStruct(source.shape, source.dtype),
        in_specs=[spec(pltpu.VMEM)],
        out_specs=spec(pltpu.VMEM),
        compiler_params=grant(2),
        cost_estimate=pl.CostEstimate(flops=WAIT_FLOPS, bytes_accessed=0, transcendentals=0),
    )(source)


def gather_sum_kernel(after, *refs):
    del after
    total = refs[0][...]
    for term in refs[1:-1]:
        total = total + term[...]
    refs[-1][...] = total


def gather_sum(after, terms):
    return pl.pallas_call(
        gather_sum_kernel,
        out_shape=jax.ShapeDtypeStruct(terms[0].shape, terms[0].dtype),
        in_specs=[spec(pl.ANY)] + [spec(pltpu.VMEM)] * len(terms),
        out_specs=spec(pltpu.VMEM),
        compiler_params=grant(4),
    )(after, *terms)


def hold_kernel(after, source, target):
    del after
    target[...] = source[...]


def hold(after, source):
    return pl.pallas_call(
        hold_kernel,
        out_shape=jax.ShapeDtypeStruct(source.shape, source.dtype),
        in_specs=[spec(pl.ANY), spec(pltpu.VMEM)],
        out_specs=spec(pltpu.VMEM),
        compiler_params=grant(2),
    )(after, source)


def project_kernel(query_out, query_act, out_basis, act_basis, total):
    half_ks = out_basis.shape[1]
    total[:, :half_ks] = jnp.dot(
        query_out[...], out_basis[...], preferred_element_type=jnp.float32
    )
    total[:, half_ks:] = jnp.dot(
        query_act[...], act_basis[...], preferred_element_type=jnp.float32
    )


def project(query_out, query_act, out_basis, act_basis):
    columns = query_out.shape[0]
    width = out_basis.shape[1] + act_basis.shape[1]
    operands = (query_out, query_act, out_basis, act_basis)
    return pl.pallas_call(
        project_kernel,
        out_shape=jax.ShapeDtypeStruct((columns, width), jnp.float32),
        in_specs=[spec(pltpu.VMEM)] * len(operands),
        out_specs=spec(pltpu.VMEM),
        compiler_params=grant(8),
        cost_estimate=pl.CostEstimate(
            flops=2 * columns * (out_basis.size + act_basis.size),
            bytes_accessed=2 * sum(x.size for x in operands),
            transcendentals=0,
        ),
    )(*operands)


def doubling_slot(distance, parts):
    bits = parts.bit_length() - 1
    return sum(1 << (bits - 1 - i) for i in range(bits) if distance >> i & 1)


def spread_kernel(place_ref, tokens_ref, ids_ref, total, first, second, *rest):
    pieces, halves = rest[:-2], rest[-2:]
    groups = len(pieces)
    each, local_rows, _ = pieces[0].shape
    parts = groups * each
    width = total.shape[1]
    row = lax.broadcasted_iota(jnp.int32, (local_rows, LANES), 0)
    lane = lax.broadcasted_iota(jnp.int32, (local_rows, LANES), 1)
    facts = jnp.where(lane < LANES // 2, ids_ref[0], tokens_ref[0]).astype(jnp.float32)
    for part in range(parts):
        start = pl.multiple_of((place_ref[0] ^ part) * local_rows, local_rows)
        piece = pieces[part % groups].at[part // groups]
        piece[:, :width] = total[pl.ds(start, local_rows), :]
        piece[:, width:] = jnp.where(row == doubling_slot(part, parts), facts, 0.0)
    count, lanes = first.shape[0], halves[0].shape[2]
    for i, joined in enumerate(halves):
        joined[:count] = first[:, :, i * lanes : (i + 1) * lanes]
        joined[count:] = second[:, :, i * lanes : (i + 1) * lanes]


def spread(place, tokens, ids, total, first, second, parts, groups):
    piece = jax.ShapeDtypeStruct(
        (parts // groups, total.shape[0] // parts, total.shape[1] + LANES), jnp.float32
    )
    joined = jax.ShapeDtypeStruct(
        (first.shape[0] + second.shape[0], first.shape[1], first.shape[2] // 2), first.dtype
    )
    return pl.pallas_call(
        spread_kernel,
        out_shape=[piece] * groups + [joined] * 2,
        in_specs=[spec(pltpu.SMEM)] * 3 + [spec(pltpu.VMEM)] * 3,
        out_specs=[spec(pltpu.VMEM)] * (groups + 2),
        compiler_params=grant(4),
    )(place, tokens, ids, total, first, second)


def split_three(x):
    high = x.astype(jnp.bfloat16)
    rest = x - high.astype(jnp.float32)
    middle = rest.astype(jnp.bfloat16)
    low = (rest - middle.astype(jnp.float32)).astype(jnp.bfloat16)
    return high, middle, low


def score_kernel(core_ref, own, other, eigen, other_eigen, *rest):
    blocks, out = rest[:-1], rest[-1]
    first = core_ref[0] == 0
    half, ka = eigen.shape
    factor_rows, lanes = blocks[0].shape[1:]
    ks = 2 * lanes - ka
    shared = own.shape[1] - LANES
    mine, theirs = own[...], other[...]
    coords = (jnp.where(first, mine, theirs), jnp.where(first, theirs, mine))
    eigens = (
        jnp.where(first, eigen[...], other_eigen[...]),
        jnp.where(first, other_eigen[...], eigen[...]),
    )
    scales = [1.0 / (e + damping) for e in eigens]
    act = jnp.concatenate([v[:, half:shared] for v in coords], axis=1)
    act_terms = split_three(act)
    out_terms = [split_three(v[:, :half]) for v in coords]
    order = ((0, 0), (0, 1), (1, 0), (1, 1), (0, 2), (2, 0))
    slot = lax.broadcasted_iota(jnp.int32, (mine.shape[0], LANES), 0)
    even = (slot // 4 + slot // 2 + slot) % 2 == 0
    facts = (mine[:, shared:], theirs[:, shared:])
    facts = jnp.concatenate(
        [jnp.where(even, facts[0], facts[1]), jnp.where(even, facts[1], facts[0])], axis=0
    )
    each = blocks[0].shape[0] // 2
    lefts, rights = [], []
    for near, far in (blocks[:2], blocks[2:]):
        lefts += [near[:each], far[:each]]
        for cut in (slice(each, each + each // 2), slice(each + each // 2, 2 * each)):
            rights += [near[cut], far[cut]]
    halves = [jnp.concatenate(x, axis=0) for x in (lefts, rights)]
    rows = jnp.concatenate(halves, axis=2)
    examples = rows.shape[0]
    lane = lax.broadcasted_iota(jnp.int32, (examples, LANES), 1).astype(jnp.float32)
    row = lax.broadcasted_iota(jnp.int32, (examples, factor_rows, ka), 1).astype(jnp.float32)
    hot = lane == facts[:, :1]
    keep = row < facts[:, LANES // 2 : LANES // 2 + 1][:, :, None]
    weights = jnp.where(keep, rows[:, :, ks:].astype(jnp.float32), 0.0)
    flat = rows[:, :, :ks].reshape(examples * factor_rows, ks)
    for q in range(out.shape[0]):
        cut = slice(q * RQ, (q + 1) * RQ)
        right = jnp.concatenate([act_terms[b][cut] for _, b in order], axis=0)
        precond = []
        for part in range(2):
            left = jnp.concatenate([out_terms[part][a][cut] for a, _ in order], axis=0)
            numer = lax.dot_general(
                left, right, (((0,), (0,)), ((), ())), preferred_element_type=jnp.float32
            )
            precond.append((numer * scales[part]).astype(jnp.bfloat16))
        precond = jnp.concatenate(precond, axis=0)
        projected = jnp.dot(flat, precond, preferred_element_type=jnp.float32)
        terms = projected.reshape(examples, factor_rows, ka) * weights
        per_example = jnp.sum(jnp.sum(terms, axis=1), axis=1, keepdims=True)
        scores = jnp.sum(jnp.where(hot, per_example, 0.0), axis=0, keepdims=True)
        out[q : q + 1, :] = scores[:, : out.shape[1]]


def score(core, own, other, eigen, other_eigen, blocks):
    examples = sum(x.shape[0] for x in blocks) // 2
    return pl.pallas_call(
        score_kernel,
        out_shape=jax.ShapeDtypeStruct((own.shape[0] // RQ, examples), jnp.float32),
        in_specs=[spec(pltpu.SMEM)] + [spec(pltpu.VMEM)] * (4 + len(blocks)),
        out_specs=spec(pltpu.VMEM),
        compiler_params=grant(12),
    )(core, own, other, eigen, other_eigen, *blocks)


def direct(
    query_out,
    query_act,
    out_basis,
    act_basis,
    eigenvalues,
    train_out,
    train_act,
    train_tokens,
    train_ids,
):
    parts = lax.axis_size("blk")
    steps = parts.bit_length() - 1
    swap = [(0, 1), (1, 0)]

    def apart(x, distance):
        return lax.ppermute(x, "blk", [(s, s ^ distance) for s in range(parts)])

    def crossed(x, i):
        pairs = [
            (2 * s + f, 2 * (s ^ (1 << i)) + 1 - f) for s in range(parts) for f in range(2)
        ]
        return lax.ppermute(x, ("blk", "fsdp"), pairs)

    place = lax.axis_index("blk").reshape(1)
    core = lax.axis_index("fsdp").reshape(1)
    block = relay(pack(train_out, train_act))
    arrived = crossed(block, 2)
    total = project(query_out.T, query_act.T, out_basis, act_basis)
    *pieces, left, right = spread(
        place, train_tokens, train_ids, total, block, arrived, parts, parts // 2
    )
    near_left = join(pieces[0], left, crossed(left, 1))
    near_right = join(pieces[0], right, crossed(right, 0))
    near = join(pieces[0], near_left, near_right)
    far_first = reversed(range(1, len(pieces)))
    terms = [pieces[0]] + [apart(pieces[d], d) for d in far_first]
    sums = gather_sum(near, terms)
    far = join(near, crossed(near_left, 0), crossed(near_right, 1))
    other_eigen = lax.ppermute(hold(near, eigenvalues), "fsdp", swap)
    other_near = lax.ppermute(near, "fsdp", swap)
    other_far = lax.ppermute(far, "fsdp", swap)
    own = sums[0] + apart(sums[1], 4)
    other = lax.ppermute(own, "fsdp", swap)
    return score(
        core, own, other, eigenvalues, other_eigen, (near, far, other_near, other_far)
    )


def score_block(precond, out_rows, act_rows, token_counts):
    factor_rows = out_rows.shape[1]
    valid = (
        lax.broadcasted_iota(jnp.int32, (out_rows.shape[0], factor_rows), 1) < token_counts[:, None]
    ).astype(jnp.float32)
    projected = jnp.einsum("nri,qij->nrqj", out_rows, precond, preferred_element_type=jnp.float32)
    weights = act_rows.astype(jnp.float32) * valid[:, :, None]
    return jnp.einsum("nrqj,nrj->qn", projected, weights, precision=lax.Precision.HIGHEST)


def gathered(
    query_out,
    query_act,
    out_basis,
    act_basis,
    eigenvalues,
    train_out,
    train_act,
    train_tokens,
    train_ids,
):
    half_ks = out_basis.shape[1]
    local_rows = query_out.shape[1] // lax.axis_size("blk")
    out_part = lax.dot_general(
        query_out, out_basis, (((0,), (0,)), ((), ())), preferred_element_type=jnp.float32
    )
    act_part = lax.dot_general(
        query_act, act_basis, (((0,), (0,)), ((), ())), preferred_element_type=jnp.float32
    )
    rotated = lax.psum_scatter(
        jnp.concatenate([out_part, act_part], axis=1), "blk", scatter_dimension=0, tiled=True
    )
    out_coords = rotated[:, :half_ks]
    act_half = rotated[:, half_ks:]
    act_coords = lax.all_gather(act_half, "fsdp", axis=1, tiled=True)
    queries = local_rows // RQ
    out_three = out_coords.reshape(queries, RQ, half_ks)
    act_three = act_coords.reshape(queries, RQ, act_coords.shape[1])
    numer = jnp.einsum("qri,qrj->qij", out_three, act_three, precision=lax.Precision.HIGHEST)
    precond = (numer / (eigenvalues + damping)).astype(jnp.bfloat16)
    train_total = train_out.shape[0] * lax.axis_size("blk") * lax.axis_size("fsdp")
    empty = jnp.zeros((queries, train_total), jnp.float32)
    full_precond = lax.all_gather(precond, "fsdp", axis=1, tiled=True)
    out_rows = lax.all_gather(train_out, "blk", axis=0, tiled=True)
    act_rows = lax.all_gather(train_act, "blk", axis=0, tiled=True)
    token_counts = lax.all_gather(train_tokens, "blk", axis=0, tiled=True)
    column_ids = lax.all_gather(train_ids, "blk", axis=0, tiled=True)
    scores = empty.at[:, column_ids].add(
        score_block(full_precond, out_rows, act_rows, token_counts)
    )
    return lax.psum(scores, "fsdp")


def solution(mesh):
    parts = mesh.shape["blk"]
    few = parts == DIRECT_PARTS and mesh.shape["fsdp"] == 2
    return jax.shard_map(
        direct if few else gathered,
        mesh=mesh,
        in_specs=(
            P("blk", None),
            P("blk", None),
            P("blk", "fsdp"),
            P("blk", "fsdp"),
            P("fsdp", None),
            P(("groups", "blk", "fsdp"), None, None),
            P(("groups", "blk", "fsdp"), None, None),
            P(("groups", "blk", "fsdp")),
            P(("groups", "blk", "fsdp")),
        ),
        out_specs=P("blk", "groups"),
        check_vma=False,
    )
```

```python
import functools

import jax
import jax.numpy as jnp
from jax import lax
from jax.experimental import pallas as pl
from jax.experimental.pallas import tpu as pltpu
from jax.sharding import PartitionSpec as P

RQ = 4
LANES = 128
DIRECT_PARTS = 8
DIRECT_STEPS = (0, 6, 4, 2)
LAST_STEP = 1
WAIT_FLOPS = 10**9


damping = 0.1


def pinned(x):
    return pltpu.with_memory_space_constraint(x, pltpu.HBM)


def grant(mebibytes):
    return pltpu.CompilerParams(vmem_limit_bytes=mebibytes * 2**20)


def spec(space):
    return pl.BlockSpec(memory_space=space)


def pack_kernel(train_out, train_act, packed, sems):
    ks = train_out.shape[2]
    copies = (
        pltpu.make_async_copy(train_out, packed.at[:, :, :ks], sems.at[0]),
        pltpu.make_async_copy(train_act, packed.at[:, :, ks:], sems.at[1]),
    )
    for copy in copies:
        copy.start()
    for copy in copies:
        copy.wait()


def pack(train_out, train_act):
    examples, rows, ks = train_out.shape
    shape = (examples, rows, ks + train_act.shape[2])
    return pl.pallas_call(
        pack_kernel,
        out_shape=jax.ShapeDtypeStruct(shape, train_out.dtype),
        in_specs=[spec(pltpu.HBM)] * 2,
        out_specs=spec(pltpu.VMEM),
        scratch_shapes=[pltpu.SemaphoreType.DMA((2,))],
        compiler_params=grant(2),
    )(pinned(train_out), pinned(train_act))


def join_kernel(after, first, second, joined):
    del after
    count = first.shape[0]
    joined[:count] = first[...]
    joined[count:] = second[...]


def joined_shape(first, second):
    return jax.ShapeDtypeStruct(
        (first.shape[0] + second.shape[0],) + first.shape[1:], first.dtype
    )


def join(after, first, second):
    return pl.pallas_call(
        join_kernel,
        out_shape=joined_shape(first, second),
        in_specs=[spec(pl.ANY)] + [spec(pltpu.VMEM)] * 2,
        out_specs=spec(pltpu.VMEM),
        compiler_params=grant(4),
    )(after, first, second)


def relay_kernel(source, target):
    target[...] = source[...]


def relay(source):
    return pl.pallas_call(
        relay_kernel,
        out_shape=jax.ShapeDtypeStruct(source.shape, source.dtype),
        in_specs=[spec(pltpu.VMEM)],
        out_specs=spec(pltpu.VMEM),
        compiler_params=grant(2),
        cost_estimate=pl.CostEstimate(flops=WAIT_FLOPS, bytes_accessed=0, transcendentals=0),
    )(source)


def gather_sum_kernel(after, *refs):
    del after
    total = refs[0][...]
    for term in refs[1:-1]:
        total = total + term[...]
    refs[-1][...] = total


def gather_sum(after, terms):
    return pl.pallas_call(
        gather_sum_kernel,
        out_shape=jax.ShapeDtypeStruct(terms[0].shape, terms[0].dtype),
        in_specs=[spec(pl.ANY)] + [spec(pltpu.VMEM)] * len(terms),
        out_specs=spec(pltpu.VMEM),
        compiler_params=grant(4),
    )(after, *terms)


def hold_kernel(after, source, target):
    del after
    target[...] = source[...]


def hold(after, source):
    return pl.pallas_call(
        hold_kernel,
        out_shape=jax.ShapeDtypeStruct(source.shape, source.dtype),
        in_specs=[spec(pl.ANY), spec(pltpu.VMEM)],
        out_specs=spec(pltpu.VMEM),
        compiler_params=grant(2),
    )(after, source)


def project_kernel(query_out, query_act, out_basis, act_basis, total):
    half_ks = out_basis.shape[1]
    total[:, :half_ks] = jnp.dot(
        query_out[...], out_basis[...], preferred_element_type=jnp.float32
    )
    total[:, half_ks:] = jnp.dot(
        query_act[...], act_basis[...], preferred_element_type=jnp.float32
    )


def project(query_out, query_act, out_basis, act_basis):
    columns = query_out.shape[0]
    width = out_basis.shape[1] + act_basis.shape[1]
    operands = (query_out, query_act, out_basis, act_basis)
    return pl.pallas_call(
        project_kernel,
        out_shape=jax.ShapeDtypeStruct((columns, width), jnp.float32),
        in_specs=[spec(pltpu.VMEM)] * len(operands),
        out_specs=spec(pltpu.VMEM),
        compiler_params=grant(8),
        cost_estimate=pl.CostEstimate(
            flops=2 * columns * (out_basis.size + act_basis.size),
            bytes_accessed=2 * sum(x.size for x in operands),
            transcendentals=0,
        ),
    )(*operands)


def doubling_slot(distance, parts):
    steps = (parts // 2, 1, 2)
    return sum(1 << i for i, step in enumerate(steps) if distance & step)


def spread_kernel(place_ref, tokens_ref, ids_ref, total, first, second, *rest):
    pieces, joined = rest[:-1], rest[-1]
    each, local_rows, _ = pieces[0].shape
    parts = each * len(pieces)
    width = total.shape[1]
    row = lax.broadcasted_iota(jnp.int32, (local_rows, LANES), 0)
    lane = lax.broadcasted_iota(jnp.int32, (local_rows, LANES), 1)
    facts = jnp.where(lane < LANES // 2, ids_ref[0], tokens_ref[0]).astype(jnp.float32)
    for part in range(parts):
        start = pl.multiple_of((place_ref[0] ^ part) * local_rows, local_rows)
        piece = pieces[DIRECT_STEPS.index(part & DIRECT_STEPS[1])].at[int(part & LAST_STEP > 0)]
        piece[:, :width] = total[pl.ds(start, local_rows), :]
        piece[:, width:] = jnp.where(row == doubling_slot(part, parts), facts, 0.0)
    join_kernel(None, first, second, joined)


def spread(place, tokens, ids, total, first, second, parts):
    piece = jax.ShapeDtypeStruct(
        (parts // len(DIRECT_STEPS), total.shape[0] // parts, total.shape[1] + LANES), jnp.float32
    )
    joined = jax.ShapeDtypeStruct(
        (first.shape[0] + second.shape[0],) + first.shape[1:], first.dtype
    )
    return pl.pallas_call(
        spread_kernel,
        out_shape=[piece] * len(DIRECT_STEPS) + [joined],
        in_specs=[spec(pltpu.SMEM)] * 3 + [spec(pltpu.VMEM)] * 3,
        out_specs=[spec(pltpu.VMEM)] * (len(DIRECT_STEPS) + 1),
        compiler_params=grant(4),
    )(place, tokens, ids, total, first, second)


def split_three(x):
    high = x.astype(jnp.bfloat16)
    rest = x - high.astype(jnp.float32)
    middle = rest.astype(jnp.bfloat16)
    low = (rest - middle.astype(jnp.float32)).astype(jnp.bfloat16)
    return high, middle, low


def score_kernel(core_ref, own, other, eigen, other_eigen, *rest):
    blocks, out = rest[:-1], rest[-1]
    first = core_ref[0] == 0
    half, ka = eigen.shape
    factor_rows, width = blocks[0].shape[1:]
    ks = width - ka
    shared = own.shape[1] - LANES
    mine, theirs = own[...], other[...]
    coords = (jnp.where(first, mine, theirs), jnp.where(first, theirs, mine))
    eigens = (
        jnp.where(first, eigen[...], other_eigen[...]),
        jnp.where(first, other_eigen[...], eigen[...]),
    )
    scales = [1.0 / (e + damping) for e in eigens]
    act = jnp.concatenate([v[:, half:shared] for v in coords], axis=1)
    act_terms = split_three(act)
    out_terms = [split_three(v[:, :half]) for v in coords]
    order = ((0, 0), (0, 1), (1, 0), (1, 1), (0, 2), (2, 0))
    slot = lax.broadcasted_iota(jnp.int32, (mine.shape[0], LANES), 0)
    even = (slot // 4 + slot // 2 + slot) % 2 == 0
    facts = (mine[:, shared:], theirs[:, shared:])
    facts = jnp.concatenate(
        [jnp.where(even, facts[0], facts[1]), jnp.where(even, facts[1], facts[0])], axis=0
    )
    rows = jnp.concatenate([x[...] for x in blocks], axis=0)
    examples = rows.shape[0]
    lane = lax.broadcasted_iota(jnp.int32, (examples, LANES), 1).astype(jnp.float32)
    row = lax.broadcasted_iota(jnp.int32, (examples, factor_rows, ka), 1).astype(jnp.float32)
    hot = lane == facts[:, :1]
    keep = row < facts[:, LANES // 2 : LANES // 2 + 1][:, :, None]
    weights = jnp.where(keep, rows[:, :, ks:].astype(jnp.float32), 0.0)
    flat = rows[:, :, :ks].reshape(examples * factor_rows, ks)
    for q in range(out.shape[0]):
        cut = slice(q * RQ, (q + 1) * RQ)
        right = jnp.concatenate([act_terms[b][cut] for _, b in order], axis=0)
        precond = []
        for part in range(2):
            left = jnp.concatenate([out_terms[part][a][cut] for a, _ in order], axis=0)
            numer = lax.dot_general(
                left, right, (((0,), (0,)), ((), ())), preferred_element_type=jnp.float32
            )
            precond.append((numer * scales[part]).astype(jnp.bfloat16))
        precond = jnp.concatenate(precond, axis=0)
        projected = jnp.dot(flat, precond, preferred_element_type=jnp.float32)
        terms = projected.reshape(examples, factor_rows, ka) * weights
        per_example = jnp.sum(jnp.sum(terms, axis=1), axis=1, keepdims=True)
        scores = jnp.sum(jnp.where(hot, per_example, 0.0), axis=0, keepdims=True)
        out[q : q + 1, :] = scores[:, : out.shape[1]]


def score(core, own, other, eigen, other_eigen, blocks):
    examples = sum(x.shape[0] for x in blocks)
    return pl.pallas_call(
        score_kernel,
        out_shape=jax.ShapeDtypeStruct((own.shape[0] // RQ, examples), jnp.float32),
        in_specs=[spec(pltpu.SMEM)] + [spec(pltpu.VMEM)] * (4 + len(blocks)),
        out_specs=spec(pltpu.VMEM),
        compiler_params=grant(12),
    )(core, own, other, eigen, other_eigen, *blocks)


def direct(
    query_out,
    query_act,
    out_basis,
    act_basis,
    eigenvalues,
    train_out,
    train_act,
    train_tokens,
    train_ids,
):
    parts = lax.axis_size("blk")
    steps = parts.bit_length() - 1
    swap = [(0, 1), (1, 0)]

    def apart(x, distance):
        return lax.ppermute(x, "blk", [(s, s ^ distance) for s in range(parts)])

    def crossed(x, i):
        pairs = [
            (2 * s + f, 2 * (s ^ (1 << i)) + 1 - f) for s in range(parts) for f in range(2)
        ]
        return lax.ppermute(x, ("blk", "fsdp"), pairs)

    place = lax.axis_index("blk").reshape(1)
    core = lax.axis_index("fsdp").reshape(1)
    block = relay(pack(train_out, train_act))
    arrived = crossed(block, 2)
    total = project(query_out.T, query_act.T, out_basis, act_basis)
    *pieces, block = spread(
        place, train_tokens, train_ids, total, block, arrived, parts
    )
    near = join(pieces[0], block, crossed(block, 0))
    terms = [apart(piece, step) for piece, step in zip(pieces[1:], DIRECT_STEPS[1:])]
    sums = gather_sum(near, [pieces[0]] + terms)
    far = crossed(near, 1)
    other_eigen = lax.ppermute(hold(near, eigenvalues), "fsdp", swap)
    other_near = lax.ppermute(near, "fsdp", swap)
    other_far = lax.ppermute(far, "fsdp", swap)
    own = sums[0] + apart(sums[1], LAST_STEP)
    other = lax.ppermute(own, "fsdp", swap)
    return score(
        core, own, other, eigenvalues, other_eigen, (near, far, other_near, other_far)
    )


def score_block(precond, out_rows, act_rows, token_counts):
    factor_rows = out_rows.shape[1]
    valid = (
        lax.broadcasted_iota(jnp.int32, (out_rows.shape[0], factor_rows), 1) < token_counts[:, None]
    ).astype(jnp.float32)
    projected = jnp.einsum("nri,qij->nrqj", out_rows, precond, preferred_element_type=jnp.float32)
    weights = act_rows.astype(jnp.float32) * valid[:, :, None]
    return jnp.einsum("nrqj,nrj->qn", projected, weights, precision=lax.Precision.HIGHEST)


def gathered(
    query_out,
    query_act,
    out_basis,
    act_basis,
    eigenvalues,
    train_out,
    train_act,
    train_tokens,
    train_ids,
):
    half_ks = out_basis.shape[1]
    local_rows = query_out.shape[1] // lax.axis_size("blk")
    out_part = lax.dot_general(
        query_out, out_basis, (((0,), (0,)), ((), ())), preferred_element_type=jnp.float32
    )
    act_part = lax.dot_general(
        query_act, act_basis, (((0,), (0,)), ((), ())), preferred_element_type=jnp.float32
    )
    rotated = lax.psum_scatter(
        jnp.concatenate([out_part, act_part], axis=1), "blk", scatter_dimension=0, tiled=True
    )
    out_coords = rotated[:, :half_ks]
    act_half = rotated[:, half_ks:]
    act_coords = lax.all_gather(act_half, "fsdp", axis=1, tiled=True)
    queries = local_rows // RQ
    out_three = out_coords.reshape(queries, RQ, half_ks)
    act_three = act_coords.reshape(queries, RQ, act_coords.shape[1])
    numer = jnp.einsum("qri,qrj->qij", out_three, act_three, precision=lax.Precision.HIGHEST)
    precond = (numer / (eigenvalues + damping)).astype(jnp.bfloat16)
    train_total = train_out.shape[0] * lax.axis_size("blk") * lax.axis_size("fsdp")
    empty = jnp.zeros((queries, train_total), jnp.float32)
    full_precond = lax.all_gather(precond, "fsdp", axis=1, tiled=True)
    out_rows = lax.all_gather(train_out, "blk", axis=0, tiled=True)
    act_rows = lax.all_gather(train_act, "blk", axis=0, tiled=True)
    token_counts = lax.all_gather(train_tokens, "blk", axis=0, tiled=True)
    column_ids = lax.all_gather(train_ids, "blk", axis=0, tiled=True)
    scores = empty.at[:, column_ids].add(
        score_block(full_precond, out_rows, act_rows, token_counts)
    )
    return lax.psum(scores, "fsdp")


def solution(mesh):
    parts = mesh.shape["blk"]
    few = parts == DIRECT_PARTS and mesh.shape["fsdp"] == 2
    return jax.shard_map(
        direct if few else gathered,
        mesh=mesh,
        in_specs=(
            P("blk", None),
            P("blk", None),
            P("blk", "fsdp"),
            P("blk", "fsdp"),
            P("fsdp", None),
            P(("groups", "blk", "fsdp"), None, None),
            P(("groups", "blk", "fsdp"), None, None),
            P(("groups", "blk", "fsdp")),
            P(("groups", "blk", "fsdp")),
        ),
        out_specs=P("blk", "groups"),
        check_vma=False,
    )
```

```python
import functools

import jax
import jax.numpy as jnp
from jax import lax
from jax.experimental import pallas as pl
from jax.experimental.pallas import tpu as pltpu
from jax.sharding import PartitionSpec as P

RQ = 4
LANES = 128
DIRECT_PARTS = 8
WAIT_FLOPS = 10**9


damping = 0.1


def pinned(x):
    return pltpu.with_memory_space_constraint(x, pltpu.HBM)


def grant(mebibytes):
    return pltpu.CompilerParams(vmem_limit_bytes=mebibytes * 2**20)


def spec(space):
    return pl.BlockSpec(memory_space=space)


def pack_kernel(train_out, train_act, packed, sems):
    ks = train_out.shape[2]
    copies = (
        pltpu.make_async_copy(train_out, packed.at[:, :, :ks], sems.at[0]),
        pltpu.make_async_copy(train_act, packed.at[:, :, ks:], sems.at[1]),
    )
    for copy in copies:
        copy.start()
    for copy in copies:
        copy.wait()


def pack(train_out, train_act):
    examples, rows, ks = train_out.shape
    shape = (examples, rows, ks + train_act.shape[2])
    return pl.pallas_call(
        pack_kernel,
        out_shape=jax.ShapeDtypeStruct(shape, train_out.dtype),
        in_specs=[spec(pltpu.HBM)] * 2,
        out_specs=spec(pltpu.VMEM),
        scratch_shapes=[pltpu.SemaphoreType.DMA((2,))],
        compiler_params=grant(2),
    )(pinned(train_out), pinned(train_act))


def join_kernel(after, first, second, joined):
    del after
    count = first.shape[0]
    joined[:count] = first[...]
    joined[count:] = second[...]


def joined_shape(first, second):
    return jax.ShapeDtypeStruct(
        (first.shape[0] + second.shape[0],) + first.shape[1:], first.dtype
    )


def join(after, first, second):
    return pl.pallas_call(
        join_kernel,
        out_shape=joined_shape(first, second),
        in_specs=[spec(pl.ANY)] + [spec(pltpu.VMEM)] * 2,
        out_specs=spec(pltpu.VMEM),
        compiler_params=grant(4),
    )(after, first, second)


def relay_kernel(source, target):
    target[...] = source[...]


def relay(source):
    return pl.pallas_call(
        relay_kernel,
        out_shape=jax.ShapeDtypeStruct(source.shape, source.dtype),
        in_specs=[spec(pltpu.VMEM)],
        out_specs=spec(pltpu.VMEM),
        compiler_params=grant(2),
        cost_estimate=pl.CostEstimate(flops=WAIT_FLOPS, bytes_accessed=0, transcendentals=0),
    )(source)


def gather_sum_kernel(after, *refs):
    del after
    total = refs[0][...]
    for term in refs[1:-1]:
        total = total + term[...]
    refs[-1][...] = total


def gather_sum(after, terms):
    return pl.pallas_call(
        gather_sum_kernel,
        out_shape=jax.ShapeDtypeStruct(terms[0].shape, terms[0].dtype),
        in_specs=[spec(pl.ANY)] + [spec(pltpu.VMEM)] * len(terms),
        out_specs=spec(pltpu.VMEM),
        compiler_params=grant(4),
    )(after, *terms)


def project_kernel(query_out, query_act, out_basis, act_basis, total):
    half_ks = out_basis.shape[1]
    total[:, :half_ks] = jnp.dot(
        query_out[...], out_basis[...], preferred_element_type=jnp.float32
    )
    total[:, half_ks:] = jnp.dot(
        query_act[...], act_basis[...], preferred_element_type=jnp.float32
    )


def project(query_out, query_act, out_basis, act_basis):
    columns = query_out.shape[0]
    width = out_basis.shape[1] + act_basis.shape[1]
    operands = (query_out, query_act, out_basis, act_basis)
    return pl.pallas_call(
        project_kernel,
        out_shape=jax.ShapeDtypeStruct((columns, width), jnp.float32),
        in_specs=[spec(pltpu.VMEM)] * len(operands),
        out_specs=spec(pltpu.VMEM),
        compiler_params=grant(8),
        cost_estimate=pl.CostEstimate(
            flops=2 * columns * (out_basis.size + act_basis.size),
            bytes_accessed=2 * sum(x.size for x in operands),
            transcendentals=0,
        ),
    )(*operands)


def doubling_slot(distance, parts):
    bits = parts.bit_length() - 1
    return sum(1 << (bits - 1 - i) for i in range(bits) if distance >> i & 1)


def spread_kernel(place_ref, tokens_ref, ids_ref, after, total, first, second, *rest):
    del after
    pieces, joined = rest[:-1], rest[-1]
    groups = len(pieces)
    each, local_rows, _ = pieces[0].shape
    parts = groups * each
    width = total.shape[1]
    row = lax.broadcasted_iota(jnp.int32, (local_rows, LANES), 0)
    lane = lax.broadcasted_iota(jnp.int32, (local_rows, LANES), 1)
    facts = jnp.where(lane < LANES // 2, ids_ref[0], tokens_ref[0]).astype(jnp.float32)
    for part in range(parts):
        start = pl.multiple_of((place_ref[0] ^ part) * local_rows, local_rows)
        piece = pieces[part % groups].at[part // groups]
        piece[:, :width] = total[pl.ds(start, local_rows), :]
        piece[:, width:] = jnp.where(row == doubling_slot(part, parts), facts, 0.0)
    join_kernel(None, first, second, joined)


def spread(place, tokens, ids, after, total, first, second, parts, groups):
    piece = jax.ShapeDtypeStruct(
        (parts // groups, total.shape[0] // parts, total.shape[1] + LANES), jnp.float32
    )
    joined = jax.ShapeDtypeStruct(
        (first.shape[0] + second.shape[0],) + first.shape[1:], first.dtype
    )
    return pl.pallas_call(
        spread_kernel,
        out_shape=[piece] * groups + [joined],
        in_specs=[spec(pltpu.SMEM)] * 3 + [spec(pl.ANY)] + [spec(pltpu.VMEM)] * 3,
        out_specs=[spec(pltpu.VMEM)] * (groups + 1),
        compiler_params=grant(4),
    )(place, tokens, ids, after, total, first, second)


def split_three(x):
    high = x.astype(jnp.bfloat16)
    rest = x - high.astype(jnp.float32)
    middle = rest.astype(jnp.bfloat16)
    low = (rest - middle.astype(jnp.float32)).astype(jnp.bfloat16)
    return high, middle, low


def scale_kernel(core_ref, after, eigen, other_eigen, scales):
    del after
    first = core_ref[0] == 0
    half = eigen.shape[0]
    scales[:half] = 1.0 / (jnp.where(first, eigen[...], other_eigen[...]) + damping)
    scales[half:] = 1.0 / (jnp.where(first, other_eigen[...], eigen[...]) + damping)


def invert(core, after, eigen, other_eigen):
    half, ka = eigen.shape
    return pl.pallas_call(
        scale_kernel,
        out_shape=jax.ShapeDtypeStruct((2 * half, ka), jnp.float32),
        in_specs=[spec(pltpu.SMEM), spec(pl.ANY)] + [spec(pltpu.VMEM)] * 2,
        out_specs=spec(pltpu.VMEM),
        compiler_params=grant(4),
    )(core, after, eigen, other_eigen)


def score_kernel(core_ref, own, other, scales, *rest):
    blocks, out = rest[:-1], rest[-1]
    first = core_ref[0] == 0
    half, ka = scales.shape[0] // 2, scales.shape[1]
    factor_rows, width = blocks[0].shape[1:]
    ks = width - ka
    shared = own.shape[1] - LANES
    mine, theirs = own[...], other[...]
    coords = (jnp.where(first, mine, theirs), jnp.where(first, theirs, mine))
    act = jnp.concatenate([v[:, half:shared] for v in coords], axis=1)
    act_terms = split_three(act)
    out_terms = split_three(jnp.concatenate([v[:, :half] for v in coords], axis=1))
    order = ((0, 0), (0, 1), (1, 0), (1, 1), (0, 2), (2, 0))
    slot = lax.broadcasted_iota(jnp.int32, (mine.shape[0], LANES), 0)
    even = (slot // 4 + slot // 2 + slot) % 2 == 0
    facts = (mine[:, shared:], theirs[:, shared:])
    facts = jnp.concatenate(
        [jnp.where(even, facts[0], facts[1]), jnp.where(even, facts[1], facts[0])], axis=0
    )
    rows = jnp.concatenate([x[...] for x in blocks], axis=0)
    examples = rows.shape[0]
    lane = lax.broadcasted_iota(jnp.int32, (examples, LANES), 1).astype(jnp.float32)
    row = lax.broadcasted_iota(jnp.int32, (examples, factor_rows, ka), 1).astype(jnp.float32)
    hot = lane == facts[:, :1]
    keep = row < facts[:, LANES // 2 : LANES // 2 + 1][:, :, None]
    weights = jnp.where(keep, rows[:, :, ks:].astype(jnp.float32), 0.0)
    flat = rows[:, :, :ks].reshape(examples * factor_rows, ks)
    for q in range(out.shape[0]):
        cut = slice(q * RQ, (q + 1) * RQ)
        right = jnp.concatenate([act_terms[b][cut] for _, b in order], axis=0)
        left = jnp.concatenate([out_terms[a][cut] for a, _ in order], axis=0)
        numer = lax.dot_general(
            left, right, (((0,), (0,)), ((), ())), preferred_element_type=jnp.float32
        )
        precond = (numer * scales[...]).astype(jnp.bfloat16)
        projected = jnp.dot(flat, precond, preferred_element_type=jnp.float32)
        terms = projected.reshape(examples, factor_rows, ka) * weights
        per_example = jnp.sum(jnp.sum(terms, axis=1), axis=1, keepdims=True)
        scores = jnp.sum(jnp.where(hot, per_example, 0.0), axis=0, keepdims=True)
        out[q : q + 1, :] = scores[:, : out.shape[1]]


def score(core, own, other, scales, blocks):
    examples = sum(x.shape[0] for x in blocks)
    return pl.pallas_call(
        score_kernel,
        out_shape=jax.ShapeDtypeStruct((own.shape[0] // RQ, examples), jnp.float32),
        in_specs=[spec(pltpu.SMEM)] + [spec(pltpu.VMEM)] * (3 + len(blocks)),
        out_specs=spec(pltpu.VMEM),
        compiler_params=grant(12),
    )(core, own, other, scales, *blocks)


def direct(
    query_out,
    query_act,
    out_basis,
    act_basis,
    eigenvalues,
    train_out,
    train_act,
    train_tokens,
    train_ids,
):
    parts = lax.axis_size("blk")
    steps = parts.bit_length() - 1
    swap = [(0, 1), (1, 0)]

    def apart(x, distance):
        return lax.ppermute(x, "blk", [(s, s ^ distance) for s in range(parts)])

    def crossed(x, i):
        pairs = [
            (2 * s + f, 2 * (s ^ (1 << i)) + 1 - f) for s in range(parts) for f in range(2)
        ]
        return lax.ppermute(x, ("blk", "fsdp"), pairs)

    place = lax.axis_index("blk").reshape(1)
    core = lax.axis_index("fsdp").reshape(1)
    other_eigen = lax.ppermute(eigenvalues, "fsdp", swap)
    block = relay(pack(train_out, train_act))
    arrived = crossed(block, 2)
    total = project(query_out.T, query_act.T, out_basis, act_basis)
    *pieces, block = spread(
        place, train_tokens, train_ids, other_eigen, total, block, arrived, parts, parts // 2
    )
    near = join(pieces[0], block, crossed(block, 1))
    far_first = reversed(range(1, len(pieces)))
    terms = [pieces[0]] + [apart(pieces[d], d) for d in far_first]
    sums = gather_sum(near, terms)
    far = crossed(near, 0)
    other_near = lax.ppermute(near, "fsdp", swap)
    other_far = lax.ppermute(far, "fsdp", swap)
    own = sums[0] + apart(sums[1], 4)
    other = lax.ppermute(own, "fsdp", swap)
    scales = invert(core, near, eigenvalues, other_eigen)
    return score(core, own, other, scales, (near, far, other_near, other_far))


def score_block(precond, out_rows, act_rows, token_counts):
    factor_rows = out_rows.shape[1]
    valid = (
        lax.broadcasted_iota(jnp.int32, (out_rows.shape[0], factor_rows), 1) < token_counts[:, None]
    ).astype(jnp.float32)
    projected = jnp.einsum("nri,qij->nrqj", out_rows, precond, preferred_element_type=jnp.float32)
    weights = act_rows.astype(jnp.float32) * valid[:, :, None]
    return jnp.einsum("nrqj,nrj->qn", projected, weights, precision=lax.Precision.HIGHEST)


def gathered(
    query_out,
    query_act,
    out_basis,
    act_basis,
    eigenvalues,
    train_out,
    train_act,
    train_tokens,
    train_ids,
):
    half_ks = out_basis.shape[1]
    local_rows = query_out.shape[1] // lax.axis_size("blk")
    out_part = lax.dot_general(
        query_out, out_basis, (((0,), (0,)), ((), ())), preferred_element_type=jnp.float32
    )
    act_part = lax.dot_general(
        query_act, act_basis, (((0,), (0,)), ((), ())), preferred_element_type=jnp.float32
    )
    rotated = lax.psum_scatter(
        jnp.concatenate([out_part, act_part], axis=1), "blk", scatter_dimension=0, tiled=True
    )
    out_coords = rotated[:, :half_ks]
    act_half = rotated[:, half_ks:]
    act_coords = lax.all_gather(act_half, "fsdp", axis=1, tiled=True)
    queries = local_rows // RQ
    out_three = out_coords.reshape(queries, RQ, half_ks)
    act_three = act_coords.reshape(queries, RQ, act_coords.shape[1])
    numer = jnp.einsum("qri,qrj->qij", out_three, act_three, precision=lax.Precision.HIGHEST)
    precond = (numer / (eigenvalues + damping)).astype(jnp.bfloat16)
    train_total = train_out.shape[0] * lax.axis_size("blk") * lax.axis_size("fsdp")
    empty = jnp.zeros((queries, train_total), jnp.float32)
    full_precond = lax.all_gather(precond, "fsdp", axis=1, tiled=True)
    out_rows = lax.all_gather(train_out, "blk", axis=0, tiled=True)
    act_rows = lax.all_gather(train_act, "blk", axis=0, tiled=True)
    token_counts = lax.all_gather(train_tokens, "blk", axis=0, tiled=True)
    column_ids = lax.all_gather(train_ids, "blk", axis=0, tiled=True)
    scores = empty.at[:, column_ids].add(
        score_block(full_precond, out_rows, act_rows, token_counts)
    )
    return lax.psum(scores, "fsdp")


def solution(mesh):
    parts = mesh.shape["blk"]
    few = parts == DIRECT_PARTS and mesh.shape["fsdp"] == 2
    return jax.shard_map(
        direct if few else gathered,
        mesh=mesh,
        in_specs=(
            P("blk", None),
            P("blk", None),
            P("blk", "fsdp"),
            P("blk", "fsdp"),
            P("fsdp", None),
            P(("groups", "blk", "fsdp"), None, None),
            P(("groups", "blk", "fsdp"), None, None),
            P(("groups", "blk", "fsdp")),
            P(("groups", "blk", "fsdp")),
        ),
        out_specs=P("blk", "groups"),
        check_vma=False,
    )
```

```python
import functools

import jax
import jax.numpy as jnp
from jax import lax
from jax.experimental import pallas as pl
from jax.experimental.pallas import tpu as pltpu
from jax.sharding import PartitionSpec as P

RQ = 4
LANES = 128
DIRECT_PARTS = 8
WAIT_FLOPS = 10**9


damping = 0.1


def pinned(x):
    return pltpu.with_memory_space_constraint(x, pltpu.HBM)


def grant(mebibytes):
    return pltpu.CompilerParams(vmem_limit_bytes=mebibytes * 2**20)


def spec(space):
    return pl.BlockSpec(memory_space=space)


def pack_kernel(train_out, train_act, packed, sems):
    ks = train_out.shape[2]
    copies = (
        pltpu.make_async_copy(train_out, packed.at[:, :, :ks], sems.at[0]),
        pltpu.make_async_copy(train_act, packed.at[:, :, ks:], sems.at[1]),
    )
    for copy in copies:
        copy.start()
    for copy in copies:
        copy.wait()


def pack(train_out, train_act):
    examples, rows, ks = train_out.shape
    shape = (examples, rows, ks + train_act.shape[2])
    return pl.pallas_call(
        pack_kernel,
        out_shape=jax.ShapeDtypeStruct(shape, train_out.dtype),
        in_specs=[spec(pltpu.HBM)] * 2,
        out_specs=spec(pltpu.VMEM),
        scratch_shapes=[pltpu.SemaphoreType.DMA((2,))],
        compiler_params=grant(2),
    )(pinned(train_out), pinned(train_act))


def join_kernel(after, first, second, joined):
    del after
    count = first.shape[0]
    joined[:count] = first[...]
    joined[count:] = second[...]


def joined_shape(first, second):
    return jax.ShapeDtypeStruct(
        (first.shape[0] + second.shape[0],) + first.shape[1:], first.dtype
    )


def join(after, first, second):
    return pl.pallas_call(
        join_kernel,
        out_shape=joined_shape(first, second),
        in_specs=[spec(pl.ANY)] + [spec(pltpu.VMEM)] * 2,
        out_specs=spec(pltpu.VMEM),
        compiler_params=grant(4),
    )(after, first, second)


def relay_kernel(source, target):
    target[...] = source[...]


def relay(source):
    return pl.pallas_call(
        relay_kernel,
        out_shape=jax.ShapeDtypeStruct(source.shape, source.dtype),
        in_specs=[spec(pltpu.VMEM)],
        out_specs=spec(pltpu.VMEM),
        compiler_params=grant(2),
        cost_estimate=pl.CostEstimate(flops=WAIT_FLOPS, bytes_accessed=0, transcendentals=0),
    )(source)


def gather_sum_kernel(after, *refs):
    del after
    total = refs[0][...]
    for term in refs[1:-1]:
        total = total + term[...]
    refs[-1][...] = total


def gather_sum(after, terms):
    return pl.pallas_call(
        gather_sum_kernel,
        out_shape=jax.ShapeDtypeStruct(terms[0].shape, terms[0].dtype),
        in_specs=[spec(pl.ANY)] + [spec(pltpu.VMEM)] * len(terms),
        out_specs=spec(pltpu.VMEM),
        compiler_params=grant(4),
    )(after, *terms)


def project_kernel(query_out, query_act, out_basis, act_basis, total):
    half_ks = out_basis.shape[1]
    total[:, :half_ks] = jnp.dot(
        query_out[...], out_basis[...], preferred_element_type=jnp.float32
    )
    total[:, half_ks:] = jnp.dot(
        query_act[...], act_basis[...], preferred_element_type=jnp.float32
    )


def project(query_out, query_act, out_basis, act_basis):
    columns = query_out.shape[0]
    width = out_basis.shape[1] + act_basis.shape[1]
    operands = (query_out, query_act, out_basis, act_basis)
    return pl.pallas_call(
        project_kernel,
        out_shape=jax.ShapeDtypeStruct((columns, width), jnp.float32),
        in_specs=[spec(pltpu.VMEM)] * len(operands),
        out_specs=spec(pltpu.VMEM),
        compiler_params=grant(8),
        cost_estimate=pl.CostEstimate(
            flops=2 * columns * (out_basis.size + act_basis.size),
            bytes_accessed=2 * sum(x.size for x in operands),
            transcendentals=0,
        ),
    )(*operands)


def doubling_slot(distance, parts):
    bits = parts.bit_length() - 1
    return sum(1 << (bits - 1 - i) for i in range(bits) if distance >> i & 1)


def spread_kernel(place_ref, tokens_ref, ids_ref, after, total, first, second, *rest):
    del after
    pieces, joined = rest[:-1], rest[-1]
    groups = len(pieces)
    each, local_rows, _ = pieces[0].shape
    parts = groups * each
    width = total.shape[1]
    row = lax.broadcasted_iota(jnp.int32, (local_rows, LANES), 0)
    lane = lax.broadcasted_iota(jnp.int32, (local_rows, LANES), 1)
    facts = jnp.where(lane < LANES // 2, ids_ref[0], tokens_ref[0]).astype(jnp.float32)
    for part in range(parts):
        start = pl.multiple_of((place_ref[0] ^ part) * local_rows, local_rows)
        piece = pieces[part % groups].at[part // groups]
        piece[:, :width] = total[pl.ds(start, local_rows), :]
        piece[:, width:] = jnp.where(row == doubling_slot(part, parts), facts, 0.0)
    join_kernel(None, first, second, joined)


def spread(place, tokens, ids, after, total, first, second, parts, groups):
    piece = jax.ShapeDtypeStruct(
        (parts // groups, total.shape[0] // parts, total.shape[1] + LANES), jnp.float32
    )
    joined = jax.ShapeDtypeStruct(
        (first.shape[0] + second.shape[0],) + first.shape[1:], first.dtype
    )
    return pl.pallas_call(
        spread_kernel,
        out_shape=[piece] * groups + [joined],
        in_specs=[spec(pltpu.SMEM)] * 3 + [spec(pl.ANY)] + [spec(pltpu.VMEM)] * 3,
        out_specs=[spec(pltpu.VMEM)] * (groups + 1),
        compiler_params=grant(4),
    )(place, tokens, ids, after, total, first, second)


def split_three(x):
    high = x.astype(jnp.bfloat16)
    rest = x - high.astype(jnp.float32)
    middle = rest.astype(jnp.bfloat16)
    low = (rest - middle.astype(jnp.float32)).astype(jnp.bfloat16)
    return high, middle, low


def scale_kernel(core_ref, after, eigen, other_eigen, scales):
    del after
    first = core_ref[0] == 0
    half = eigen.shape[0]
    scales[:half] = 1.0 / (jnp.where(first, eigen[...], other_eigen[...]) + damping)
    scales[half:] = 1.0 / (jnp.where(first, other_eigen[...], eigen[...]) + damping)


def invert(core, after, eigen, other_eigen):
    half, ka = eigen.shape
    return pl.pallas_call(
        scale_kernel,
        out_shape=jax.ShapeDtypeStruct((2 * half, ka), jnp.float32),
        in_specs=[spec(pltpu.SMEM), spec(pl.ANY)] + [spec(pltpu.VMEM)] * 2,
        out_specs=spec(pltpu.VMEM),
        compiler_params=grant(4),
    )(core, after, eigen, other_eigen)


def score_kernel(core_ref, own, other, scales, *rest):
    blocks, out = rest[:-1], rest[-1]
    first = core_ref[0] == 0
    half, ka = scales.shape[0] // 2, scales.shape[1]
    factor_rows, width = blocks[0].shape[1:]
    ks = width - ka
    shared = own.shape[1] - LANES
    mine, theirs = own[...], other[...]
    coords = (jnp.where(first, mine, theirs), jnp.where(first, theirs, mine))
    act = jnp.concatenate([v[:, half:shared] for v in coords], axis=1)
    act_terms = split_three(act)
    out_terms = split_three(jnp.concatenate([v[:, :half] for v in coords], axis=1))
    order = ((0, 0), (0, 1), (1, 0), (1, 1), (0, 2), (2, 0))
    slot = lax.broadcasted_iota(jnp.int32, (mine.shape[0], LANES), 0)
    even = (slot // 4 + slot // 2 + slot) % 2 == 0
    facts = (mine[:, shared:], theirs[:, shared:])
    facts = jnp.concatenate(
        [jnp.where(even, facts[0], facts[1]), jnp.where(even, facts[1], facts[0])], axis=0
    )
    rows = jnp.concatenate([x[...] for x in blocks], axis=0)
    examples = rows.shape[0]
    lane = lax.broadcasted_iota(jnp.int32, (examples, LANES), 1).astype(jnp.float32)
    row = lax.broadcasted_iota(jnp.int32, (examples, factor_rows, ka), 1).astype(jnp.float32)
    hot = lane == facts[:, :1]
    keep = row < facts[:, LANES // 2 : LANES // 2 + 1][:, :, None]
    weights = jnp.where(keep, rows[:, :, ks:].astype(jnp.float32), 0.0)
    flat = rows[:, :, :ks].reshape(examples * factor_rows, ks)
    queries = out.shape[0]
    preconds = []
    for q in range(queries):
        cut = slice(q * RQ, (q + 1) * RQ)
        right = jnp.concatenate([act_terms[b][cut] for _, b in order], axis=0)
        left = jnp.concatenate([out_terms[a][cut] for a, _ in order], axis=0)
        numer = lax.dot_general(
            left, right, (((0,), (0,)), ((), ())), preferred_element_type=jnp.float32
        )
        preconds.append((numer * scales[...]).astype(jnp.bfloat16))
    precond = jnp.concatenate(preconds, axis=1)
    projected = jnp.dot(flat, precond, preferred_element_type=jnp.float32)
    for q in range(queries):
        terms = projected[:, q * ka : (q + 1) * ka].reshape(examples, factor_rows, ka) * weights
        per_example = jnp.sum(jnp.sum(terms, axis=1), axis=1, keepdims=True)
        scores = jnp.sum(jnp.where(hot, per_example, 0.0), axis=0, keepdims=True)
        out[q : q + 1, :] = scores[:, : out.shape[1]]


def score(core, own, other, scales, blocks):
    examples = sum(x.shape[0] for x in blocks)
    return pl.pallas_call(
        score_kernel,
        out_shape=jax.ShapeDtypeStruct((own.shape[0] // RQ, examples), jnp.float32),
        in_specs=[spec(pltpu.SMEM)] + [spec(pltpu.VMEM)] * (3 + len(blocks)),
        out_specs=spec(pltpu.VMEM),
        compiler_params=grant(12),
    )(core, own, other, scales, *blocks)


def direct(
    query_out,
    query_act,
    out_basis,
    act_basis,
    eigenvalues,
    train_out,
    train_act,
    train_tokens,
    train_ids,
):
    parts = lax.axis_size("blk")
    steps = parts.bit_length() - 1
    swap = [(0, 1), (1, 0)]

    def apart(x, distance):
        return lax.ppermute(x, "blk", [(s, s ^ distance) for s in range(parts)])

    def crossed(x, i):
        pairs = [
            (2 * s + f, 2 * (s ^ (1 << i)) + 1 - f) for s in range(parts) for f in range(2)
        ]
        return lax.ppermute(x, ("blk", "fsdp"), pairs)

    place = lax.axis_index("blk").reshape(1)
    core = lax.axis_index("fsdp").reshape(1)
    other_eigen = lax.ppermute(eigenvalues, "fsdp", swap)
    block = relay(pack(train_out, train_act))
    arrived = crossed(block, 2)
    total = project(query_out.T, query_act.T, out_basis, act_basis)
    *pieces, block = spread(
        place, train_tokens, train_ids, other_eigen, total, block, arrived, parts, parts // 2
    )
    near = join(pieces[0], block, crossed(block, 1))
    far_first = reversed(range(1, len(pieces)))
    terms = [pieces[0]] + [apart(pieces[d], d) for d in far_first]
    sums = gather_sum(near, terms)
    far = crossed(near, 0)
    other_near = lax.ppermute(near, "fsdp", swap)
    other_far = lax.ppermute(far, "fsdp", swap)
    own = sums[0] + apart(sums[1], 4)
    other = lax.ppermute(own, "fsdp", swap)
    scales = invert(core, near, eigenvalues, other_eigen)
    return score(core, own, other, scales, (near, far, other_near, other_far))


def score_block(precond, out_rows, act_rows, token_counts):
    factor_rows = out_rows.shape[1]
    valid = (
        lax.broadcasted_iota(jnp.int32, (out_rows.shape[0], factor_rows), 1) < token_counts[:, None]
    ).astype(jnp.float32)
    projected = jnp.einsum("nri,qij->nrqj", out_rows, precond, preferred_element_type=jnp.float32)
    weights = act_rows.astype(jnp.float32) * valid[:, :, None]
    return jnp.einsum("nrqj,nrj->qn", projected, weights, precision=lax.Precision.HIGHEST)


def gathered(
    query_out,
    query_act,
    out_basis,
    act_basis,
    eigenvalues,
    train_out,
    train_act,
    train_tokens,
    train_ids,
):
    half_ks = out_basis.shape[1]
    local_rows = query_out.shape[1] // lax.axis_size("blk")
    out_part = lax.dot_general(
        query_out, out_basis, (((0,), (0,)), ((), ())), preferred_element_type=jnp.float32
    )
    act_part = lax.dot_general(
        query_act, act_basis, (((0,), (0,)), ((), ())), preferred_element_type=jnp.float32
    )
    rotated = lax.psum_scatter(
        jnp.concatenate([out_part, act_part], axis=1), "blk", scatter_dimension=0, tiled=True
    )
    out_coords = rotated[:, :half_ks]
    act_half = rotated[:, half_ks:]
    act_coords = lax.all_gather(act_half, "fsdp", axis=1, tiled=True)
    queries = local_rows // RQ
    out_three = out_coords.reshape(queries, RQ, half_ks)
    act_three = act_coords.reshape(queries, RQ, act_coords.shape[1])
    numer = jnp.einsum("qri,qrj->qij", out_three, act_three, precision=lax.Precision.HIGHEST)
    precond = (numer / (eigenvalues + damping)).astype(jnp.bfloat16)
    train_total = train_out.shape[0] * lax.axis_size("blk") * lax.axis_size("fsdp")
    empty = jnp.zeros((queries, train_total), jnp.float32)
    full_precond = lax.all_gather(precond, "fsdp", axis=1, tiled=True)
    out_rows = lax.all_gather(train_out, "blk", axis=0, tiled=True)
    act_rows = lax.all_gather(train_act, "blk", axis=0, tiled=True)
    token_counts = lax.all_gather(train_tokens, "blk", axis=0, tiled=True)
    column_ids = lax.all_gather(train_ids, "blk", axis=0, tiled=True)
    scores = empty.at[:, column_ids].add(
        score_block(full_precond, out_rows, act_rows, token_counts)
    )
    return lax.psum(scores, "fsdp")


def solution(mesh):
    parts = mesh.shape["blk"]
    few = parts == DIRECT_PARTS and mesh.shape["fsdp"] == 2
    return jax.shard_map(
        direct if few else gathered,
        mesh=mesh,
        in_specs=(
            P("blk", None),
            P("blk", None),
            P("blk", "fsdp"),
            P("blk", "fsdp"),
            P("fsdp", None),
            P(("groups", "blk", "fsdp"), None, None),
            P(("groups", "blk", "fsdp"), None, None),
            P(("groups", "blk", "fsdp")),
            P(("groups", "blk", "fsdp")),
        ),
        out_specs=P("blk", "groups"),
        check_vma=False,
    )
```

```python
import functools

import jax
import jax.numpy as jnp
from jax import lax
from jax.experimental import pallas as pl
from jax.experimental.pallas import tpu as pltpu
from jax.sharding import PartitionSpec as P

RQ = 4
LANES = 128
DIRECT_PARTS = 8
WAIT_FLOPS = 10**9


damping = 0.1


def pinned(x):
    return pltpu.with_memory_space_constraint(x, pltpu.HBM)


def grant(mebibytes):
    return pltpu.CompilerParams(vmem_limit_bytes=mebibytes * 2**20)


def spec(space):
    return pl.BlockSpec(memory_space=space)


def pack_kernel(train_out, train_act, packed, sems):
    ks = train_out.shape[2]
    copies = (
        pltpu.make_async_copy(train_out, packed.at[:, :, :ks], sems.at[0]),
        pltpu.make_async_copy(train_act, packed.at[:, :, ks:], sems.at[1]),
    )
    for copy in copies:
        copy.start()
    for copy in copies:
        copy.wait()


def pack(train_out, train_act):
    examples, rows, ks = train_out.shape
    shape = (examples, rows, ks + train_act.shape[2])
    return pl.pallas_call(
        pack_kernel,
        out_shape=jax.ShapeDtypeStruct(shape, train_out.dtype),
        in_specs=[spec(pltpu.HBM)] * 2,
        out_specs=spec(pltpu.VMEM),
        scratch_shapes=[pltpu.SemaphoreType.DMA((2,))],
        compiler_params=grant(2),
    )(pinned(train_out), pinned(train_act))


def join_kernel(after, first, second, joined):
    del after
    count = first.shape[0]
    joined[:count] = first[...]
    joined[count:] = second[...]


def joined_shape(first, second):
    return jax.ShapeDtypeStruct(
        (first.shape[0] + second.shape[0],) + first.shape[1:], first.dtype
    )


def join(after, first, second):
    return pl.pallas_call(
        join_kernel,
        out_shape=joined_shape(first, second),
        in_specs=[spec(pl.ANY)] + [spec(pltpu.VMEM)] * 2,
        out_specs=spec(pltpu.VMEM),
        compiler_params=grant(4),
    )(after, first, second)


def relay_kernel(source, target):
    target[...] = source[...]


def relay(source):
    return pl.pallas_call(
        relay_kernel,
        out_shape=jax.ShapeDtypeStruct(source.shape, source.dtype),
        in_specs=[spec(pltpu.VMEM)],
        out_specs=spec(pltpu.VMEM),
        compiler_params=grant(2),
        cost_estimate=pl.CostEstimate(flops=WAIT_FLOPS, bytes_accessed=0, transcendentals=0),
    )(source)


def gather_sum_kernel(after, *refs):
    del after
    total = refs[0][...]
    for term in refs[1:-1]:
        total = total + term[...]
    refs[-1][...] = total


def gather_sum(after, terms):
    return pl.pallas_call(
        gather_sum_kernel,
        out_shape=jax.ShapeDtypeStruct(terms[0].shape, terms[0].dtype),
        in_specs=[spec(pl.ANY)] + [spec(pltpu.VMEM)] * len(terms),
        out_specs=spec(pltpu.VMEM),
        compiler_params=grant(4),
    )(after, *terms)


def project_kernel(query_out, query_act, out_basis, act_basis, total):
    half_ks = out_basis.shape[1]
    total[:, :half_ks] = jnp.dot(
        query_out[...], out_basis[...], preferred_element_type=jnp.float32
    )
    total[:, half_ks:] = jnp.dot(
        query_act[...], act_basis[...], preferred_element_type=jnp.float32
    )


def project(query_out, query_act, out_basis, act_basis):
    columns = query_out.shape[0]
    width = out_basis.shape[1] + act_basis.shape[1]
    operands = (query_out, query_act, out_basis, act_basis)
    return pl.pallas_call(
        project_kernel,
        out_shape=jax.ShapeDtypeStruct((columns, width), jnp.float32),
        in_specs=[spec(pltpu.VMEM)] * len(operands),
        out_specs=spec(pltpu.VMEM),
        compiler_params=grant(8),
        cost_estimate=pl.CostEstimate(
            flops=2 * columns * (out_basis.size + act_basis.size),
            bytes_accessed=2 * sum(x.size for x in operands),
            transcendentals=0,
        ),
    )(*operands)


def doubling_slot(distance, parts):
    bits = parts.bit_length() - 1
    return sum(1 << (bits - 1 - i) for i in range(bits) if distance >> i & 1)


def spread_kernel(place_ref, tokens_ref, ids_ref, after, total, first, second, *rest):
    del after
    pieces, joined = rest[:-1], rest[-1]
    groups = len(pieces)
    each, local_rows, _ = pieces[0].shape
    parts = groups * each
    width = total.shape[1]
    row = lax.broadcasted_iota(jnp.int32, (local_rows, LANES), 0)
    lane = lax.broadcasted_iota(jnp.int32, (local_rows, LANES), 1)
    facts = jnp.where(lane < LANES // 2, ids_ref[0], tokens_ref[0]).astype(jnp.float32)
    for part in range(parts):
        start = pl.multiple_of((place_ref[0] ^ part) * local_rows, local_rows)
        piece = pieces[part % groups].at[part // groups]
        piece[:, :width] = total[pl.ds(start, local_rows), :]
        piece[:, width:] = jnp.where(row == doubling_slot(part, parts), facts, 0.0)
    join_kernel(None, first, second, joined)


def spread(place, tokens, ids, after, total, first, second, parts, groups):
    piece = jax.ShapeDtypeStruct(
        (parts // groups, total.shape[0] // parts, total.shape[1] + LANES), jnp.float32
    )
    joined = jax.ShapeDtypeStruct(
        (first.shape[0] + second.shape[0],) + first.shape[1:], first.dtype
    )
    return pl.pallas_call(
        spread_kernel,
        out_shape=[piece] * groups + [joined],
        in_specs=[spec(pltpu.SMEM)] * 3 + [spec(pl.ANY)] + [spec(pltpu.VMEM)] * 3,
        out_specs=[spec(pltpu.VMEM)] * (groups + 1),
        compiler_params=grant(4),
    )(place, tokens, ids, after, total, first, second)


def split_three(x):
    high = x.astype(jnp.bfloat16)
    rest = x - high.astype(jnp.float32)
    middle = rest.astype(jnp.bfloat16)
    low = (rest - middle.astype(jnp.float32)).astype(jnp.bfloat16)
    return high, middle, low


def score_kernel(core_ref, own, other, eigen, other_eigen, *rest):
    blocks, out = rest[:-1], rest[-1]
    first = core_ref[0] == 0
    half, ka = eigen.shape
    factor_rows, width = blocks[0].shape[1:]
    ks = width - ka
    shared = own.shape[1] - LANES
    mine, theirs = own[...], other[...]
    coords = (jnp.where(first, mine, theirs), jnp.where(first, theirs, mine))
    eigens = (
        jnp.where(first, eigen[...], other_eigen[...]),
        jnp.where(first, other_eigen[...], eigen[...]),
    )
    scales = [1.0 / (e + damping) for e in eigens]
    act = jnp.concatenate([v[:, half:shared] for v in coords], axis=1)
    act_terms = split_three(act)
    out_terms = [split_three(v[:, :half]) for v in coords]
    order = ((0, 0), (0, 1), (1, 0), (1, 1), (0, 2), (2, 0))
    slot = lax.broadcasted_iota(jnp.int32, (mine.shape[0], LANES), 0)
    even = (slot // 4 + slot // 2 + slot) % 2 == 0
    facts = (mine[:, shared:], theirs[:, shared:])
    facts = jnp.concatenate(
        [jnp.where(even, facts[0], facts[1]), jnp.where(even, facts[1], facts[0])], axis=0
    )
    rows = jnp.concatenate([x[...] for x in blocks], axis=0)
    examples = rows.shape[0]
    lane = lax.broadcasted_iota(jnp.int32, (examples, LANES), 1).astype(jnp.float32)
    row = lax.broadcasted_iota(jnp.int32, (examples, factor_rows, ka), 1).astype(jnp.float32)
    hot = lane == facts[:, :1]
    keep = row < facts[:, LANES // 2 : LANES // 2 + 1][:, :, None]
    weights = jnp.where(keep, rows[:, :, ks:].astype(jnp.float32), 0.0)
    flat = rows[:, :, :ks].reshape(examples * factor_rows, ks)
    for q in range(out.shape[0]):
        cut = slice(q * RQ, (q + 1) * RQ)
        right = jnp.concatenate([act_terms[b][cut] for _, b in order], axis=0)
        precond = []
        for part in range(2):
            left = jnp.concatenate([out_terms[part][a][cut] for a, _ in order], axis=0)
            numer = lax.dot_general(
                left, right, (((0,), (0,)), ((), ())), preferred_element_type=jnp.float32
            )
            precond.append((numer * scales[part]).astype(jnp.bfloat16))
        precond = jnp.concatenate(precond, axis=0)
        projected = jnp.dot(flat, precond, preferred_element_type=jnp.float32)
        terms = projected.reshape(examples, factor_rows, ka) * weights
        per_example = jnp.sum(jnp.sum(terms, axis=1), axis=1, keepdims=True)
        scores = jnp.sum(jnp.where(hot, per_example, 0.0), axis=0, keepdims=True)
        out[q : q + 1, :] = scores[:, : out.shape[1]]


def score(core, own, other, eigen, other_eigen, blocks):
    examples = sum(x.shape[0] for x in blocks)
    return pl.pallas_call(
        score_kernel,
        out_shape=jax.ShapeDtypeStruct((own.shape[0] // RQ, examples), jnp.float32),
        in_specs=[spec(pltpu.SMEM)] + [spec(pltpu.VMEM)] * (4 + len(blocks)),
        out_specs=spec(pltpu.VMEM),
        compiler_params=grant(12),
    )(core, own, other, eigen, other_eigen, *blocks)


def direct(
    query_out,
    query_act,
    out_basis,
    act_basis,
    eigenvalues,
    train_out,
    train_act,
    train_tokens,
    train_ids,
):
    parts = lax.axis_size("blk")
    steps = parts.bit_length() - 1
    swap = [(0, 1), (1, 0)]

    def apart(x, distance):
        return lax.ppermute(x, "blk", [(s, s ^ distance) for s in range(parts)])

    def crossed(x, i):
        pairs = [
            (2 * s + f, 2 * (s ^ (1 << i)) + 1 - f) for s in range(parts) for f in range(2)
        ]
        return lax.ppermute(x, ("blk", "fsdp"), pairs)

    place = lax.axis_index("blk").reshape(1)
    core = lax.axis_index("fsdp").reshape(1)
    other_eigen = lax.ppermute(eigenvalues, "fsdp", swap)
    block = relay(pack(train_out, train_act))
    arrived = crossed(block, 2)
    total = project(query_out.T, query_act.T, out_basis, act_basis)
    *pieces, block = spread(
        place, train_tokens, train_ids, other_eigen, total, block, arrived, parts, parts // 2
    )
    near = join(pieces[0], block, crossed(block, 1))
    far_first = (len(pieces) - 1, *range(1, len(pieces) - 1))
    terms = [pieces[0]] + [apart(pieces[d], d) for d in far_first]
    sums = gather_sum(near, terms)
    far = crossed(near, 0)
    other_near = lax.ppermute(near, "fsdp", swap)
    other_far = lax.ppermute(far, "fsdp", swap)
    own = sums[0] + apart(sums[1], 4)
    other = lax.ppermute(own, "fsdp", swap)
    return score(
        core, own, other, eigenvalues, other_eigen, (near, far, other_near, other_far)
    )


def score_block(precond, out_rows, act_rows, token_counts):
    factor_rows = out_rows.shape[1]
    valid = (
        lax.broadcasted_iota(jnp.int32, (out_rows.shape[0], factor_rows), 1) < token_counts[:, None]
    ).astype(jnp.float32)
    projected = jnp.einsum("nri,qij->nrqj", out_rows, precond, preferred_element_type=jnp.float32)
    weights = act_rows.astype(jnp.float32) * valid[:, :, None]
    return jnp.einsum("nrqj,nrj->qn", projected, weights, precision=lax.Precision.HIGHEST)


def gathered(
    query_out,
    query_act,
    out_basis,
    act_basis,
    eigenvalues,
    train_out,
    train_act,
    train_tokens,
    train_ids,
):
    half_ks = out_basis.shape[1]
    local_rows = query_out.shape[1] // lax.axis_size("blk")
    out_part = lax.dot_general(
        query_out, out_basis, (((0,), (0,)), ((), ())), preferred_element_type=jnp.float32
    )
    act_part = lax.dot_general(
        query_act, act_basis, (((0,), (0,)), ((), ())), preferred_element_type=jnp.float32
    )
    rotated = lax.psum_scatter(
        jnp.concatenate([out_part, act_part], axis=1), "blk", scatter_dimension=0, tiled=True
    )
    out_coords = rotated[:, :half_ks]
    act_half = rotated[:, half_ks:]
    act_coords = lax.all_gather(act_half, "fsdp", axis=1, tiled=True)
    queries = local_rows // RQ
    out_three = out_coords.reshape(queries, RQ, half_ks)
    act_three = act_coords.reshape(queries, RQ, act_coords.shape[1])
    numer = jnp.einsum("qri,qrj->qij", out_three, act_three, precision=lax.Precision.HIGHEST)
    precond = (numer / (eigenvalues + damping)).astype(jnp.bfloat16)
    train_total = train_out.shape[0] * lax.axis_size("blk") * lax.axis_size("fsdp")
    empty = jnp.zeros((queries, train_total), jnp.float32)
    full_precond = lax.all_gather(precond, "fsdp", axis=1, tiled=True)
    out_rows = lax.all_gather(train_out, "blk", axis=0, tiled=True)
    act_rows = lax.all_gather(train_act, "blk", axis=0, tiled=True)
    token_counts = lax.all_gather(train_tokens, "blk", axis=0, tiled=True)
    column_ids = lax.all_gather(train_ids, "blk", axis=0, tiled=True)
    scores = empty.at[:, column_ids].add(
        score_block(full_precond, out_rows, act_rows, token_counts)
    )
    return lax.psum(scores, "fsdp")


def solution(mesh):
    parts = mesh.shape["blk"]
    few = parts == DIRECT_PARTS and mesh.shape["fsdp"] == 2
    return jax.shard_map(
        direct if few else gathered,
        mesh=mesh,
        in_specs=(
            P("blk", None),
            P("blk", None),
            P("blk", "fsdp"),
            P("blk", "fsdp"),
            P("fsdp", None),
            P(("groups", "blk", "fsdp"), None, None),
            P(("groups", "blk", "fsdp"), None, None),
            P(("groups", "blk", "fsdp")),
            P(("groups", "blk", "fsdp")),
        ),
        out_specs=P("blk", "groups"),
        check_vma=False,
    )
```

```python
import functools

import jax
import jax.numpy as jnp
from jax import lax
from jax.experimental import pallas as pl
from jax.experimental.pallas import tpu as pltpu
from jax.sharding import PartitionSpec as P

RQ = 4
LANES = 128
DIRECT_PARTS = 8
WAIT_FLOPS = 10**9


damping = 0.1


def pinned(x):
    return pltpu.with_memory_space_constraint(x, pltpu.HBM)


def grant(mebibytes):
    return pltpu.CompilerParams(vmem_limit_bytes=mebibytes * 2**20)


def spec(space):
    return pl.BlockSpec(memory_space=space)


def pack_kernel(train_out, train_act, packed, sems):
    ks = train_out.shape[2]
    copies = (
        pltpu.make_async_copy(train_out, packed.at[:, :, :ks], sems.at[0]),
        pltpu.make_async_copy(train_act, packed.at[:, :, ks:], sems.at[1]),
    )
    for copy in copies:
        copy.start()
    for copy in copies:
        copy.wait()


def pack(train_out, train_act):
    examples, rows, ks = train_out.shape
    shape = (examples, rows, ks + train_act.shape[2])
    return pl.pallas_call(
        pack_kernel,
        out_shape=jax.ShapeDtypeStruct(shape, train_out.dtype),
        in_specs=[spec(pltpu.HBM)] * 2,
        out_specs=spec(pltpu.VMEM),
        scratch_shapes=[pltpu.SemaphoreType.DMA((2,))],
        compiler_params=grant(2),
    )(pinned(train_out), pinned(train_act))


def join_kernel(after, first, second, joined):
    del after
    count = first.shape[0]
    joined[:count] = first[...]
    joined[count:] = second[...]


def joined_shape(first, second):
    return jax.ShapeDtypeStruct(
        (first.shape[0] + second.shape[0],) + first.shape[1:], first.dtype
    )


def join(after, first, second):
    return pl.pallas_call(
        join_kernel,
        out_shape=joined_shape(first, second),
        in_specs=[spec(pl.ANY)] + [spec(pltpu.VMEM)] * 2,
        out_specs=spec(pltpu.VMEM),
        compiler_params=grant(4),
    )(after, first, second)


def relay_kernel(source, target):
    target[...] = source[...]


def relay(source):
    return pl.pallas_call(
        relay_kernel,
        out_shape=jax.ShapeDtypeStruct(source.shape, source.dtype),
        in_specs=[spec(pltpu.VMEM)],
        out_specs=spec(pltpu.VMEM),
        compiler_params=grant(2),
        cost_estimate=pl.CostEstimate(flops=WAIT_FLOPS, bytes_accessed=0, transcendentals=0),
    )(source)


def gather_sum_kernel(after, *refs):
    del after
    total = refs[0][...]
    for term in refs[1:-1]:
        total = total + term[...]
    refs[-1][...] = total


def gather_sum(after, terms):
    return pl.pallas_call(
        gather_sum_kernel,
        out_shape=jax.ShapeDtypeStruct(terms[0].shape, terms[0].dtype),
        in_specs=[spec(pl.ANY)] + [spec(pltpu.VMEM)] * len(terms),
        out_specs=spec(pltpu.VMEM),
        compiler_params=grant(4),
    )(after, *terms)


def hold_kernel(after, source, target):
    del after
    target[...] = source[...]


def hold(after, source):
    return pl.pallas_call(
        hold_kernel,
        out_shape=jax.ShapeDtypeStruct(source.shape, source.dtype),
        in_specs=[spec(pl.ANY), spec(pltpu.VMEM)],
        out_specs=spec(pltpu.VMEM),
        compiler_params=grant(2),
    )(after, source)


def project_kernel(query_out, query_act, out_basis, act_basis, total):
    half_ks = out_basis.shape[1]
    total[:, :half_ks] = jnp.dot(
        query_out[...], out_basis[...], preferred_element_type=jnp.float32
    )
    total[:, half_ks:] = jnp.dot(
        query_act[...], act_basis[...], preferred_element_type=jnp.float32
    )


def project(query_out, query_act, out_basis, act_basis):
    columns = query_out.shape[0]
    width = out_basis.shape[1] + act_basis.shape[1]
    operands = (query_out, query_act, out_basis, act_basis)
    return pl.pallas_call(
        project_kernel,
        out_shape=jax.ShapeDtypeStruct((columns, width), jnp.float32),
        in_specs=[spec(pltpu.VMEM)] * len(operands),
        out_specs=spec(pltpu.VMEM),
        compiler_params=grant(8),
        cost_estimate=pl.CostEstimate(
            flops=2 * columns * (out_basis.size + act_basis.size),
            bytes_accessed=2 * sum(x.size for x in operands),
            transcendentals=0,
        ),
    )(*operands)


def doubling_slot(distance, parts):
    bits = parts.bit_length() - 1
    return sum(1 << (bits - 1 - i) for i in range(bits) if distance >> i & 1)


def spread_kernel(place_ref, tokens_ref, ids_ref, total, first, second, *rest):
    pieces, joined = rest[:-1], rest[-1]
    groups = len(pieces)
    each, local_rows, _ = pieces[0].shape
    parts = groups * each
    width = total.shape[1]
    row = lax.broadcasted_iota(jnp.int32, (local_rows, LANES), 0)
    lane = lax.broadcasted_iota(jnp.int32, (local_rows, LANES), 1)
    facts = jnp.where(lane < LANES // 2, ids_ref[0], tokens_ref[0]).astype(jnp.float32)
    for part in range(parts):
        start = pl.multiple_of((place_ref[0] ^ part) * local_rows, local_rows)
        piece = pieces[part % groups].at[part // groups]
        piece[:, :width] = total[pl.ds(start, local_rows), :]
        piece[:, width:] = jnp.where(row == doubling_slot(part, parts), facts, 0.0)
    join_kernel(None, first, second, joined)


def spread(place, tokens, ids, total, first, second, parts, groups):
    piece = jax.ShapeDtypeStruct(
        (parts // groups, total.shape[0] // parts, total.shape[1] + LANES), jnp.float32
    )
    joined = jax.ShapeDtypeStruct(
        (first.shape[0] + second.shape[0],) + first.shape[1:], first.dtype
    )
    return pl.pallas_call(
        spread_kernel,
        out_shape=[piece] * groups + [joined],
        in_specs=[spec(pltpu.SMEM)] * 3 + [spec(pltpu.VMEM)] * 3,
        out_specs=[spec(pltpu.VMEM)] * (groups + 1),
        compiler_params=grant(4),
    )(place, tokens, ids, total, first, second)


def split_three(x):
    high = x.astype(jnp.bfloat16)
    rest = x - high.astype(jnp.float32)
    middle = rest.astype(jnp.bfloat16)
    low = (rest - middle.astype(jnp.float32)).astype(jnp.bfloat16)
    return high, middle, low


def score_kernel(core_ref, own, other, eigen, other_eigen, *rest):
    blocks, out = rest[:-1], rest[-1]
    first = core_ref[0] == 0
    half, ka = eigen.shape
    factor_rows, width = blocks[0].shape[1:]
    ks = width - ka
    shared = own.shape[1] - LANES
    mine, theirs = own[...], other[...]
    coords = (jnp.where(first, mine, theirs), jnp.where(first, theirs, mine))
    eigens = (
        jnp.where(first, eigen[...], other_eigen[...]),
        jnp.where(first, other_eigen[...], eigen[...]),
    )
    scales = [1.0 / (e + damping) for e in eigens]
    act = jnp.concatenate([v[:, half:shared] for v in coords], axis=1)
    act_terms = split_three(act)
    out_terms = [split_three(v[:, :half]) for v in coords]
    order = ((0, 0), (0, 1), (1, 0), (1, 1), (0, 2), (2, 0))
    slot = lax.broadcasted_iota(jnp.int32, (mine.shape[0], LANES), 0)
    even = (slot // 4 + slot // 2 + slot) % 2 == 0
    facts = (mine[:, shared:], theirs[:, shared:])
    facts = jnp.concatenate(
        [jnp.where(even, facts[0], facts[1]), jnp.where(even, facts[1], facts[0])], axis=0
    )
    rows = jnp.concatenate([x[...] for x in blocks], axis=0)
    examples = rows.shape[0]
    lane = lax.broadcasted_iota(jnp.int32, (examples, LANES), 1).astype(jnp.float32)
    row = lax.broadcasted_iota(jnp.int32, (examples, factor_rows, ka), 1).astype(jnp.float32)
    hot = lane == facts[:, :1]
    keep = row < facts[:, LANES // 2 : LANES // 2 + 1][:, :, None]
    weights = jnp.where(keep, rows[:, :, ks:].astype(jnp.float32), 0.0)
    flat = rows[:, :, :ks].reshape(examples * factor_rows, ks)
    for q in range(out.shape[0]):
        cut = slice(q * RQ, (q + 1) * RQ)
        right = jnp.concatenate([act_terms[b][cut] for _, b in order], axis=0)
        precond = []
        for part in range(2):
            left = jnp.concatenate([out_terms[part][a][cut] for a, _ in order], axis=0)
            numer = lax.dot_general(
                left, right, (((0,), (0,)), ((), ())), preferred_element_type=jnp.float32
            )
            precond.append((numer * scales[part]).astype(jnp.bfloat16))
        precond = jnp.concatenate(precond, axis=0)
        projected = jnp.dot(flat, precond, preferred_element_type=jnp.float32)
        terms = projected.reshape(examples, factor_rows, ka) * weights
        per_example = jnp.sum(jnp.sum(terms, axis=1), axis=1, keepdims=True)
        scores = jnp.sum(jnp.where(hot, per_example, 0.0), axis=0, keepdims=True)
        out[q : q + 1, :] = scores[:, : out.shape[1]]


def score(core, own, other, eigen, other_eigen, blocks):
    examples = sum(x.shape[0] for x in blocks)
    return pl.pallas_call(
        score_kernel,
        out_shape=jax.ShapeDtypeStruct((own.shape[0] // RQ, examples), jnp.float32),
        in_specs=[spec(pltpu.SMEM)] + [spec(pltpu.VMEM)] * (4 + len(blocks)),
        out_specs=spec(pltpu.VMEM),
        compiler_params=grant(12),
    )(core, own, other, eigen, other_eigen, *blocks)


def direct(
    query_out,
    query_act,
    out_basis,
    act_basis,
    eigenvalues,
    train_out,
    train_act,
    train_tokens,
    train_ids,
):
    parts = lax.axis_size("blk")
    steps = parts.bit_length() - 1
    swap = [(0, 1), (1, 0)]

    def apart(x, distance):
        return lax.ppermute(x, "blk", [(s, s ^ distance) for s in range(parts)])

    def crossed(x, i):
        pairs = [
            (2 * s + f, 2 * (s ^ (1 << i)) + 1 - f) for s in range(parts) for f in range(2)
        ]
        return lax.ppermute(x, ("blk", "fsdp"), pairs)

    place = lax.axis_index("blk").reshape(1)
    core = lax.axis_index("fsdp").reshape(1)
    block = relay(pack(train_out, train_act))
    arrived = crossed(block, 2)
    total = project(query_out.T, query_act.T, out_basis, act_basis)
    *pieces, block = spread(
        place, train_tokens, train_ids, total, block, arrived, parts, parts // 2
    )
    near = join(pieces[0], block, crossed(block, 1))
    far_first = (len(pieces) - 1, *range(1, len(pieces) - 1))
    terms = [pieces[0]] + [apart(pieces[d], d) for d in far_first]
    sums = gather_sum(near, terms)
    far = crossed(near, 0)
    other_eigen = lax.ppermute(hold(near, eigenvalues), "fsdp", swap)
    other_near = lax.ppermute(near, "fsdp", swap)
    other_far = lax.ppermute(far, "fsdp", swap)
    own = sums[0] + apart(sums[1], 4)
    other = lax.ppermute(own, "fsdp", swap)
    return score(
        core, own, other, eigenvalues, other_eigen, (near, far, other_near, other_far)
    )


def score_block(precond, out_rows, act_rows, token_counts):
    factor_rows = out_rows.shape[1]
    valid = (
        lax.broadcasted_iota(jnp.int32, (out_rows.shape[0], factor_rows), 1) < token_counts[:, None]
    ).astype(jnp.float32)
    projected = jnp.einsum("nri,qij->nrqj", out_rows, precond, preferred_element_type=jnp.float32)
    weights = act_rows.astype(jnp.float32) * valid[:, :, None]
    return jnp.einsum("nrqj,nrj->qn", projected, weights, precision=lax.Precision.HIGHEST)


def gathered(
    query_out,
    query_act,
    out_basis,
    act_basis,
    eigenvalues,
    train_out,
    train_act,
    train_tokens,
    train_ids,
):
    half_ks = out_basis.shape[1]
    local_rows = query_out.shape[1] // lax.axis_size("blk")
    out_part = lax.dot_general(
        query_out, out_basis, (((0,), (0,)), ((), ())), preferred_element_type=jnp.float32
    )
    act_part = lax.dot_general(
        query_act, act_basis, (((0,), (0,)), ((), ())), preferred_element_type=jnp.float32
    )
    rotated = lax.psum_scatter(
        jnp.concatenate([out_part, act_part], axis=1), "blk", scatter_dimension=0, tiled=True
    )
    out_coords = rotated[:, :half_ks]
    act_half = rotated[:, half_ks:]
    act_coords = lax.all_gather(act_half, "fsdp", axis=1, tiled=True)
    queries = local_rows // RQ
    out_three = out_coords.reshape(queries, RQ, half_ks)
    act_three = act_coords.reshape(queries, RQ, act_coords.shape[1])
    numer = jnp.einsum("qri,qrj->qij", out_three, act_three, precision=lax.Precision.HIGHEST)
    precond = (numer / (eigenvalues + damping)).astype(jnp.bfloat16)
    train_total = train_out.shape[0] * lax.axis_size("blk") * lax.axis_size("fsdp")
    empty = jnp.zeros((queries, train_total), jnp.float32)
    full_precond = lax.all_gather(precond, "fsdp", axis=1, tiled=True)
    out_rows = lax.all_gather(train_out, "blk", axis=0, tiled=True)
    act_rows = lax.all_gather(train_act, "blk", axis=0, tiled=True)
    token_counts = lax.all_gather(train_tokens, "blk", axis=0, tiled=True)
    column_ids = lax.all_gather(train_ids, "blk", axis=0, tiled=True)
    scores = empty.at[:, column_ids].add(
        score_block(full_precond, out_rows, act_rows, token_counts)
    )
    return lax.psum(scores, "fsdp")


def solution(mesh):
    parts = mesh.shape["blk"]
    few = parts == DIRECT_PARTS and mesh.shape["fsdp"] == 2
    return jax.shard_map(
        direct if few else gathered,
        mesh=mesh,
        in_specs=(
            P("blk", None),
            P("blk", None),
            P("blk", "fsdp"),
            P("blk", "fsdp"),
            P("fsdp", None),
            P(("groups", "blk", "fsdp"), None, None),
            P(("groups", "blk", "fsdp"), None, None),
            P(("groups", "blk", "fsdp")),
            P(("groups", "blk", "fsdp")),
        ),
        out_specs=P("blk", "groups"),
        check_vma=False,
    )
```

```python
import functools

import jax
import jax.numpy as jnp
from jax import lax
from jax.experimental import pallas as pl
from jax.experimental.pallas import tpu as pltpu
from jax.sharding import PartitionSpec as P

RQ = 4
LANES = 128
DIRECT_PARTS = 8
WAIT_FLOPS = 10**9


damping = 0.1


def pinned(x):
    return pltpu.with_memory_space_constraint(x, pltpu.HBM)


def grant(mebibytes):
    return pltpu.CompilerParams(vmem_limit_bytes=mebibytes * 2**20)


def spec(space):
    return pl.BlockSpec(memory_space=space)


def pack_kernel(train_out, train_act, packed, sems):
    ks = train_out.shape[2]
    copies = (
        pltpu.make_async_copy(train_out, packed.at[:, :, :ks], sems.at[0]),
        pltpu.make_async_copy(train_act, packed.at[:, :, ks:], sems.at[1]),
    )
    for copy in copies:
        copy.start()
    for copy in copies:
        copy.wait()


def pack(train_out, train_act):
    examples, rows, ks = train_out.shape
    shape = (examples, rows, ks + train_act.shape[2])
    return pl.pallas_call(
        pack_kernel,
        out_shape=jax.ShapeDtypeStruct(shape, train_out.dtype),
        in_specs=[spec(pltpu.HBM)] * 2,
        out_specs=spec(pltpu.VMEM),
        scratch_shapes=[pltpu.SemaphoreType.DMA((2,))],
        compiler_params=grant(2),
    )(pinned(train_out), pinned(train_act))


def join_kernel(after, first, second, joined):
    del after
    count = first.shape[0]
    joined[:count] = first[...]
    joined[count:] = second[...]


def joined_shape(first, second):
    return jax.ShapeDtypeStruct(
        (first.shape[0] + second.shape[0],) + first.shape[1:], first.dtype
    )


def join(after, first, second):
    return pl.pallas_call(
        join_kernel,
        out_shape=joined_shape(first, second),
        in_specs=[spec(pl.ANY)] + [spec(pltpu.VMEM)] * 2,
        out_specs=spec(pltpu.VMEM),
        compiler_params=grant(4),
    )(after, first, second)


def relay_kernel(source, target):
    target[...] = source[...]


def relay(source):
    return pl.pallas_call(
        relay_kernel,
        out_shape=jax.ShapeDtypeStruct(source.shape, source.dtype),
        in_specs=[spec(pltpu.VMEM)],
        out_specs=spec(pltpu.VMEM),
        compiler_params=grant(2),
        cost_estimate=pl.CostEstimate(flops=WAIT_FLOPS, bytes_accessed=0, transcendentals=0),
    )(source)


def gather_sum_kernel(after, *refs):
    del after
    total = refs[0][...]
    for term in refs[1:-1]:
        total = total + term[...]
    refs[-1][...] = total


def gather_sum(after, terms):
    return pl.pallas_call(
        gather_sum_kernel,
        out_shape=jax.ShapeDtypeStruct(terms[0].shape, terms[0].dtype),
        in_specs=[spec(pl.ANY)] + [spec(pltpu.VMEM)] * len(terms),
        out_specs=spec(pltpu.VMEM),
        compiler_params=grant(4),
    )(after, *terms)


def project_kernel(query_out, query_act, out_basis, act_basis, total):
    half_ks = out_basis.shape[1]
    total[:, :half_ks] = jnp.dot(
        query_out[...], out_basis[...], preferred_element_type=jnp.float32
    )
    total[:, half_ks:] = jnp.dot(
        query_act[...], act_basis[...], preferred_element_type=jnp.float32
    )


def project(query_out, query_act, out_basis, act_basis):
    columns = query_out.shape[0]
    width = out_basis.shape[1] + act_basis.shape[1]
    operands = (query_out, query_act, out_basis, act_basis)
    return pl.pallas_call(
        project_kernel,
        out_shape=jax.ShapeDtypeStruct((columns, width), jnp.float32),
        in_specs=[spec(pltpu.VMEM)] * len(operands),
        out_specs=spec(pltpu.VMEM),
        compiler_params=grant(8),
        cost_estimate=pl.CostEstimate(
            flops=2 * columns * (out_basis.size + act_basis.size),
            bytes_accessed=2 * sum(x.size for x in operands),
            transcendentals=0,
        ),
    )(*operands)


def doubling_slot(distance, parts):
    bits = parts.bit_length() - 1
    return sum(1 << (bits - 1 - i) for i in range(bits) if distance >> i & 1)


def spread_kernel(place_ref, tokens_ref, ids_ref, after, total, first, second, *rest):
    del after
    pieces, joined = rest[:-1], rest[-1]
    groups = len(pieces)
    each, local_rows, _ = pieces[0].shape
    parts = groups * each
    width = total.shape[1]
    row = lax.broadcasted_iota(jnp.int32, (local_rows, LANES), 0)
    lane = lax.broadcasted_iota(jnp.int32, (local_rows, LANES), 1)
    facts = jnp.where(lane < LANES // 2, ids_ref[0], tokens_ref[0]).astype(jnp.float32)
    for part in range(parts):
        start = pl.multiple_of((place_ref[0] ^ part) * local_rows, local_rows)
        piece = pieces[part % groups].at[part // groups]
        piece[:, :width] = total[pl.ds(start, local_rows), :]
        piece[:, width:] = jnp.where(row == doubling_slot(part, parts), facts, 0.0)
    join_kernel(None, first, second, joined)


def spread(place, tokens, ids, after, total, first, second, parts, groups):
    piece = jax.ShapeDtypeStruct(
        (parts // groups, total.shape[0] // parts, total.shape[1] + LANES), jnp.float32
    )
    joined = jax.ShapeDtypeStruct(
        (first.shape[0] + second.shape[0],) + first.shape[1:], first.dtype
    )
    return pl.pallas_call(
        spread_kernel,
        out_shape=[piece] * groups + [joined],
        in_specs=[spec(pltpu.SMEM)] * 3 + [spec(pl.ANY)] + [spec(pltpu.VMEM)] * 3,
        out_specs=[spec(pltpu.VMEM)] * (groups + 1),
        compiler_params=grant(4),
    )(place, tokens, ids, after, total, first, second)


def split_three(x):
    high = x.astype(jnp.bfloat16)
    rest = x - high.astype(jnp.float32)
    middle = rest.astype(jnp.bfloat16)
    low = (rest - middle.astype(jnp.float32)).astype(jnp.bfloat16)
    return high, middle, low


def score_kernel(core_ref, own, other, eigen, other_eigen, *rest):
    blocks, out = rest[:-1], rest[-1]
    first = core_ref[0] == 0
    half, ka = eigen.shape
    factor_rows, width = blocks[0].shape[1:]
    ks = width - ka
    shared = own.shape[1] - LANES
    mine, theirs = own[...], other[...]
    coords = (jnp.where(first, mine, theirs), jnp.where(first, theirs, mine))
    eigens = (
        jnp.where(first, eigen[...], other_eigen[...]),
        jnp.where(first, other_eigen[...], eigen[...]),
    )
    scales = [1.0 / (e + damping) for e in eigens]
    act = jnp.concatenate([v[:, half:shared] for v in coords], axis=1)
    act_terms = split_three(act)
    out_terms = [split_three(v[:, :half]) for v in coords]
    order = ((0, 0), (0, 1), (1, 0), (1, 1), (0, 2), (2, 0))
    slot = lax.broadcasted_iota(jnp.int32, (mine.shape[0], LANES), 0)
    even = (slot // 4 + slot // 2 + slot) % 2 == 0
    facts = (mine[:, shared:], theirs[:, shared:])
    facts = jnp.concatenate(
        [jnp.where(even, facts[0], facts[1]), jnp.where(even, facts[1], facts[0])], axis=0
    )
    rows = jnp.concatenate([x[...] for x in blocks], axis=0)
    examples = rows.shape[0]
    lane = lax.broadcasted_iota(jnp.int32, (examples, LANES), 1).astype(jnp.float32)
    row = lax.broadcasted_iota(jnp.int32, (examples, factor_rows, ka), 1).astype(jnp.float32)
    hot = lane == facts[:, :1]
    keep = row < facts[:, LANES // 2 : LANES // 2 + 1][:, :, None]
    weights = jnp.where(keep, rows[:, :, ks:].astype(jnp.float32), 0.0)
    flat = rows[:, :, :ks].reshape(examples * factor_rows, ks)
    for q in range(out.shape[0]):
        cut = slice(q * RQ, (q + 1) * RQ)
        right = jnp.concatenate([act_terms[b][cut] for _, b in order], axis=0)
        precond = []
        for part in range(2):
            left = jnp.concatenate([out_terms[part][a][cut] for a, _ in order], axis=0)
            numer = lax.dot_general(
                left, right, (((0,), (0,)), ((), ())), preferred_element_type=jnp.float32
            )
            precond.append((numer * scales[part]).astype(jnp.bfloat16))
        precond = jnp.concatenate(precond, axis=0)
        projected = jnp.dot(flat, precond, preferred_element_type=jnp.float32)
        terms = projected.reshape(examples, factor_rows, ka) * weights
        per_example = jnp.sum(jnp.sum(terms, axis=1), axis=1, keepdims=True)
        scores = jnp.sum(jnp.where(hot, per_example, 0.0), axis=0, keepdims=True)
        out[q : q + 1, :] = scores[:, : out.shape[1]]


def score(core, own, other, eigen, other_eigen, blocks):
    examples = sum(x.shape[0] for x in blocks)
    return pl.pallas_call(
        score_kernel,
        out_shape=jax.ShapeDtypeStruct((own.shape[0] // RQ, examples), jnp.float32),
        in_specs=[spec(pltpu.SMEM)] + [spec(pltpu.VMEM)] * (4 + len(blocks)),
        out_specs=spec(pltpu.VMEM),
        compiler_params=grant(12),
    )(core, own, other, eigen, other_eigen, *blocks)


def direct(
    query_out,
    query_act,
    out_basis,
    act_basis,
    eigenvalues,
    train_out,
    train_act,
    train_tokens,
    train_ids,
):
    parts = lax.axis_size("blk")
    steps = parts.bit_length() - 1
    swap = [(0, 1), (1, 0)]

    def apart(x, distance):
        return lax.ppermute(x, "blk", [(s, s ^ distance) for s in range(parts)])

    def crossed(x, i):
        pairs = [
            (2 * s + f, 2 * (s ^ (1 << i)) + 1 - f) for s in range(parts) for f in range(2)
        ]
        return lax.ppermute(x, ("blk", "fsdp"), pairs)

    place = lax.axis_index("blk").reshape(1)
    core = lax.axis_index("fsdp").reshape(1)
    other_eigen = lax.ppermute(eigenvalues, "fsdp", swap)
    block = relay(pack(train_out, train_act))
    arrived = crossed(block, 2)
    total = project(query_out.T, query_act.T, out_basis, act_basis)
    *pieces, block = spread(
        place, train_tokens, train_ids, other_eigen, total, block, arrived, parts, parts // 2
    )
    near = join(pieces[0], block, crossed(block, 1))
    far_first = (1, *range(len(pieces) - 1, 1, -1))
    terms = [pieces[0]] + [apart(pieces[d], d) for d in far_first]
    sums = gather_sum(near, terms)
    far = crossed(near, 0)
    other_near = lax.ppermute(near, "fsdp", swap)
    other_far = lax.ppermute(far, "fsdp", swap)
    own = sums[0] + apart(sums[1], 4)
    other = lax.ppermute(own, "fsdp", swap)
    return score(
        core, own, other, eigenvalues, other_eigen, (near, far, other_near, other_far)
    )


def score_block(precond, out_rows, act_rows, token_counts):
    factor_rows = out_rows.shape[1]
    valid = (
        lax.broadcasted_iota(jnp.int32, (out_rows.shape[0], factor_rows), 1) < token_counts[:, None]
    ).astype(jnp.float32)
    projected = jnp.einsum("nri,qij->nrqj", out_rows, precond, preferred_element_type=jnp.float32)
    weights = act_rows.astype(jnp.float32) * valid[:, :, None]
    return jnp.einsum("nrqj,nrj->qn", projected, weights, precision=lax.Precision.HIGHEST)


def gathered(
    query_out,
    query_act,
    out_basis,
    act_basis,
    eigenvalues,
    train_out,
    train_act,
    train_tokens,
    train_ids,
):
    half_ks = out_basis.shape[1]
    local_rows = query_out.shape[1] // lax.axis_size("blk")
    out_part = lax.dot_general(
        query_out, out_basis, (((0,), (0,)), ((), ())), preferred_element_type=jnp.float32
    )
    act_part = lax.dot_general(
        query_act, act_basis, (((0,), (0,)), ((), ())), preferred_element_type=jnp.float32
    )
    rotated = lax.psum_scatter(
        jnp.concatenate([out_part, act_part], axis=1), "blk", scatter_dimension=0, tiled=True
    )
    out_coords = rotated[:, :half_ks]
    act_half = rotated[:, half_ks:]
    act_coords = lax.all_gather(act_half, "fsdp", axis=1, tiled=True)
    queries = local_rows // RQ
    out_three = out_coords.reshape(queries, RQ, half_ks)
    act_three = act_coords.reshape(queries, RQ, act_coords.shape[1])
    numer = jnp.einsum("qri,qrj->qij", out_three, act_three, precision=lax.Precision.HIGHEST)
    precond = (numer / (eigenvalues + damping)).astype(jnp.bfloat16)
    train_total = train_out.shape[0] * lax.axis_size("blk") * lax.axis_size("fsdp")
    empty = jnp.zeros((queries, train_total), jnp.float32)
    full_precond = lax.all_gather(precond, "fsdp", axis=1, tiled=True)
    out_rows = lax.all_gather(train_out, "blk", axis=0, tiled=True)
    act_rows = lax.all_gather(train_act, "blk", axis=0, tiled=True)
    token_counts = lax.all_gather(train_tokens, "blk", axis=0, tiled=True)
    column_ids = lax.all_gather(train_ids, "blk", axis=0, tiled=True)
    scores = empty.at[:, column_ids].add(
        score_block(full_precond, out_rows, act_rows, token_counts)
    )
    return lax.psum(scores, "fsdp")


def solution(mesh):
    parts = mesh.shape["blk"]
    few = parts == DIRECT_PARTS and mesh.shape["fsdp"] == 2
    return jax.shard_map(
        direct if few else gathered,
        mesh=mesh,
        in_specs=(
            P("blk", None),
            P("blk", None),
            P("blk", "fsdp"),
            P("blk", "fsdp"),
            P("fsdp", None),
            P(("groups", "blk", "fsdp"), None, None),
            P(("groups", "blk", "fsdp"), None, None),
            P(("groups", "blk", "fsdp")),
            P(("groups", "blk", "fsdp")),
        ),
        out_specs=P("blk", "groups"),
        check_vma=False,
    )
```
